32 devices in a mesh: seq: 2 (over core), row: 4 (over y, x), col: 4 (over z).
Axes of the slice: x: 2, y: 2, z: 4, core: 2. Of those that a mesh axis runs over, the one named last changes fastest.
Arguments:
- tokens: bfloat16 [1024, 4096], P('seq', ('row', 'col')), may hold values from -6 to 6
- lengths: int32 [16], replicated, may hold values from 1 to 256, 1024 in all
- deal: int32 [16], replicated, may hold values from 0 to 15, each once
- pre_gain: float32 [4096], replicated, may hold values from 0.5 to 1.5
- w_inner: bfloat16 [4096, 2, 8192], P(None, None, ('row', 'col'))
- w_group: bfloat16 [4096, 2, 8, 128], P(None, None, 'row'), may hold values from -0.09375 to 0.09375
- w_step: bfloat16 [4096, 128], P(None, ('row', 'col')), may hold values from -0.09375 to 0.09375
- conv_inner: float32 [4, 8192], P(None, ('row', 'col')), may hold values from -0.5 to 0.5
- conv_group: float32 [4, 2, 8, 128], P(None, None, 'row'), may hold values from -0.5 to 0.5
- conv_bias_inner: float32 [8192], P(('row', 'col')), may hold values from -0.5 to 0.5
- conv_bias_group: float32 [2, 8, 128], P(None, 'row'), may hold values from -0.5 to 0.5
- edge_inner: bfloat16 [16, 3, 8192], P(None, None, ('row', 'col')), may hold values from -6 to 6
- edge_group: bfloat16 [16, 3, 2, 8, 128], P(None, None, None, 'row'), may hold values from -6 to 6
- init_states: float32 [16, 128, 64, 128], P(None, ('row', 'col')), may hold values from -1.25 to 1.25
- step_bias: float32 [128], P(('row', 'col')), may hold values from -5.3 to -2.3
- decay_log: float32 [128], P(('row', 'col')), may hold values from -3.9 to 0
- skip: float32 [128], P(('row', 'col')), may hold values from 0.5 to 1.5
- inner_gain: float32 [8192], P(('row', 'col')), may hold values from 0.5 to 1.5
- w_out: bfloat16 [8192, 4096], P(('row', 'col')), may hold values from -0.09375 to 0.09375
- final_gain: float32 [4096], replicated, may hold values from 0.5 to 1.5
- w_head: bfloat16 [4096, 32768], P(None, ('seq', 'row', 'col')), may hold values from -0.09375 to 0.09375
Outputs:
- hidden_out: bfloat16 [1024, 4096], P('seq', ('row', 'col'))
- final_states: float32 [16, 128, 64, 128], P('seq', ('row', 'col'))
- logits: float32 [16, 32768], P(None, ('seq', 'row', 'col'))
The draws below stay inside these ranges and needn't reach their ends.
Inputs may be any that keep to these rules, and one draw needn't show every extreme that they name: The lengths sum to 1024 and the longest is exactly 256. `deal`: each owner slot appears once.
All inputs are finite; a program needn't handle non-finite values.
Results may differ from the reference program's by a relative error of at most 0.012.
Values may be sent and summed in bfloat16 or wider, within the bound.
No kernel may reach another device: no remote copies, remote signals or barrier semaphores. Data moves between devices by JAX's collectives and lax.ppermute only.
A program may use at most 128 MiB of HBM per device.

```python
import math
import jax
import jax.numpy as jnp
import numpy as np
from jax import lax

D = 4096
HEADS = 128
HEAD = 64
STATE = 128
GROUPS = 8
VOCAB = 32768
KERNEL = 4
BLOCK = 256
REQS = 16
E = 8192
TOKENS = 1024


def draw_w_inner(key, part):
    noise_key = jax.random.fold_in(key, 11)
    scale_key = jax.random.fold_in(key, 12)
    span = E // GROUPS
    place = (jnp.arange(E) % span).astype(jnp.float32) / span
    column = jnp.power(3.0, place - 0.5) * jnp.exp(jax.random.uniform(scale_key, (E,), jnp.float32, -0.5, 0.5))
    values = jnp.clip(jax.random.normal(noise_key, (D, 2, E), jnp.float32), -4.0, 4.0)
    return (values * column * D ** (-0.5)).astype(jnp.bfloat16)


def spiked(values, own_key, source, target, blocks, factor):
    def block_of(dim):
        return (jnp.arange(values.shape[dim]) // (values.shape[dim] // blocks)).reshape((-1,) + (1,) * (values.ndim - 1 - dim))

    near = jax.random.permutation(own_key, blocks)[block_of(target)]
    other_side = (block_of(target) + blocks // 2) % blocks
    return jnp.where((block_of(source) == near) | (block_of(source) == other_side), factor * values, values)


def steps_of(key, extent, cuts, smallest, high):
    gain, own = 1.0, jax.random.fold_in(key, 6)
    for dim, shards_of in cuts:
        heights = jnp.exp(jax.random.uniform(jax.random.fold_in(own, dim), (shards_of,), jnp.float32, smallest / len(cuts), high / len(cuts)))
        gain = gain * jnp.repeat(heights, extent[dim] // shards_of).reshape([-1 if axis == dim else 1 for axis in range(len(extent))])
    return gain


def split_up(amount, total, limit, slope):
    weights = [(1 << 20) // math.isqrt(grade ** slope) + 1 for grade in range(2, amount + 1)]
    spare, counts = total - limit - (amount - 1), [1] * (amount - 1)
    while spare > 0:
        movable = [i for i in range(amount - 1) if counts[i] < limit]
        whole, left = sum([weights[i] for i in movable]), spare
        for i in movable:
            more = min(limit - counts[i], max(1, left * weights[i] // whole), spare)
            counts[i] = counts[i] + more
            spare = spare - more
    return np.array([limit] + counts)


def uneven(own_key, number_of, total, limit, skew):
    if number_of == 2:
        one = jax.random.randint(own_key, (), max(1, total - limit), min(limit, total - 1) + 1)
        return jnp.stack([one, total - one])
    tallies = jnp.asarray(split_up(number_of, total, limit, skew), jnp.int32)
    couples = (number_of - 1) // 2
    source_of, taker = tallies[1:1 + 2 * couples:2], tallies[2:2 + 2 * couples:2]
    slack = jnp.minimum(source_of - 1, limit - taker)
    shifted = jax.random.randint(jax.random.fold_in(own_key, 1), (couples,), 0, 1 << 20) % (slack + 1)
    tallies = tallies.at[1:1 + 2 * couples:2].set(source_of - shifted).at[2:2 + 2 * couples:2].set(taker + shifted)
    return tallies[jax.random.permutation(jax.random.fold_in(own_key, 2), number_of)]


def scatter_about(key, extent, width, bound, shards=(), kind=jnp.bfloat16):
    level = steps_of(key, extent, shards, -0.22, 0.18) if shards else 1.0
    values = jax.random.normal(key, extent, jnp.float32) * width * level
    return jnp.minimum(jnp.maximum(values, -bound), bound).astype(kind)


def heavy_noise(rng, extent, width, bound, split, heavy, held_as=jnp.bfloat16):
    array = width * jax.random.normal(rng, extent, jnp.float32)
    if split:
        array = array * steps_of(rng, extent, split, -0.22, 0.18)
    return jnp.clip(spiked(array, jax.random.fold_in(rng, 3), *heavy), -bound, bound).astype(held_as)


def setup_inputs(seed: int = 0) -> dict:
    splits = jax.random.split(jax.random.key(seed), 22)
    return {
        "tokens": scatter_about(splits[0], (TOKENS, D), 1.0, 6.0, ((0, 2), (1, 16))),
        "lengths": uneven(splits[1], REQS, TOKENS, TOKENS // 4, 2).astype(jnp.int32),
        "deal": jax.random.permutation(splits[2], REQS).astype(jnp.int32),
        "pre_gain": jnp.clip(1.0 + 0.1 * jax.random.normal(splits[3], (D,), jnp.float32), 0.5, 1.5),
        "w_inner": draw_w_inner(jax.random.fold_in(splits[21], 71), 0),
        "w_group": scatter_about(splits[5], (D, 2, GROUPS, STATE), D ** -0.5, 0.09375, ((2, 4),)),
        "w_step": scatter_about(splits[6], (D, HEADS), D ** -0.5, 0.09375, ((1, 16),)),
        "conv_inner": jnp.clip(jax.random.uniform(splits[7], (KERNEL, E), jnp.float32, -0.5, 0.5) * steps_of(splits[7], (KERNEL, E), ((1, 16),), -0.4, 0.0), -0.5, 0.5),
        "conv_group": jnp.clip(jax.random.uniform(splits[8], (KERNEL, 2, GROUPS, STATE), jnp.float32, -0.5, 0.5) * steps_of(splits[8], (KERNEL, 2, GROUPS, STATE), ((2, 4),), -0.4, 0.0), -0.5, 0.5),
        "conv_bias_inner": jnp.clip(jax.random.uniform(splits[9], (E,), jnp.float32, -0.5, 0.5) * steps_of(splits[9], (E,), ((0, 16),), -0.4, 0.0), -0.5, 0.5),
        "conv_bias_group": jnp.clip(jax.random.uniform(splits[10], (2, GROUPS, STATE), jnp.float32, -0.5, 0.5) * steps_of(splits[10], (2, GROUPS, STATE), ((1, 4),), -0.4, 0.0), -0.5, 0.5),
        "edge_inner": scatter_about(splits[11], (REQS, KERNEL - 1, E), 1.0, 6.0, ((2, 16),)),
        "edge_group": scatter_about(splits[12], (REQS, KERNEL - 1, 2, GROUPS, STATE), 1.0, 6.0, ((3, 4),)),
        "init_states": scatter_about(splits[13], (REQS, HEADS, HEAD, STATE), (STATE ** -0.5), 1.25, ((1, 16),), jnp.float32),
        "step_bias": jnp.clip(-5.3 + 3.0000002 * jax.random.uniform(splits[14], (HEADS,), jnp.float32) ** steps_of(splits[14], (HEADS,), ((0, 16),), -0.2, 0.2), -5.3, -2.3),
        "decay_log": jnp.clip(-3.9 + 3.9 * jax.random.uniform(splits[15], (HEADS,), jnp.float32) ** steps_of(splits[15], (HEADS,), ((0, 16),), -0.2, 0.2), -3.9, 0.0),
        "skip": jnp.clip(0.5 + 1.0 * jax.random.uniform(splits[16], (HEADS,), jnp.float32) ** steps_of(splits[16], (HEADS,), ((0, 16),), -0.2, 0.2), 0.5, 1.5),
        "inner_gain": jnp.clip(1.0 + 0.1 * jax.random.normal(splits[17], (E,), jnp.float32), 0.5, 1.5),
        "w_out": heavy_noise(splits[18], (E, D), E ** -0.5, 0.09375, ((0, 16),), (0, 1, 16, 2.0)),
        "final_gain": jnp.clip(1.0 + 0.1 * jax.random.normal(splits[19], (D,), jnp.float32), 0.5, 1.5),
        "w_head": scatter_about(splits[20], (D, VOCAB), D ** -0.5, 0.09375, ((1, 32),)),
    }


EPSILON = 1e-05
HIGHEST = lax.Precision.HIGHEST

def rms_scale(values, axis):
    return lax.rsqrt(lax.optimization_barrier(jnp.mean(values * values, axis=axis)) + EPSILON)

def block_basics(log_block, seg_block, prev_block):
    running = jnp.cumsum(log_block, axis=0)
    flag = seg_block == prev_block[0]
    lower = jnp.arange(BLOCK)[:, None] >= jnp.arange(BLOCK)[None, :]
    same = (seg_block[:, None] == seg_block[None, :]) & lower
    first = seg_block != prev_block
    base = jnp.einsum('ts,sh->th', (same & first[None, :]).astype(jnp.float32), running - log_block, precision=HIGHEST)
    init_coef = jnp.where(flag[:, None], 0.0, jnp.exp(running - base))
    carry_coef = jnp.where(flag[:, None], jnp.exp(running), 0.0)
    return (running, same, init_coef, carry_coef)

def state_at(place, entry, x_block, key_heads, step_block, running, same, init_coef, carry_coef, seg_block, init_dealt):
    keep = same[place][:, None]
    decay_row = jnp.where(keep, jnp.exp(jnp.where(keep, running[place][None, :] - running, 0.0)), 0.0)
    share = (decay_row * step_block).astype(jnp.bfloat16)
    share = lax.optimization_barrier(share).astype(jnp.float32)
    term = jnp.einsum('sh,shp,shn->hpn', share, x_block.astype(jnp.float32), key_heads, precision=HIGHEST)
    chosen = init_dealt[seg_block[place]]
    return term + init_coef[place][:, None, None] * chosen + carry_coef[place][:, None, None] * entry

def reference(tokens, lengths, deal, pre_gain, w_inner, w_group, w_step, conv_inner, conv_group, conv_bias_inner, conv_bias_group, edge_inner, edge_group, init_states, step_bias, decay_log, skip, inner_gain, w_out, final_gain, w_head):
    wide = tokens.astype(jnp.float32)
    inv_rms = rms_scale(wide, 1)[:, None]
    scaled = (wide * pre_gain).astype(jnp.bfloat16)
    gate_x = jnp.dot(scaled, w_inner.reshape(D, 2 * E), preferred_element_type=jnp.float32) * inv_rms
    gate_in = gate_x[:, :E].astype(jnp.bfloat16)
    inner_in = gate_x[:, E:].astype(jnp.bfloat16)
    pair_width = 2 * GROUPS * STATE
    group_in = (jnp.dot(scaled, w_group.reshape(D, pair_width), preferred_element_type=jnp.float32) * inv_rms).astype(jnp.bfloat16)
    step_raw = jnp.dot(scaled, w_step, preferred_element_type=jnp.float32) * inv_rms
    ends = jnp.cumsum(lengths).astype(jnp.int32)
    begins = (ends - lengths).astype(jnp.int32)
    position = jnp.arange(TOKENS, dtype=jnp.int32)
    segment = (lax.optimization_barrier(jnp.sum((begins[None, :] <= position[:, None]).astype(jnp.int32), axis=1)) - 1).astype(jnp.int32)
    seg_before = (lax.optimization_barrier(jnp.sum((begins[None, :] < position[:, None]).astype(jnp.int32), axis=1)) - 1).astype(jnp.int32)
    offset = (position - begins[segment]).astype(jnp.int32)
    owner = deal[segment].astype(jnp.int32)
    channels = jnp.concatenate([inner_in, group_in], axis=1)
    conv_taps = jnp.concatenate([conv_inner, conv_group.reshape(KERNEL, pair_width)], axis=1)
    conv_shift = jnp.concatenate([conv_bias_inner, conv_bias_group.reshape(pair_width)])
    edges = jnp.concatenate([edge_inner, edge_group.reshape(REQS, KERNEL - 1, pair_width)], axis=2)
    summed = conv_shift + conv_taps[KERNEL - 1] * channels.astype(jnp.float32)
    for back in range(1, KERNEL):
        earlier = jnp.concatenate([jnp.zeros((back, channels.shape[1]), jnp.bfloat16), channels[:-back]], axis=0)
        slot = jnp.clip(KERNEL - 1 - back + offset, 0, KERNEL - 2).astype(jnp.int32)
        from_edge = edges[owner, slot]
        value = jnp.where((offset >= back)[:, None], earlier, from_edge)
        summed = summed + conv_taps[KERNEL - 1 - back] * value.astype(jnp.float32)
    mixed_in = jax.nn.silu(summed).astype(jnp.bfloat16)
    inner_x = mixed_in[:, :E].reshape(TOKENS, HEADS, HEAD)
    keys = mixed_in[:, E:E + GROUPS * STATE].reshape(TOKENS, GROUPS, STATE)
    queries = mixed_in[:, E + GROUPS * STATE:].reshape(TOKENS, GROUPS, STATE)
    step = jax.nn.softplus(step_raw + step_bias)
    log_decay = -jnp.exp(decay_log) * step
    init_dealt = init_states[deal]
    blocks = TOKENS // BLOCK
    repeat = HEADS // GROUPS

    def heads_of(grouped):
        return jnp.repeat(grouped.astype(jnp.float32), repeat, axis=1)

    def shaped(values):
        return values.reshape((blocks, BLOCK) + values.shape[1:])
    pieces = (shaped(inner_x), shaped(keys), shaped(queries), shaped(step), shaped(log_decay), shaped(segment), shaped(seg_before))

    def block_step(entry, block_pieces):
        x_block, key_block, query_block, step_block, log_block, seg_block, prev_block = block_pieces
        running, same, init_coef, carry_coef = block_basics(log_block, seg_block, prev_block)
        keep = same[:, :, None]
        diff = running[:, None, :] - running[None, :, :]
        decay = jnp.where(keep, jnp.exp(jnp.where(keep, diff, 0.0)), 0.0)
        scores = jnp.einsum('tgn,sgn->tsg', query_block.astype(jnp.float32), key_block.astype(jnp.float32), precision=HIGHEST)
        scores = jnp.repeat(scores, repeat, axis=2)
        weight = (scores * decay * step_block[None, :, :]).astype(jnp.bfloat16)
        weight = lax.optimization_barrier(weight).astype(jnp.float32)
        within = jnp.einsum('tsh,shp->thp', weight, x_block.astype(jnp.float32), precision=HIGHEST)
        query_heads = heads_of(query_block)

        def init_piece(piece_in):
            query_part, seg_part = piece_in
            return jnp.einsum('thn,thpn->thp', query_part, init_dealt[seg_part], precision=HIGHEST)
        init_dot = lax.map(init_piece, (query_heads.reshape(BLOCK // 16, 16, HEADS, STATE), seg_block.reshape(BLOCK // 16, 16)))
        init_dot = init_dot.reshape(BLOCK, HEADS, HEAD)
        carry_dot = jnp.einsum('thn,hpn->thp', query_heads, entry, precision=HIGHEST)
        result = within + init_coef[:, :, None] * init_dot
        result = result + carry_coef[:, :, None] * carry_dot
        result = result + skip[None, :, None] * x_block.astype(jnp.float32)
        leaving = state_at(BLOCK - 1, entry, x_block, heads_of(key_block), step_block, running, same, init_coef, carry_coef, seg_block, init_dealt)
        return (leaving, (result, entry))
    entry_zero = jnp.zeros((HEADS, HEAD, STATE), jnp.float32)
    _, (results, entries) = lax.scan(block_step, entry_zero, pieces)

    def final_of(request):
        last = ends[request] - 1
        which = (last // BLOCK).astype(jnp.int32)
        place = (last % BLOCK).astype(jnp.int32)

        def take(values):
            return lax.dynamic_index_in_dim(values, which, 0, keepdims=False)
        running, same, init_coef, carry_coef = block_basics(take(pieces[4]), take(pieces[5]), take(pieces[6]))
        return state_at(place, take(entries), take(pieces[0]), heads_of(take(pieces[1])), take(pieces[3]), running, same, init_coef, carry_coef, take(pieces[5]), init_dealt)
    finals = lax.map(final_of, jnp.arange(REQS, dtype=jnp.int32))
    final_states = jnp.zeros_like(init_states).at[deal].set(finals)
    y_flat = results.reshape(TOKENS, E)
    gated = y_flat * jax.nn.silu(gate_in.astype(jnp.float32))
    grouped = gated.reshape(TOKENS, GROUPS, E // GROUPS)
    normed = ((grouped * rms_scale(grouped, 2)[:, :, None]).reshape(TOKENS, E) * inner_gain).astype(jnp.bfloat16)
    mixed = jnp.dot(normed, w_out, preferred_element_type=jnp.float32)
    hidden_out = (wide + mixed).astype(jnp.bfloat16)
    last_rows = hidden_out[ends - 1].astype(jnp.float32)
    head_in = (last_rows * rms_scale(last_rows, 1)[:, None] * final_gain).astype(jnp.bfloat16)
    scores_out = jnp.dot(head_in, w_head, preferred_element_type=jnp.float32)
    logits = jnp.zeros((REQS, VOCAB), jnp.float32).at[deal].set(scores_out)
    return (hidden_out, final_states, logits)
```

```python
import jax
import jax.numpy as jnp
from jax import lax
from jax.sharding import PartitionSpec as P

BLOCK = 256


EPSILON = 1e-05
HIGHEST = lax.Precision.HIGHEST


def from_behind(block, axis, distance):
    devices = range(lax.axis_size(axis))
    route = [(i - distance, i) for i in devices if i - distance in devices]
    return lax.ppermute(block, axis, route)


def from_partner(x, axis, bit):
    return lax.ppermute(x, axis, [(i, i ^ 1 << bit) for i in range(lax.axis_size(axis))])


def from_ahead(x, axis, distance):
    size = lax.axis_size(axis)
    return lax.ppermute(x, axis, [((i + distance) % size, i) for i in range(size)])


def plane_gather(block):
    half = block.shape[0] // 2
    width = block.shape[1]
    upper, lower = block[:half], block[half:]
    upper_far = from_partner(upper, "row", 1)
    lower_near = from_partner(lower, "row", 0)
    upper_rest = from_partner(jnp.concatenate([upper, upper_far], axis=1), "row", 0)
    lower_rest = from_partner(jnp.concatenate([lower, lower_near], axis=1), "row", 1)
    upper_all = [upper, upper_rest[:, :width], upper_far, upper_rest[:, width:]]
    lower_all = [lower, lower_near, lower_rest[:, :width], lower_rest[:, width:]]
    return jnp.concatenate(
        [jnp.concatenate(upper_all, axis=1), jnp.concatenate(lower_all, axis=1)], axis=0
    )


def plane_scatter(part):
    half = part.shape[0] // 2
    upper, lower = part[:half], part[half:]

    def sent(x):
        return x.astype(jnp.bfloat16)

    def taken(x):
        return x.astype(jnp.float32)

    upper_near = [upper[:, 0], upper[:, 2]]
    got = from_partner(sent(jnp.concatenate([upper[:, 1], upper[:, 3]], axis=1)), "row", 0)
    width = part.shape[2]
    upper_near = [upper[:, 0] + taken(got[:, :width]), upper[:, 2] + taken(got[:, width:])]
    upper_sum = upper_near[0] + taken(from_partner(sent(upper_near[1]), "row", 1))
    got = from_partner(sent(jnp.concatenate([lower[:, 2], lower[:, 3]], axis=1)), "row", 1)
    lower_near = [lower[:, 0] + taken(got[:, :width]), lower[:, 1] + taken(got[:, width:])]
    lower_sum = lower_near[0] + taken(from_partner(sent(lower_near[1]), "row", 0))
    return jnp.concatenate([upper_sum, lower_sum], axis=0)


def pick_group(table, axis, which):
    return lax.dynamic_index_in_dim(table, which, axis, keepdims=False)


def exact_pairs(spread, keys_bf, form):
    upper = spread.astype(jnp.bfloat16)
    lower_part = (spread - upper.astype(jnp.float32)).astype(jnp.bfloat16)
    first_term = jnp.einsum(form, upper, keys_bf, preferred_element_type=jnp.float32)
    return first_term + jnp.einsum(form, lower_part, keys_bf, preferred_element_type=jnp.float32)


def per_device(
    tokens,
    lengths,
    deal,
    pre_gain,
    w_inner,
    w_group,
    w_step,
    conv_inner,
    conv_group,
    conv_bias_inner,
    conv_bias_group,
    edge_inner,
    edge_group,
    init_states,
    step_bias,
    decay_log,
    skip,
    inner_gain,
    w_out,
    final_gain,
    w_head,
):
    rows = tokens.shape[0]
    model_width = pre_gain.shape[0]
    requests = lengths.shape[0]
    kernel = conv_inner.shape[0]
    inner_dev = w_inner.shape[2]
    heads_dev = w_step.shape[1]
    head_size = inner_dev // heads_dev
    state_size = w_group.shape[3]
    group_local = lax.axis_index("col") * w_group.shape[2] // lax.axis_size("col")
    w_gate_x = jnp.reshape(w_inner, (model_width, 2 * inner_dev))
    w_pair = jnp.reshape(pick_group(w_group, 2, group_local), (model_width, 2 * state_size))
    row_at, col_at = lax.axis_index("row"), lax.axis_index("col")
    row_size, col_size = lax.axis_size("row"), lax.axis_size("col")
    width = tokens.shape[1]
    w_all = jnp.concatenate([w_gate_x, w_pair, w_step], axis=1)
    ends = jnp.cumsum(lengths)
    begins = ends - lengths
    first_row = lax.axis_index("seq") * rows
    slot_end = jnp.sum(
        jnp.where(deal[None, :] == jnp.arange(requests, dtype=jnp.int32)[:, None], ends[None, :], 0),
        axis=1,
    )
    chooser = (
        slot_end[:, None] - 1 - first_row == jnp.arange(rows, dtype=jnp.int32)[None, :]
    ).astype(jnp.bfloat16)

    def feature_rows(table, shift, across):
        block = (row_at ^ across) * col_size + (col_at + shift) % col_size
        return lax.dynamic_slice_in_dim(table, block * width, width, 0)

    projected = 0.0
    squares = 0.0
    token_ends = []
    for shift in range(col_size):
        block = tokens if shift == 0 else from_ahead(tokens, "col", shift)
        part = plane_gather(block)
        token_ends.append(jnp.dot(chooser, part, preferred_element_type=jnp.float32))
        part = part.astype(jnp.float32)
        gains = jnp.concatenate([feature_rows(pre_gain, shift, i) for i in range(row_size)])
        w_part = jnp.concatenate([feature_rows(w_all, shift, i) for i in range(row_size)], axis=0)
        scaled = (part * gains).astype(jnp.bfloat16)
        projected = projected + jnp.dot(scaled, w_part, preferred_element_type=jnp.float32)
        squares = squares + jnp.sum(part * part, axis=1)
    gate_x = projected[:, : 2 * inner_dev]
    pair = projected[:, 2 * inner_dev : 2 * inner_dev + 2 * state_size]
    steps = projected[:, 2 * inner_dev + 2 * state_size :]
    inv_rms = lax.rsqrt(squares / model_width + EPSILON)[:, None]
    gate_in = (gate_x[:, :inner_dev] * inv_rms).astype(jnp.bfloat16)
    inner_in = (gate_x[:, inner_dev:] * inv_rms).astype(jnp.bfloat16)
    pair_in = (pair * inv_rms).astype(jnp.bfloat16)
    step_raw = steps * inv_rms
    position = first_row + jnp.arange(rows, dtype=jnp.int32)
    segment = jnp.sum((begins[None, :] <= position[:, None]).astype(jnp.int32), axis=1) - 1
    seg_before = jnp.sum((begins[None, :] < position[:, None]).astype(jnp.int32), axis=1) - 1
    member = segment[:, None] == jnp.arange(requests, dtype=jnp.int32)[None, :]
    offset = position - jnp.sum(jnp.where(member, begins[None, :], 0), axis=1)
    owner = jnp.sum(jnp.where(member, deal[None, :], 0), axis=1)
    channels = jnp.concatenate([inner_in, pair_in], axis=1)
    width_all = channels.shape[1]
    conv_taps = jnp.concatenate(
        [conv_inner, jnp.reshape(pick_group(conv_group, 2, group_local), (kernel, 2 * state_size))],
        axis=1,
    )
    conv_shift = jnp.concatenate(
        [
            conv_bias_inner,
            jnp.reshape(pick_group(conv_bias_group, 1, group_local), (2 * state_size,)),
        ]
    )
    edges = jnp.concatenate(
        [
            edge_inner,
            jnp.reshape(
                pick_group(edge_group, 3, group_local), (requests, kernel - 1, 2 * state_size)
            ),
        ],
        axis=2,
    )
    edges = jnp.reshape(edges, (requests * (kernel - 1), width_all))
    rim = from_behind(channels[rows - (kernel - 1) :], "seq", 1)
    extended = jnp.concatenate([rim, channels], axis=0)
    summed = conv_shift + conv_taps[kernel - 1] * channels.astype(jnp.float32)
    slots = jnp.arange(requests * (kernel - 1), dtype=jnp.int32)
    for back in range(1, kernel):
        earlier = extended[kernel - 1 - back : kernel - 1 - back + rows]
        slot = owner * (kernel - 1) + (kernel - 1 - back) + offset
        lookup = ((slot[:, None] == slots[None, :]) & (offset < back)[:, None]).astype(jnp.bfloat16)
        from_edge = jnp.dot(lookup, edges, preferred_element_type=jnp.float32)
        value = jnp.where((offset >= back)[:, None], earlier.astype(jnp.float32), from_edge)
        summed = summed + conv_taps[kernel - 1 - back] * value
    mixed_in = jax.nn.silu(summed).astype(jnp.bfloat16)
    blocks = rows // BLOCK
    inner_x = jnp.reshape(mixed_in[:, :inner_dev], (blocks, BLOCK, heads_dev, head_size))
    keys = jnp.reshape(mixed_in[:, inner_dev : inner_dev + state_size], (blocks, BLOCK, state_size))
    queries = jnp.reshape(mixed_in[:, inner_dev + state_size :], (blocks, BLOCK, state_size))
    step = jax.nn.softplus(step_raw + step_bias)
    log_decay = -jnp.exp(decay_log) * step
    step_blocks = jnp.reshape(step, (blocks, BLOCK, heads_dev))
    log_blocks = jnp.reshape(log_decay, (blocks, BLOCK, heads_dev))
    running = jnp.cumsum(log_blocks, axis=1)
    seg_blocks = jnp.reshape(segment, (blocks, BLOCK))
    prev_blocks = jnp.reshape(seg_before, (blocks, BLOCK))
    flag = seg_blocks == prev_blocks[:, :1]
    lower = jnp.arange(BLOCK)[:, None] >= jnp.arange(BLOCK)[None, :]
    same = (seg_blocks[:, :, None] == seg_blocks[:, None, :]) & lower[None]
    first = seg_blocks != prev_blocks
    base = jnp.einsum(
        "cts,csh->cth",
        (same & first[:, None, :]).astype(jnp.float32),
        running - log_blocks,
        precision=HIGHEST,
    )
    keep = same[..., None]
    diff = running[:, :, None, :] - running[:, None, :, :]
    decay = jnp.where(keep, jnp.exp(jnp.where(keep, diff, 0.0)), 0.0)
    scores = jnp.einsum("ctn,csn->cts", queries, keys, preferred_element_type=jnp.float32)
    weight = (scores[..., None] * decay * step_blocks[:, None, :, :]).astype(jnp.bfloat16)
    within = jnp.einsum("ctsh,cshp->cthp", weight, inner_x, preferred_element_type=jnp.float32)
    dealing = (deal[:, None] == jnp.arange(requests, dtype=jnp.int32)[None, :]).astype(jnp.float32)
    init_dealt = jnp.reshape(
        jnp.dot(dealing, jnp.reshape(init_states, (requests, -1)), precision=HIGHEST),
        init_states.shape,
    )
    member_blocks = jnp.reshape(member.astype(jnp.float32), (blocks, BLOCK, requests))
    query_wide = queries.astype(jnp.float32)
    picked = jnp.where(
        jnp.reshape(member, (blocks, BLOCK, requests))[..., None],
        queries[:, :, None, :],
        jnp.zeros((), jnp.bfloat16),
    )
    init_high = init_dealt.astype(jnp.bfloat16)
    init_rest = init_dealt - init_high.astype(jnp.float32)
    init_mid = init_rest.astype(jnp.bfloat16)
    init_low = (init_rest - init_mid.astype(jnp.float32)).astype(jnp.bfloat16)
    init_dot = jnp.einsum("ctrn,rhpn->cthp", picked, init_high, preferred_element_type=jnp.float32)
    init_dot = init_dot + jnp.einsum(
        "ctrn,rhpn->cthp", picked, init_mid, preferred_element_type=jnp.float32
    )
    init_dot = init_dot + jnp.einsum(
        "ctrn,rhpn->cthp", picked, init_low, preferred_element_type=jnp.float32
    )
    init_coef = jnp.where(flag[..., None], 0.0, jnp.exp(running - base))
    carry_coef = jnp.where(flag[..., None], jnp.exp(running), 0.0)
    local_y = within + init_coef[..., None] * init_dot
    end_local = ends - 1 - first_row
    local_pos = jnp.reshape(jnp.arange(rows, dtype=jnp.int32), (blocks, BLOCK))
    select = (local_pos[:, None, :] == end_local[None, :, None]).astype(jnp.float32)
    block_pick = jnp.sum(select, axis=2)
    sel_init = jnp.einsum("cjt,cth->cjh", select, init_coef, precision=HIGHEST)
    sel_carry = jnp.einsum("cjt,cth->cjh", select, carry_coef, precision=HIGHEST)
    sel_member = jnp.einsum("cjt,ctr->cjr", select, member_blocks, precision=HIGHEST)
    sel_inits = jnp.einsum("cjr,rhpn->cjhpn", sel_member, init_dealt, precision=HIGHEST)
    decay_req = jnp.einsum("cjt,ctsh->jsh", select, decay, precision=HIGHEST)
    step_req = jnp.einsum("cj,csh->jsh", block_pick, step_blocks, precision=HIGHEST)
    pick_bf = block_pick.astype(jnp.bfloat16)
    x_req = jnp.einsum(
        "cj,cshp->jshp", pick_bf, inner_x, preferred_element_type=jnp.float32
    ).astype(jnp.bfloat16)
    keys_req = jnp.einsum("cj,csn->jsn", pick_bf, keys, preferred_element_type=jnp.float32).astype(
        jnp.bfloat16
    )
    share_req = (decay_req * step_req).astype(jnp.bfloat16)
    share_req = lax.optimization_barrier(share_req).astype(jnp.float32)
    spread_req = share_req[..., None] * x_req.astype(jnp.float32)
    local_req = exact_pairs(spread_req, keys_req, "jshp,jsn->jhpn")
    share_last = (decay[:, BLOCK - 1] * step_blocks).astype(jnp.bfloat16)
    share_last = lax.optimization_barrier(share_last).astype(jnp.float32)
    spread_last = share_last[..., None] * inner_x.astype(jnp.float32)
    last_state = exact_pairs(spread_last, keys, "cshp,csn->chpn")
    last_init = init_coef[:, BLOCK - 1]
    last_member = member_blocks[:, BLOCK - 1]
    last_inits = jnp.einsum("cr,rhpn->chpn", last_member, init_dealt, precision=HIGHEST)
    last_state = last_state + last_init[..., None, None] * last_inits
    last_carry = carry_coef[:, BLOCK - 1]
    gain_run = jnp.ones((heads_dev,), jnp.float32)
    state_run = jnp.zeros((heads_dev, head_size, state_size), jnp.float32)
    gain_list = []
    state_list = []
    for block in range(blocks):
        gain_list.append(gain_run)
        state_list.append(state_run)
        factor = last_carry[block]
        gain_run = factor * gain_run
        state_run = factor[:, None, None] * state_run + last_state[block]

    def relay_step(turn, entering):
        leaving = gain_run[:, None, None] * entering + state_run
        return from_behind(leaving, "seq", 1)

    entry_dev = lax.fori_loop(0, lax.axis_size("seq") - 1, relay_step, jnp.zeros_like(state_run))
    entries = jnp.stack(gain_list)[:, :, None, None] * entry_dev[None] + jnp.stack(state_list)
    carry_dot = jnp.einsum("ctn,chpn->cthp", query_wide, entries, precision=HIGHEST)
    outputs = local_y + carry_coef[..., None] * carry_dot
    outputs = outputs + skip[:, None] * inner_x.astype(jnp.float32)
    finals = local_req + jnp.sum(sel_init[..., None, None] * sel_inits, axis=0)
    finals = finals + jnp.sum(sel_carry[..., None, None] * entries[:, None], axis=0)
    owned = jnp.reshape(
        jnp.dot(dealing.T, jnp.reshape(finals, (requests, -1)), precision=HIGHEST), finals.shape
    )
    final_states = lax.psum_scatter(owned, "seq", scatter_dimension=0, tiled=True)
    y_flat = jnp.reshape(outputs, (rows, inner_dev))
    gated = y_flat * jax.nn.silu(gate_in.astype(jnp.float32))
    own_squares = jnp.sum(gated * gated, axis=1)
    other_squares = from_partner(own_squares, "col", 0)
    norm_scale = lax.rsqrt((own_squares + other_squares) / (2 * inner_dev) + EPSILON)
    normed = (gated * norm_scale[:, None] * inner_gain).astype(jnp.bfloat16)
    w_out_blocks = jnp.reshape(w_out, (inner_dev, row_size, col_size, width))
    order = [(row_at ^ i) for i in range(row_size)]
    normed_ends = jnp.dot(chooser, normed, preferred_element_type=jnp.float32).astype(jnp.bfloat16)
    end_sum = jnp.dot(normed_ends, w_out, preferred_element_type=jnp.float32)
    for axis, bit in (("row", 0), ("row", 1), ("col", 0), ("col", 1)):
        end_sum = end_sum + from_partner(end_sum.astype(jnp.bfloat16), axis, bit).astype(
            jnp.float32
        )
    mixed = 0.0
    for shift in (2, 1, 3, 0):
        w_cols = lax.dynamic_index_in_dim(
            w_out_blocks, (col_at + shift) % col_size, 2, keepdims=False
        )
        parts = [
            jnp.dot(
                normed,
                lax.dynamic_index_in_dim(w_cols, i, 1, keepdims=False),
                preferred_element_type=jnp.float32,
            )
            for i in order
        ]
        summed_part = plane_scatter(jnp.stack(parts, axis=1))
        if shift:
            summed_part = from_ahead(
                summed_part.astype(jnp.bfloat16), "col", col_size - shift
            ).astype(jnp.float32)
        mixed = mixed + summed_part
    hidden_out = (tokens.astype(jnp.float32) + mixed).astype(jnp.bfloat16)
    ends_wide = jnp.zeros((requests, row_size, col_size, width), jnp.float32)
    for shift in range(col_size):
        for i in range(row_size):
            ends_wide = lax.dynamic_update_slice(
                ends_wide,
                jnp.reshape(
                    token_ends[shift][:, i * width : (i + 1) * width], (requests, 1, 1, width)
                ),
                (0, order[i], (col_at + shift) % col_size, 0),
            )
    ending = jnp.reshape(ends_wide, (requests, model_width)) + end_sum
    last_rows = lax.psum(ending, "seq").astype(jnp.bfloat16)
    last_wide = last_rows.astype(jnp.float32)
    final_scale = lax.rsqrt(jnp.sum(last_wide * last_wide, axis=1) / model_width + EPSILON)
    head_in = (last_wide * final_scale[:, None] * final_gain).astype(jnp.bfloat16)
    logits = jnp.dot(head_in, w_head, preferred_element_type=jnp.float32)
    return (hidden_out, final_states, logits)


def solution(mesh):
    in_specs = (
        P("seq", ("row", "col")),
        P(),
        P(),
        P(),
        P(None, None, ("row", "col")),
        P(None, None, "row", None),
        P(None, ("row", "col")),
        P(None, ("row", "col")),
        P(None, None, "row", None),
        P(("row", "col")),
        P(None, "row", None),
        P(None, None, ("row", "col")),
        P(None, None, None, "row", None),
        P(None, ("row", "col"), None, None),
        P(("row", "col")),
        P(("row", "col")),
        P(("row", "col")),
        P(("row", "col")),
        P(("row", "col"), None),
        P(),
        P(None, ("seq", "row", "col")),
    )
    out_specs = (
        P("seq", ("row", "col")),
        P("seq", ("row", "col"), None, None),
        P(None, ("seq", "row", "col")),
    )
    return jax.shard_map(
        per_device, mesh=mesh, in_specs=in_specs, out_specs=out_specs, check_vma=False
    )
```

```python
import functools

import jax
import jax.numpy as jnp
from jax import lax
from jax.experimental import pallas as pl
from jax.experimental.pallas import tpu as pltpu
from jax.sharding import PartitionSpec as P

EPSILON = 1e-05
HIGHEST = lax.Precision.HIGHEST
F32 = jnp.float32
BF16 = jnp.bfloat16
LANES = 128
RIM = 16
VMEM = 40 * 1024 * 1024
ROWS_BY_ROWS = (((1,), (1,)), ((), ()))


def from_behind(block, axis, distance):
    devices = range(lax.axis_size(axis))
    route = [(i - distance, i) for i in devices if i - distance in devices]
    return lax.ppermute(block, axis, route)


def from_partner(x, axis, bit):
    return lax.ppermute(x, axis, [(i, i ^ 1 << bit) for i in range(lax.axis_size(axis))])


def from_ahead(x, axis, distance):
    size = lax.axis_size(axis)
    return lax.ppermute(x, axis, [((i + distance) % size, i) for i in range(size)])


def call(kernel, outs, *args, prefetch=None, grid=(1,), in_specs=None, out_specs=None, cost=(0, 0)):
    params = pltpu.CompilerParams(vmem_limit_bytes=VMEM)
    shapes = [jax.ShapeDtypeStruct(shape, kind) for shape, kind in outs]

    def whole(shape):
        zeros = (0,) * len(shape)
        return pl.BlockSpec(shape, lambda *_: zeros)

    specs = [
        whole(a.shape) if spec is None else spec
        for a, spec in zip(args, in_specs or [None] * len(args))
    ]
    gives = [
        whole(shape) if spec is None else spec
        for (shape, _), spec in zip(outs, out_specs or [None] * len(outs))
    ]
    prefetch = jnp.zeros((1,), jnp.int32) if prefetch is None else prefetch
    spec = pltpu.PrefetchScalarGridSpec(
        num_scalar_prefetch=1, grid=grid, in_specs=specs, out_specs=gives
    )
    flops, moved = cost
    return pl.pallas_call(
        kernel,
        out_shape=shapes,
        grid_spec=spec,
        compiler_params=params,
        cost_estimate=pl.CostEstimate(flops=flops, bytes_accessed=moved, transcendentals=0),
    )(prefetch, *args)


def plane_gather(block):
    half = block.shape[0] // 2
    upper, lower = block[:half], block[half:]
    upper_far = from_partner(upper, "row", 1)
    lower_near = from_partner(lower, "row", 0)
    upper_rest = from_partner(jnp.concatenate([upper, upper_far], axis=1), "row", 0)
    lower_rest = from_partner(jnp.concatenate([lower, lower_near], axis=1), "row", 1)
    return upper, upper_far, upper_rest, lower, lower_near, lower_rest


def table_kernel(which, group_ref, step_ref, out_ref):
    rows, pair, _, state = group_ref.shape
    flat = group_ref[...].reshape(rows * pair * 2, state)
    depth = 256
    take = depth // 4
    row = lax.broadcasted_iota(jnp.int32, (depth // 2, depth), 0)
    column = lax.broadcasted_iota(jnp.int32, (depth // 2, depth), 1)
    source = jnp.where(row < take, 4 * row, 4 * (row - take) + 2) + which[0]
    pick = jnp.where(source == column, 1.0, 0.0).astype(BF16)
    for at in range(rows // take):
        got = jnp.dot(pick, flat[at * depth : (at + 1) * depth], preferred_element_type=F32)
        got = got.astype(BF16)
        out_ref[at * take : (at + 1) * take, :state] = got[:take]
        out_ref[at * take : (at + 1) * take, state : 2 * state] = got[take:]
    out_ref[:, 2 * state :] = jnp.zeros((rows, LANES), BF16)
    out_ref[:, 2 * state : 2 * state + step_ref.shape[1]] = step_ref[...]


def project_kernel(first, last, width, inner, model_width, blocks, *refs):
    del blocks
    pieces, refs = refs[:6], refs[6:]
    chooser_ref, refs = refs[0], refs[1:]
    gains, w_main, w_rest, refs = refs[:4], refs[4:8], refs[8:12], refs[12:]
    if not first:
        total_in, squares_in, refs = refs[0], refs[1], refs[2:]
    ends_ref, refs = refs[0], refs[1:]
    upper, upper_far, upper_rest, lower, lower_near, lower_rest = [p[...] for p in pieces]
    tops = [upper, upper_rest[:, :width], upper_far, upper_rest[:, width:]]
    bottoms = [lower, lower_near, lower_rest[:, :width], lower_rest[:, width:]]
    raw = [jnp.concatenate([top, bottom], axis=0) for top, bottom in zip(tops, bottoms)]
    ends_ref[...] = jnp.dot(
        chooser_ref[...], jnp.concatenate(raw, axis=1), preferred_element_type=F32
    )
    squares = None if first else squares_in[...]
    scaled = []
    for piece, gain in zip(raw, gains):
        wide = piece.astype(F32)
        scaled.append((wide * gain[...]).astype(BF16))
        square = wide * wide
        for at in range(0, width, LANES):
            part = square[:, at : at + LANES]
            squares = part if squares is None else squares + part
    scaled = jnp.concatenate(scaled, axis=1)
    main = jnp.dot(
        scaled, jnp.concatenate([w[...] for w in w_main], axis=0), preferred_element_type=F32
    )
    rest = jnp.dot(
        scaled, jnp.concatenate([w[...] for w in w_rest], axis=0), preferred_element_type=F32
    )
    if not first:
        main = main + total_in[:, : 2 * inner]
        rest = rest + total_in[:, 2 * inner :]
    if not last:
        total_ref, squares_ref = refs
        total_ref[:, : 2 * inner] = main
        total_ref[:, 2 * inner :] = rest
        squares_ref[...] = squares
        return
    gate_ref, channels_ref, steps_ref = refs
    inv_rms = lax.rsqrt(jnp.sum(squares, axis=1, keepdims=True) / model_width + EPSILON)
    gate_ref[...] = (main[:, :inner] * inv_rms).astype(BF16)
    channels_ref[:, :inner] = (main[:, inner:] * inv_rms).astype(BF16)
    channels_ref[:, inner:] = (rest[:, :-LANES] * inv_rms).astype(BF16)
    steps_ref[...] = rest[:, -LANES:] * inv_rms


def both_heads(table, pair, head_size):
    rows = table.shape[0]
    lane = lax.broadcasted_iota(jnp.int32, (rows, 2 * head_size), 1)
    return jnp.where(
        lane < head_size, table[:, 2 * pair : 2 * pair + 1], table[:, 2 * pair + 1 : 2 * pair + 2]
    )


def over_states(row, heads, head_size):
    return jnp.concatenate(
        [jnp.broadcast_to(row[:, h : h + 1], (head_size, LANES)) for h in range(heads)], axis=0
    )


def conv_kernel(
    heads,
    owner_last,
    channels_ref,
    rim_ref,
    edges_ref,
    taps_ref,
    bias_ref,
    steps_ref,
    step_bias_ref,
    decay_ref,
    marks_ref,
    segment_ref,
    init_ref,
    x_ref,
    keys_ref,
    queries_ref,
    run_ref,
    less_ref,
    spread_ref,
    leaving_ref,
    gain_ref,
):
    del owner_last
    rows, inner = x_ref.shape
    state = keys_ref.shape[1]
    head_size = inner // heads
    taps = taps_ref.shape[0]
    channels = channels_ref[...]
    sources = jnp.concatenate([channels, rim_ref[...], edges_ref[...]], axis=0)
    summed = bias_ref[...] + taps_ref[taps - 1 : taps] * channels.astype(F32)
    column = lax.broadcasted_iota(jnp.int32, (rows, sources.shape[0]), 1)
    for back in range(1, taps):
        pick = jnp.where(marks_ref[:, back - 1 : back] == column, 1.0, 0.0).astype(BF16)
        value = jnp.dot(pick, sources, preferred_element_type=F32)
        summed = summed + taps_ref[taps - 1 - back : taps - back] * value
    mixed = (summed / (1.0 + jnp.exp(-summed))).astype(BF16)
    x = mixed[:, :inner]
    keys = mixed[:, inner : inner + state]
    x_ref[...] = x
    keys_ref[...] = keys
    queries_ref[...] = mixed[:, inner + state :]
    raw = steps_ref[...] + step_bias_ref[...]
    step = jnp.maximum(raw, 0.0) + jnp.log1p(jnp.exp(-jnp.abs(raw)))
    log_decay = -jnp.exp(decay_ref[...]) * step
    segment = marks_ref[:, 4:5]
    same = segment == segment_ref[0:1, :]
    row = lax.broadcasted_iota(jnp.int32, (rows, rows), 0)
    other = lax.broadcasted_iota(jnp.int32, (rows, rows), 1)
    until = jnp.where(same & (other <= row), 1.0, 0.0)
    after = jnp.where(same & (other > row), 1.0, 0.0)
    run = jnp.dot(until, log_decay, precision=HIGHEST, preferred_element_type=F32)
    tail = jnp.dot(after, log_decay, precision=HIGHEST, preferred_element_type=F32)
    run_ref[...] = run
    less_ref[...] = (run - jnp.log(step)).T[:8]
    share = (jnp.exp(tail) * step).astype(BF16).astype(F32)
    spread = jnp.concatenate(
        [
            both_heads(share, p, head_size)
            * x[:, p * 2 * head_size : (p + 1) * 2 * head_size].astype(F32)
            for p in range(heads // 2)
        ],
        axis=1,
    )
    spread = spread.T.astype(BF16)
    spread_ref[...] = spread
    last = jnp.where(segment == segment[rows - 1 : rows], 1.0, 0.0)
    leaving = jnp.dot(spread, (keys.astype(F32) * last).astype(BF16), preferred_element_type=F32)
    gain = jnp.exp(run[rows - 1 : rows])
    carried = jnp.broadcast_to(marks_ref[rows - 1 : rows, 5:6], (heads * head_size, state)) > 0
    gain_wide = over_states(gain, heads, head_size)
    leaving_ref[...] = jnp.where(carried, leaving, leaving + gain_wide * init_ref[0])
    gain_ref[...] = jnp.where(carried, gain_wide, 0.0)


def scan_kernel(
    heads,
    block,
    unused,
    x_ref,
    keys_ref,
    queries_ref,
    run_ref,
    less_ref,
    marks_ref,
    segment_ref,
    table_ref,
    skip_ref,
    y_ref,
    masked_ref,
    begun_ref,
):
    del unused
    rows, inner = x_ref.shape
    head_size = inner // heads
    slots = table_ref.shape[1] // queries_ref.shape[1]
    queries = queries_ref[...].astype(F32)
    slot = marks_ref[:, 3:4]
    placed = jnp.concatenate(
        [(queries * jnp.where(slot == o, 1.0, 0.0)).astype(BF16) for o in range(slots)], axis=1
    )
    begun_ref[...] = lax.dot_general(
        placed, table_ref[...], ROWS_BY_ROWS, preferred_element_type=F32
    )
    blocks = [(t, s) for t in range(rows // block) for s in range(t + 1)]
    for at, (t, s) in enumerate(blocks):
        here, there = pl.ds(t * block, block), pl.ds(s * block, block)
        scores = lax.dot_general(
            queries_ref[here], keys_ref[there], ROWS_BY_ROWS, preferred_element_type=F32
        )
        same = marks_ref[here, 4:5] == segment_ref[0:1, there]
        if t == s:
            row = lax.broadcasted_iota(jnp.int32, (block, block), 0)
            other = lax.broadcasted_iota(jnp.int32, (block, block), 1)
            same = same & (other <= row)
        masked_ref[at] = jnp.where(same, scores, 0.0)
    grown = jnp.exp(run_ref[...])
    lane = lax.broadcasted_iota(jnp.int32, (block, 2 * head_size), 1)
    for p in range(heads // 2):
        wide = slice(p * 2 * head_size, (p + 1) * 2 * head_size)
        x = x_ref[:, wide].astype(F32)
        y = both_heads(grown, p, head_size) * begun_ref[:, wide] + skip_ref[:, wide] * x
        sums = [y[t * block : (t + 1) * block] for t in range(rows // block)]
        for at, (t, s) in enumerate(blocks):
            here, there = slice(t * block, (t + 1) * block), slice(s * block, (s + 1) * block)
            for side in range(2):
                head = 2 * p + side
                mine = (lane < head_size) if side == 0 else (lane >= head_size)
                x_own = jnp.where(mine, x[there], 0.0).astype(BF16)
                gap = run_ref[here, head : head + 1] - less_ref[head : head + 1, there]
                weight = (masked_ref[at] * jnp.exp(jnp.minimum(gap, 80.0))).astype(BF16)
                sums[t] = sums[t] + jnp.dot(weight, x_own, preferred_element_type=F32)
        for t in range(rows // block):
            y_ref[t * block : (t + 1) * block, wide] = sums[t]


def gate_kernel(
    heads, unused, y_ref, queries_ref, run_ref, marks_ref, entry_ref, gate_ref, gain_ref, out_ref, sq_ref
):
    del unused
    rows, inner = y_ref.shape
    head_size = inner // heads
    carried = jnp.where(marks_ref[:, 5:6] > 0, 1.0, 0.0)
    queries = (queries_ref[...].astype(F32) * carried).astype(BF16)
    held = lax.dot_general(
        queries, entry_ref[...].astype(BF16), ROWS_BY_ROWS, preferred_element_type=F32
    )
    grown = jnp.exp(run_ref[...])
    grown = jnp.concatenate([both_heads(grown, p, head_size) for p in range(heads // 2)], axis=1)
    gate = gate_ref[...].astype(F32)
    gated = (y_ref[...] + grown * held) * (gate / (1.0 + jnp.exp(-gate)))
    out_ref[...] = (gated * gain_ref[...]).astype(BF16)
    square = jnp.sum(gated * gated, axis=1, keepdims=True)
    sq_ref[...] = jnp.broadcast_to(square, (rows, LANES)).T[:8]


def norm_scale(own_ref, other_ref, channels):
    scale = lax.rsqrt((own_ref[0:1] + other_ref[0:1]) / channels + EPSILON)
    return jnp.broadcast_to(scale, (LANES, scale.shape[1])).T


def out_kernel(
    width, blocks, gated_ref, own_ref, other_ref, w0, w1, w2, w3, upper_out, upper_in, lower_out, lower_in
):
    del blocks
    rows, inner = gated_ref.shape
    half = rows // 2
    scale = norm_scale(own_ref, other_ref, 2 * inner)
    scale = jnp.concatenate([scale] * (width // LANES), axis=1)
    gated = gated_ref[...]
    parts = [
        jnp.dot(gated, w[...], preferred_element_type=F32) * scale for w in (w0, w1, w2, w3)
    ]
    upper_in[:, :width] = parts[0][:half]
    upper_in[:, width:] = parts[2][:half]
    upper_out[:, :width] = parts[1][:half].astype(BF16)
    upper_out[:, width:] = parts[3][:half].astype(BF16)
    lower_in[:, :width] = parts[0][half:]
    lower_in[:, width:] = parts[1][half:]
    lower_out[:, :width] = parts[2][half:].astype(BF16)
    lower_out[:, width:] = parts[3][half:].astype(BF16)


def finals_kernel(heads, added, slots, spread_ref, keys_ref, marks_ref, ends_ref, entry_ref, init_ref, *refs):
    out_ref = refs[-1]
    head_size = spread_ref.shape[0] // heads
    slot = slots[pl.program_id(0)]
    here = jnp.where(marks_ref[:, 6:7] == slot, 1.0, 0.0) * ends_ref[0][:, heads : heads + 1]
    keys = (keys_ref[...].astype(F32) * here).astype(BF16)
    state = jnp.dot(spread_ref[...], keys, preferred_element_type=F32)
    gain = over_states(ends_ref[0], heads, head_size)
    carried = jnp.broadcast_to(ends_ref[0][:, heads + 1 : heads + 2], state.shape) > 0.5
    state = state + gain * jnp.where(carried, entry_ref[...], init_ref[0])
    out_ref[0] = state + refs[0][0] if added else state


def per_device(
    tokens,
    lengths,
    deal,
    pre_gain,
    w_inner,
    w_group,
    w_step,
    conv_inner,
    conv_group,
    conv_bias_inner,
    conv_bias_group,
    edge_inner,
    edge_group,
    init_states,
    step_bias,
    decay_log,
    skip,
    inner_gain,
    w_out,
    final_gain,
    w_head,
):
    rows, width = tokens.shape
    model_width = pre_gain.shape[0]
    requests = lengths.shape[0]
    taps = conv_inner.shape[0]
    inner = w_inner.shape[2]
    heads = w_step.shape[1]
    head_size = inner // heads
    state = w_group.shape[3]
    row_at, col_at, seq_at = (lax.axis_index(name) for name in ("row", "col", "seq"))
    row_size, col_size, seq_size = (lax.axis_size(name) for name in ("row", "col", "seq"))
    group_local = col_at * w_group.shape[2] // col_size
    across = [row_at ^ i for i in range(row_size)]

    def own_group(table, axis):
        return lax.dynamic_index_in_dim(table, group_local, axis, keepdims=False)

    def in_lanes(values):
        return jnp.pad(values, (0, LANES - heads))[None, :]

    slot_ids = jnp.arange(requests, dtype=jnp.int32)
    ends = jnp.cumsum(lengths)
    begins = ends - lengths
    first_row = seq_at * rows
    local = jnp.arange(rows, dtype=jnp.int32)
    position = first_row + local
    segment = jnp.sum((begins[None, :] <= position[:, None]).astype(jnp.int32), axis=1) - 1
    member = segment[:, None] == slot_ids[None, :]
    begin_of = jnp.sum(jnp.where(member, begins[None, :], 0), axis=1)
    offset = position - begin_of
    owner = jnp.sum(jnp.where(member, deal[None, :], 0), axis=1)
    carried = (begin_of < first_row).astype(jnp.int32)
    marks = [
        jnp.where(
            offset >= back,
            jnp.where(local >= back, local - back, rows + RIM + local - back),
            rows + RIM + owner * (taps - 1) + (taps - 1 - back) + offset,
        )
        for back in range(1, taps)
    ]
    marks += [jnp.where(carried > 0, requests, owner), segment, carried, owner, owner]
    marks = jnp.stack(marks, axis=1)
    segment_row = jnp.broadcast_to(segment[None, :], (8, rows))
    dealt = deal[None, :] == slot_ids[:, None]
    slot_end = jnp.sum(jnp.where(dealt, ends[None, :], 0), axis=1) - 1 - first_row
    slot_begin = jnp.sum(jnp.where(dealt, begins[None, :], 0), axis=1) - first_row
    ends_here = (slot_end >= 0) & (slot_end < rows)
    chooser = (slot_end[:, None] == local[None, :]).astype(BF16)

    w_main = jnp.reshape(w_inner, (model_width, 2 * inner))
    w_rows = 512
    (w_rest,) = call(
        table_kernel,
        [((model_width, 2 * state + LANES), BF16)],
        w_group,
        w_step,
        prefetch=jnp.reshape(group_local, (1,)).astype(jnp.int32),
        grid=(model_width // w_rows,),
        in_specs=[
            pl.BlockSpec((w_rows,) + w_group.shape[1:], lambda i, _: (i, 0, 0, 0)),
            pl.BlockSpec((w_rows, heads), lambda i, _: (i, 0)),
        ],
        out_specs=[pl.BlockSpec((w_rows, 2 * state + LANES), lambda i, _: (i, 0))],
        cost=(model_width * state * 512, 8 * model_width * state * 2),
    )
    init_flat = jnp.reshape(init_states, (requests, inner, state))
    table = jnp.reshape(
        jnp.transpose(init_flat.astype(BF16), (1, 0, 2)), (inner, requests * state)
    )
    conv_taps = jnp.concatenate(
        [conv_inner, jnp.reshape(own_group(conv_group, 2), (taps, 2 * state))], axis=1
    )
    conv_bias = jnp.concatenate(
        [conv_bias_inner, jnp.reshape(own_group(conv_bias_group, 1), (2 * state,))]
    )[None, :]
    edges = jnp.concatenate(
        [edge_inner, jnp.reshape(own_group(edge_group, 3), (requests, taps - 1, 2 * state))],
        axis=2,
    )
    edges = jnp.reshape(edges, (requests * (taps - 1), inner + 2 * state))
    skip_row = jnp.repeat(skip, head_size)[None, :]
    gains = pre_gain[None, :]

    n_main, n_rest = 2 * inner, 2 * state + LANES
    token_ends = []
    carry = ()
    for shift in range(col_size):
        first, last = shift == 0, shift == col_size - 1
        pieces = plane_gather(tokens if first else from_ahead(tokens, "col", shift))
        blocks = jnp.stack([a * col_size + (col_at + shift) % col_size for a in across])
        in_specs = [None] * 7
        in_specs += [
            pl.BlockSpec((1, width), lambda i, b, at=at: (0, b[at])) for at in range(row_size)
        ]
        for n in (n_main, n_rest):
            in_specs += [
                pl.BlockSpec((width, n), lambda i, b, at=at: (b[at], 0)) for at in range(row_size)
            ]
        in_specs += [None] * len(carry)
        outs = [((requests, row_size * width), F32)]
        if last:
            outs += [((rows, inner), BF16), ((rows, inner + 2 * state), BF16), ((rows, LANES), F32)]
        else:
            outs += [((rows, n_main + n_rest), F32), ((rows, LANES), F32)]
        piece_ends, *carry = call(
            functools.partial(project_kernel, first, last, width, inner, model_width),
            outs,
            *pieces,
            chooser,
            *[gains] * row_size,
            *[w_main] * row_size,
            *[w_rest] * row_size,
            *carry,
            prefetch=blocks.astype(jnp.int32),
            in_specs=in_specs,
            cost=(2 * rows * row_size * width * (n_main + n_rest), 8 * 1024 * 1024),
        )
        token_ends.append(piece_ends)
    gate_in, channels, step_raw = carry

    rim = from_behind(channels[rows - RIM :], "seq", 1)
    x, keys, queries, run, less, spread, leaving, gain_carried = call(
        functools.partial(conv_kernel, heads),
        [
            ((rows, inner), BF16),
            ((rows, state), BF16),
            ((rows, state), BF16),
            ((rows, LANES), F32),
            ((8, rows), F32),
            ((inner, rows), BF16),
            ((inner, state), F32),
            ((inner, state), F32),
        ],
        channels,
        rim,
        edges,
        conv_taps,
        conv_bias,
        step_raw,
        in_lanes(step_bias),
        in_lanes(decay_log),
        marks,
        segment_row,
        init_flat,
        prefetch=owner[rows - 1 :],
        in_specs=[None] * 10 + [pl.BlockSpec((1, inner, state), lambda i, b: (b[0], 0, 0))],
        cost=(6 * rows * rows * (inner + 2 * state), 8 * 1024 * 1024),
    )
    entry = from_behind(leaving, "seq", 1)
    for _ in range(seq_size - 2):
        entry = from_behind(gain_carried * entry + leaving, "seq", 1)

    block = 256
    pairs = (rows // block) * (rows // block + 1) // 2
    y = pl.pallas_call(
        functools.partial(scan_kernel, heads, block),
        out_shape=jax.ShapeDtypeStruct((rows, inner), F32),
        grid_spec=pltpu.PrefetchScalarGridSpec(
            num_scalar_prefetch=1,
            grid=(1,),
            in_specs=[
                pl.BlockSpec(a.shape, lambda *_: (0, 0))
                for a in (x, keys, queries, run, less, marks, segment_row, table, skip_row)
            ],
            out_specs=pl.BlockSpec((rows, inner), lambda *_: (0, 0)),
            scratch_shapes=[
                pltpu.VMEM((pairs, block, block), F32),
                pltpu.VMEM((rows, inner), F32),
            ],
        ),
        compiler_params=pltpu.CompilerParams(vmem_limit_bytes=VMEM),
        cost_estimate=pl.CostEstimate(
            flops=4 * rows * rows * inner, bytes_accessed=8 * 1024 * 1024, transcendentals=0
        ),
    )(
        jnp.zeros((1,), jnp.int32),
        x,
        keys,
        queries,
        run,
        less,
        marks,
        segment_row,
        table,
        skip_row,
    )
    gated, own_squares = call(
        functools.partial(gate_kernel, heads),
        [((rows, inner), BF16), ((8, rows), F32)],
        y,
        queries,
        run,
        marks,
        entry,
        gate_in,
        inner_gain[None, :],
        cost=(2 * rows * inner * state, 4 * 1024 * 1024),
    )
    other_squares = from_partner(own_squares, "col", 0)

    mixed = 0.0
    for shift in (2, 1, 3, 0):
        blocks = jnp.stack([a * col_size + (col_at + shift) % col_size for a in across])
        half = (rows // 2, 2 * width)
        upper_out, upper_in, lower_out, lower_in = call(
            functools.partial(out_kernel, width),
            [(half, BF16), (half, F32), (half, BF16), (half, F32)],
            gated,
            own_squares,
            other_squares,
            *[w_out] * row_size,
            prefetch=blocks.astype(jnp.int32),
            in_specs=[None] * 3
            + [
                pl.BlockSpec((inner, width), lambda i, b, at=at: (0, b[at]))
                for at in range(row_size)
            ],
            cost=(2 * rows * inner * row_size * width, 4 * 1024 * 1024),
        )
        upper_got = from_partner(upper_out, "row", 0)
        lower_got = from_partner(lower_out, "row", 1)
        upper_far = (upper_in[:, width:] + upper_got[:, width:].astype(F32)).astype(BF16)
        lower_near = (lower_in[:, width:] + lower_got[:, width:].astype(F32)).astype(BF16)
        upper_far = from_partner(upper_far, "row", 1)
        lower_near = from_partner(lower_near, "row", 0)
        upper = upper_in[:, :width] + upper_got[:, :width].astype(F32) + upper_far.astype(F32)
        lower = lower_in[:, :width] + lower_got[:, :width].astype(F32) + lower_near.astype(F32)
        part = jnp.concatenate([upper, lower], axis=0)
        if shift:
            part = from_ahead(part.astype(BF16), "col", col_size - shift).astype(F32)
        mixed = mixed + part
    hidden_out = (tokens.astype(F32) + mixed).astype(BF16)

    scale = lax.rsqrt((own_squares[0] + other_squares[0]) / (2 * inner) + EPSILON)
    end_scale = jnp.sum(chooser.astype(F32) * scale[None, :], axis=1)
    normed_ends = jnp.dot(chooser, gated, preferred_element_type=F32) * end_scale[:, None]
    end_sum = jnp.dot(normed_ends.astype(BF16), w_out, preferred_element_type=F32)
    for axis, bit in (("row", 0), ("row", 1), ("col", 0), ("col", 1)):
        end_sum = end_sum + from_partner(end_sum.astype(BF16), axis, bit).astype(F32)
    ends_wide = jnp.zeros((requests, row_size, col_size, width), F32)
    for shift in range(col_size):
        for i in range(row_size):
            ends_wide = lax.dynamic_update_slice(
                ends_wide,
                jnp.reshape(
                    token_ends[shift][:, i * width : (i + 1) * width], (requests, 1, 1, width)
                ),
                (0, across[i], (col_at + shift) % col_size, 0),
            )
    ending = jnp.reshape(ends_wide, (requests, model_width)) + end_sum
    last_rows = lax.psum(ending, "seq").astype(BF16).astype(F32)
    final_scale = lax.rsqrt(jnp.sum(last_rows * last_rows, axis=1) / model_width + EPSILON)
    head_in = (last_rows * final_scale[:, None] * final_gain).astype(BF16)
    logits = jnp.dot(head_in, w_head, preferred_element_type=F32)

    end_run = jnp.dot(chooser.astype(F32), run, precision=HIGHEST)[:, :heads]
    end_gain = jnp.where(ends_here[:, None], jnp.exp(end_run), 0.0)
    end_marks = jnp.concatenate(
        [
            end_gain,
            ends_here.astype(F32)[:, None],
            (slot_begin < 0).astype(F32)[:, None],
            jnp.zeros((requests, LANES - heads - 2), F32),
        ],
        axis=1,
    )[:, None, :]

    def finals_of(slots, extra):
        count = slots.shape[0]
        by_slot = pl.BlockSpec((1, inner, state), lambda i, s: (s[i], 0, 0))
        by_step = pl.BlockSpec((1, inner, state), lambda i, s: (i, 0, 0))
        return call(
            functools.partial(finals_kernel, heads, bool(extra)),
            [((count, inner, state), F32)],
            spread,
            keys,
            marks,
            end_marks,
            entry,
            init_flat,
            *extra,
            prefetch=slots,
            grid=(count,),
            in_specs=[None] * 3
            + [pl.BlockSpec((1, 1, LANES), lambda i, s: (s[i], 0, 0)), None, by_slot]
            + [by_step] * len(extra),
            out_specs=[by_step],
            cost=(2 * count * rows * inner * state, 4 * count * inner * state * 4),
        )[0]

    if seq_size == 2:
        kept = requests // 2
        lent = finals_of((1 - seq_at) * kept + slot_ids[:kept], [])
        finals = finals_of(seq_at * kept + slot_ids[:kept], [from_partner(lent, "seq", 0)])
    else:
        finals = lax.psum_scatter(
            finals_of(slot_ids, []), "seq", scatter_dimension=0, tiled=True
        )
    final_states = jnp.reshape(finals, (finals.shape[0], heads, head_size, state))
    return (hidden_out, final_states, logits)


def solution(mesh):
    in_specs = (
        P("seq", ("row", "col")),
        P(),
        P(),
        P(),
        P(None, None, ("row", "col")),
        P(None, None, "row", None),
        P(None, ("row", "col")),
        P(None, ("row", "col")),
        P(None, None, "row", None),
        P(("row", "col")),
        P(None, "row", None),
        P(None, None, ("row", "col")),
        P(None, None, None, "row", None),
        P(None, ("row", "col"), None, None),
        P(("row", "col")),
        P(("row", "col")),
        P(("row", "col")),
        P(("row", "col")),
        P(("row", "col"), None),
        P(),
        P(None, ("seq", "row", "col")),
    )
    out_specs = (
        P("seq", ("row", "col")),
        P("seq", ("row", "col"), None, None),
        P(None, ("seq", "row", "col")),
    )
    return jax.shard_map(
        per_device, mesh=mesh, in_specs=in_specs, out_specs=out_specs, check_vma=False
    )
```

```python
import functools

import jax
import jax.numpy as jnp
from jax import lax
from jax.experimental import pallas as pl
from jax.experimental.pallas import tpu as pltpu
from jax.sharding import PartitionSpec as P

EPSILON = 1e-05
HIGHEST = lax.Precision.HIGHEST
F32 = jnp.float32
BF16 = jnp.bfloat16
LANES = 128
RIM = 16
MIB = 1024 * 1024
ROWS_BY_ROWS = (((1,), (1,)), ((), ()))


def from_behind(block, axis, distance):
    devices = range(lax.axis_size(axis))
    route = [(i - distance, i) for i in devices if i - distance in devices]
    return lax.ppermute(block, axis, route)


def from_partner(x, axis, bit):
    return lax.ppermute(x, axis, [(i, i ^ 1 << bit) for i in range(lax.axis_size(axis))])


def from_ahead(x, axis, distance):
    size = lax.axis_size(axis)
    return lax.ppermute(x, axis, [((i + distance) % size, i) for i in range(size)])


def after(x, *others):
    return lax.optimization_barrier((x,) + others)[0]


def call(kernel, outs, *args, prefetch=None, grid=(1,), in_specs=None, out_specs=None, scratch=(), vmem=12, work=20):
    params = pltpu.CompilerParams(vmem_limit_bytes=vmem * MIB)
    shapes = [jax.ShapeDtypeStruct(shape, kind) for shape, kind in outs]

    def whole(shape):
        zeros = (0,) * len(shape)
        return pl.BlockSpec(shape, lambda *_: zeros)

    specs = [
        whole(a.shape) if spec is None else spec
        for a, spec in zip(args, in_specs or [None] * len(args))
    ]
    gives = [
        whole(shape) if spec is None else spec
        for (shape, _), spec in zip(outs, out_specs or [None] * len(outs))
    ]
    prefetch = jnp.zeros((1,), jnp.int32) if prefetch is None else prefetch
    spec = pltpu.PrefetchScalarGridSpec(
        num_scalar_prefetch=1, grid=grid, in_specs=specs, out_specs=gives,
        scratch_shapes=[pltpu.VMEM(shape, kind) for shape, kind in scratch],
    )
    return pl.pallas_call(
        kernel,
        out_shape=shapes,
        grid_spec=spec,
        compiler_params=params,
        cost_estimate=pl.CostEstimate(flops=work * 1_000_000_000, bytes_accessed=100_000_000 if work else 1000, transcendentals=0),
    )(prefetch, *args)


def plane_gather(block):
    half = block.shape[0] // 2
    upper, lower = block[:half], block[half:]
    upper_far = from_partner(upper, "row", 1)
    lower_near = from_partner(lower, "row", 0)
    upper_rest = from_partner(jnp.concatenate([upper, upper_far], axis=1), "row", 0)
    lower_rest = from_partner(jnp.concatenate([lower, lower_near], axis=1), "row", 1)
    return upper, upper_far, upper_rest, lower, lower_near, lower_rest


def setup_kernel(taps, counts, marks_ref, segment_ref, chooser_ref, slots_ref):
    requests = chooser_ref.shape[0]
    rows = marks_ref.shape[0]
    first_row = counts[2 * requests]
    begins, owners = [], []
    total = jnp.int32(0)
    for k in range(requests):
        begins.append(total - first_row)
        owners.append(counts[requests + k])
        total = total + counts[k]
    stops = begins[1:] + [total - first_row]

    def latest(position, values):
        found = jnp.full(position.shape, values[0], jnp.int32)
        for begin, value in zip(begins[1:], values[1:]):
            found = jnp.where(position >= begin, value, found)
        return found

    position = lax.broadcasted_iota(jnp.int32, (rows, LANES), 0)
    lane = lax.broadcasted_iota(jnp.int32, (rows, LANES), 1)
    owner = latest(position, owners)
    begin = latest(position, begins)
    offset = position - begin
    marks = owner
    for back in range(1, taps):
        edge = rows + RIM + owner * (taps - 1) + (taps - 1 - back) + offset
        inside = jnp.where(position >= back, position - back, rows + RIM + position - back)
        marks = jnp.where(lane == back - 1, jnp.where(offset >= back, inside, edge), marks)
    marks = jnp.where((lane == 3) & (begin < 0), requests, marks)
    marks = jnp.where(lane == 4, begin, marks)
    marks = jnp.where(lane == 5, jnp.where(begin < 0, 1, 0), marks)
    marks_ref[...] = marks
    across = lax.broadcasted_iota(jnp.int32, (8, rows), 1)
    segment_ref[...] = latest(across, begins)
    slot = lax.broadcasted_iota(jnp.int32, (requests, rows), 0)
    column = lax.broadcasted_iota(jnp.int32, (requests, rows), 1)
    slot_lane = lax.broadcasted_iota(jnp.int32, (requests, LANES), 0)
    chooser = jnp.zeros((requests, rows), F32)
    slot_begin = jnp.zeros((requests, LANES), F32)
    slot_end = jnp.zeros((requests, LANES), F32)
    for k in range(requests):
        last = stops[k] - 1
        chooser = jnp.where((slot == owners[k]) & (column == last), 1.0, chooser)
        here = jnp.where((last >= 0) & (last < rows), 1.0, 0.0)
        slot_end = jnp.where(slot_lane == owners[k], here, slot_end)
        before = jnp.where(begins[k] < 0, 1.0, 0.0)
        slot_begin = jnp.where(slot_lane == owners[k], before, slot_begin)
    chooser_ref[...] = chooser.astype(BF16)
    slots_ref[:, :LANES] = slot_end
    slots_ref[:, LANES:] = slot_begin


def weights_kernel(parts, place, *refs):
    out_ref, gain_out = refs[4 * parts :]
    rows = refs[0].shape[0]
    for part in range(parts):
        main_ref, group_ref, step_ref, gain_ref = refs[part : 4 * parts : parts]
        weights_block(
            place[2],
            main_ref,
            group_ref,
            step_ref,
            out_ref.at[pl.ds(part * rows, rows)],
        )
        gain_out[:, part * rows : (part + 1) * rows] = gain_ref[...]


def weights_block(group, main_ref, group_ref, step_ref, out_ref):
    rows, _, inner = main_ref.shape
    state = group_ref.shape[3]
    heads = step_ref.shape[0]
    half = rows // 2
    row = lax.broadcasted_iota(jnp.int32, (rows, rows), 0)
    column = lax.broadcasted_iota(jnp.int32, (rows, rows), 1)
    source = jnp.where(row < half, 2 * row, 2 * (row - half) + 1)
    pick = jnp.where(source == column, 1.0, 0.0).astype(BF16)
    flat = main_ref[...].reshape(2 * rows, inner)
    for at in range(2):
        got = jnp.dot(pick, flat[at * rows : (at + 1) * rows], preferred_element_type=F32)
        got = got.astype(BF16)
        out_ref[at * half : (at + 1) * half, :inner] = got[:half]
        out_ref[at * half : (at + 1) * half, inner : 2 * inner] = got[half:]
    take = rows // 4
    row, column = row[:half], column[:half]
    source = jnp.where(row < take, 4 * row, 4 * (row - take) + 2) + group
    pick = jnp.where(source == column, 1.0, 0.0).astype(BF16)
    flat = group_ref[...].reshape(4 * rows, state)
    for at in range(4):
        got = jnp.dot(pick, flat[at * rows : (at + 1) * rows], preferred_element_type=F32)
        got = got.astype(BF16)
        out_ref[at * take : (at + 1) * take, 2 * inner : 2 * inner + state] = got[:take]
        out_ref[at * take : (at + 1) * take, 2 * inner + state : 2 * inner + 2 * state] = got[take:]
    steps = jnp.concatenate(
        [step_ref[...].astype(F32), jnp.zeros((LANES - heads, rows), F32)], axis=0
    )
    out_ref[:, 2 * inner + 2 * state :] = steps.T.astype(BF16)


def table_kernel(unused, init_ref, out_ref):
    del unused
    out_ref[...] = init_ref[0].astype(BF16)


def project_kernel(first, inner, model_width, unused, *refs):
    del unused
    pieces, refs = refs[:6], refs[6:]
    chooser_ref, gain_ref, weights_ref, refs = refs[0], refs[1], refs[2], refs[3:]
    if not first:
        total_in, squares_in, refs = refs[0], refs[1], refs[2:]
    if first:
        ends_ref, total_ref, squares_ref = refs
    else:
        ends_ref, gate_ref, channels_ref, steps_ref, total_ref, squares_ref = refs
    width = pieces[0].shape[1]

    def add(raw, fresh):
        ends_ref[...] = jnp.dot(chooser_ref[...], raw, preferred_element_type=F32)
        wide = raw.astype(F32)
        scaled = (wide * gain_ref[...]).astype(BF16)
        product = jnp.dot(scaled, weights_ref[...], preferred_element_type=F32)
        square = wide * wide
        parts = [square[:, at : at + LANES] for at in range(0, 2 * width, LANES)]
        if fresh:
            total_ref[...] = product if first else product + total_in[...]
            squares_ref[...] = functools.reduce(jnp.add, parts if first else parts + [squares_in[...]])
        else:
            total_ref[...] += product
            squares_ref[...] += functools.reduce(jnp.add, parts)

    upper, upper_far, upper_rest, lower, lower_near, lower_rest = pieces

    @pl.when(pl.program_id(0) == 0)
    def _():
        top = jnp.concatenate([upper[...], upper_rest[:, :width]], axis=1)
        bottom = jnp.concatenate([lower[...], lower_near[...]], axis=1)
        add(jnp.concatenate([top, bottom], axis=0), True)

    @pl.when(pl.program_id(0) == 1)
    def _():
        top = jnp.concatenate([upper_far[...], upper_rest[:, width:]], axis=1)
        add(jnp.concatenate([top, lower_rest[...]], axis=0), False)
        if first:
            return
        inv_rms = jnp.sum(squares_ref[...], axis=1, keepdims=True) / model_width
        inv_rms = lax.rsqrt(inv_rms + EPSILON)
        gate_ref[...] = (total_ref[:, :inner] * inv_rms).astype(BF16)
        channels_ref[...] = (total_ref[:, inner:-LANES] * inv_rms).astype(BF16)
        steps_ref[...] = total_ref[:, -LANES:] * inv_rms


def both_heads(table, pair, head_size):
    rows = table.shape[0]
    lane = lax.broadcasted_iota(jnp.int32, (rows, 2 * head_size), 1)
    return jnp.where(
        lane < head_size, table[:, 2 * pair : 2 * pair + 1], table[:, 2 * pair + 1 : 2 * pair + 2]
    )


def over_states(row, heads, head_size):
    return jnp.concatenate(
        [jnp.broadcast_to(row[:, h : h + 1], (head_size, LANES)) for h in range(heads)], axis=0
    )


def conv_kernel(
    heads,
    unused,
    channels_ref,
    rim_ref,
    edges_ref,
    taps_ref,
    bias_ref,
    steps_ref,
    step_bias_ref,
    decay_ref,
    marks_ref,
    segment_ref,
    init_ref,
    x_ref,
    keys_ref,
    queries_ref,
    run_ref,
    less_ref,
    spread_ref,
    leaving_ref,
    gain_ref,
):
    del unused
    rows, inner = x_ref.shape
    state = keys_ref.shape[1]
    head_size = inner // heads
    taps = taps_ref.shape[0]
    channels = channels_ref[...]
    sources = jnp.concatenate([channels, rim_ref[...], edges_ref[...]], axis=0)
    summed = bias_ref[...] + taps_ref[taps - 1 : taps] * channels.astype(F32)
    column = lax.broadcasted_iota(jnp.int32, (rows, sources.shape[0]), 1)
    for back in range(1, taps):
        pick = jnp.where(marks_ref[:, back - 1 : back] == column, 1.0, 0.0).astype(BF16)
        value = jnp.dot(pick, sources, preferred_element_type=F32)
        summed = summed + taps_ref[taps - 1 - back : taps - back] * value
    mixed = (summed / (1.0 + jnp.exp(-summed))).astype(BF16)
    x = mixed[:, :inner]
    keys = mixed[:, inner : inner + state]
    x_ref[...] = x
    keys_ref[...] = keys
    queries_ref[...] = mixed[:, inner + state :]
    raw = steps_ref[...] + step_bias_ref[...]
    step = jnp.maximum(raw, 0.0) + jnp.log1p(jnp.exp(-jnp.abs(raw)))
    log_decay = -jnp.exp(decay_ref[...]) * step
    segment = marks_ref[:, 4:5]
    same = segment == segment_ref[0:1, :]
    row = lax.broadcasted_iota(jnp.int32, (rows, rows), 0)
    other = lax.broadcasted_iota(jnp.int32, (rows, rows), 1)
    until = jnp.where(same & (other <= row), 1.0, 0.0)
    after = jnp.where(same & (other > row), 1.0, 0.0)
    run = jnp.dot(until, log_decay, precision=HIGHEST, preferred_element_type=F32)
    tail = jnp.dot(after, log_decay, precision=HIGHEST, preferred_element_type=F32)
    run_ref[...] = run
    less_ref[...] = (run - jnp.log(step)).T[:8]
    share = (jnp.exp(tail) * step).astype(BF16).astype(F32)
    spread = jnp.concatenate(
        [
            both_heads(share, p, head_size)
            * x[:, p * 2 * head_size : (p + 1) * 2 * head_size].astype(F32)
            for p in range(heads // 2)
        ],
        axis=1,
    )
    spread = spread.T.astype(BF16)
    spread_ref[...] = spread
    last = jnp.where(segment == segment[rows - 1 : rows], 1.0, 0.0)
    leaving = jnp.dot(spread, (keys.astype(F32) * last).astype(BF16), preferred_element_type=F32)
    gain = jnp.exp(run[rows - 1 : rows])
    carried = jnp.broadcast_to(marks_ref[rows - 1 : rows, 5:6], (heads * head_size, state)) > 0
    gain_wide = over_states(gain, heads, head_size)
    leaving_ref[...] = jnp.where(carried, leaving, leaving + gain_wide * init_ref[...])
    gain_ref[...] = jnp.where(carried, gain_wide, 0.0)


def scan_kernel(
    heads,
    block,
    unused,
    x_ref,
    keys_ref,
    queries_ref,
    run_ref,
    less_ref,
    marks_ref,
    segment_ref,
    table_ref,
    skip_ref,
    y_ref,
    masked_ref,
    begun_ref,
):
    del unused
    rows, inner = x_ref.shape
    head_size = inner // heads
    slots = table_ref.shape[1] // queries_ref.shape[1]
    queries = queries_ref[...].astype(F32)
    slot = marks_ref[:, 3:4]
    placed = jnp.concatenate(
        [(queries * jnp.where(slot == o, 1.0, 0.0)).astype(BF16) for o in range(slots)], axis=1
    )
    begun_ref[...] = lax.dot_general(
        placed, table_ref[...], ROWS_BY_ROWS, preferred_element_type=F32
    )
    blocks = [(t, s) for t in range(rows // block) for s in range(t + 1)]
    for at, (t, s) in enumerate(blocks):
        here, there = pl.ds(t * block, block), pl.ds(s * block, block)
        scores = lax.dot_general(
            queries_ref[here], keys_ref[there], ROWS_BY_ROWS, preferred_element_type=F32
        )
        same = marks_ref[here, 4:5] == segment_ref[0:1, there]
        if t == s:
            row = lax.broadcasted_iota(jnp.int32, (block, block), 0)
            other = lax.broadcasted_iota(jnp.int32, (block, block), 1)
            same = same & (other <= row)
        masked_ref[at] = jnp.where(same, scores, 0.0)
    grown = jnp.exp(run_ref[...])
    lane = lax.broadcasted_iota(jnp.int32, (block, 2 * head_size), 1)
    for p in range(heads // 2):
        wide = slice(p * 2 * head_size, (p + 1) * 2 * head_size)
        x = x_ref[:, wide].astype(F32)
        y = both_heads(grown, p, head_size) * begun_ref[:, wide] + both_heads(skip_ref[...], p, head_size) * x
        sums = [y[t * block : (t + 1) * block] for t in range(rows // block)]
        for at, (t, s) in enumerate(blocks):
            here, there = slice(t * block, (t + 1) * block), slice(s * block, (s + 1) * block)
            for side in range(2):
                head = 2 * p + side
                mine = (lane < head_size) if side == 0 else (lane >= head_size)
                x_own = jnp.where(mine, x[there], 0.0).astype(BF16)
                gap = run_ref[here, head : head + 1] - less_ref[head : head + 1, there]
                weight = (masked_ref[at] * jnp.exp(jnp.minimum(gap, 80.0))).astype(BF16)
                sums[t] = sums[t] + jnp.dot(weight, x_own, preferred_element_type=F32)
        for t in range(rows // block):
            y_ref[t * block : (t + 1) * block, wide] = sums[t]


def gate_kernel(
    heads, unused, y_ref, queries_ref, run_ref, marks_ref, entry_ref, gate_ref, gain_ref, out_ref, sq_ref
):
    del unused
    rows, inner = y_ref.shape
    head_size = inner // heads
    carried = jnp.where(marks_ref[:, 5:6] > 0, 1.0, 0.0)
    queries = (queries_ref[...].astype(F32) * carried).astype(BF16)
    held = lax.dot_general(
        queries, entry_ref[...].astype(BF16), ROWS_BY_ROWS, preferred_element_type=F32
    )
    grown = jnp.exp(run_ref[...])
    grown = jnp.concatenate([both_heads(grown, p, head_size) for p in range(heads // 2)], axis=1)
    gate = gate_ref[...].astype(F32)
    gated = (y_ref[...] + grown * held) * (gate / (1.0 + jnp.exp(-gate)))
    out_ref[...] = (gated * gain_ref[...]).astype(BF16)
    square = jnp.sum(gated * gated, axis=1, keepdims=True)
    sq_ref[...] = jnp.broadcast_to(square, (rows, LANES)).T[:8]


def norm_scale(own_ref, other_ref, channels):
    scale = lax.rsqrt((own_ref[0:1] + other_ref[0:1]) / channels + EPSILON)
    return jnp.broadcast_to(scale, (LANES, scale.shape[1])).T


def out_kernel(width, count, blocks, gated_ref, own_ref, other_ref, chooser_ref, *refs):
    del blocks
    weights, outs = refs[: 4 * count], refs[4 * count :]
    upper_out, upper_in, lower_out, lower_in, ends_ref = outs
    rows, inner = gated_ref.shape
    half = rows // 2
    scale = norm_scale(own_ref, other_ref, 2 * inner)
    scale = jnp.concatenate([scale] * (width // LANES), axis=1)
    gated = gated_ref[...]
    end_rows = jnp.dot(chooser_ref[...], gated, preferred_element_type=F32).astype(BF16)
    end_scale = jnp.dot(
        chooser_ref[...].astype(F32), scale, precision=HIGHEST, preferred_element_type=F32
    )
    for at, w in enumerate(weights):
        index, place = divmod(at, count)
        part = jnp.dot(gated, w[...], preferred_element_type=F32) * scale
        top, bottom = part[:half], part[half:]
        low = (index // 2) * count + place
        if index % 2:
            upper_out[:, low * width : (low + 1) * width] = top.astype(BF16)
        else:
            upper_in[:, low * width : (low + 1) * width] = top
        low = (index % 2) * count + place
        if index // 2:
            lower_out[:, low * width : (low + 1) * width] = bottom.astype(BF16)
        else:
            lower_in[:, low * width : (low + 1) * width] = bottom
        ends_ref[:, at * width : (at + 1) * width] = (
            jnp.dot(end_rows, w[...], preferred_element_type=F32) * end_scale
        )


def near_kernel(unused, upper_ref, upper_got, lower_ref, lower_got, *outs):
    del unused
    for kept, got, keep_ref, send_ref in (
        (upper_ref, upper_got, outs[0], outs[1]),
        (lower_ref, lower_got, outs[2], outs[3]),
    ):
        wide = keep_ref.shape[1]
        keep_ref[...] = kept[:, :wide] + got[:, :wide].astype(F32)
        send_ref[...] = (kept[:, wide:] + got[:, wide:].astype(F32)).astype(BF16)


def plane_kernel(unused, upper_ref, upper_got, lower_ref, lower_got, *outs):
    del unused
    half, width = upper_ref.shape[0], outs[0].shape[1]
    for at, out_ref in enumerate(outs):
        wide = slice(at * width, (at + 1) * width)
        upper = upper_ref[:, wide] + upper_got[:, wide].astype(F32)
        lower = lower_ref[:, wide] + lower_got[:, wide].astype(F32)
        out_ref[:half] = upper.astype(out_ref.dtype)
        out_ref[half:] = lower.astype(out_ref.dtype)


def hidden_kernel(unused, tokens_ref, own_ref, *refs):
    del unused
    total = own_ref[...]
    for part in refs[:-1]:
        total = total + part[...].astype(F32)
    refs[-1][...] = (tokens_ref[...].astype(F32) + total).astype(BF16)


def ends_kernel(width, block_of, place, *refs):
    sources, outs = refs[:4], refs[4:]
    half = sources[0].shape[1] // width
    for at in range(2 * half):
        which, low = divmod(at, half)
        block = block_of(which, low, place)
        to = pl.ds(pl.multiple_of(block * width, width), width)
        outs[0][:, to] = sources[which][:, low * width : (low + 1) * width]
        outs[1][:, to] = sources[2 + which][:, low * width : (low + 1) * width]


def finals_kernel(
    heads, added, first, spread_ref, keys_ref, marks_ref, ends_ref, entry_ref, init_ref, _, *refs
):
    out_ref = refs[-1]
    count, inner, state = out_ref.shape
    head_size = inner // heads
    slot = (first[0] + pl.program_id(0)) * count
    keys = keys_ref[...].astype(F32)
    owner = marks_ref[:, 6:7]
    mine = [
        (keys * jnp.where(owner == slot + i, ends_ref[i, :, heads : heads + 1], 0.0)).astype(BF16)
        for i in range(count)
    ]
    states = jnp.dot(
        spread_ref[...], jnp.concatenate(mine, axis=1), preferred_element_type=F32
    )
    for i in range(count):
        gain = over_states(ends_ref[i], heads, head_size)
        carried = jnp.broadcast_to(ends_ref[i, :, heads + 1 : heads + 2], (inner, state)) > 0.5
        value = states[:, i * state : (i + 1) * state]
        value = value + gain * jnp.where(carried, entry_ref[...], init_ref[i])
        out_ref[i] = value + refs[0][i] if added else value


def per_device(
    tokens,
    lengths,
    deal,
    pre_gain,
    w_inner,
    w_group,
    w_step,
    conv_inner,
    conv_group,
    conv_bias_inner,
    conv_bias_group,
    edge_inner,
    edge_group,
    init_states,
    step_bias,
    decay_log,
    skip,
    inner_gain,
    w_out,
    final_gain,
    w_head,
):
    rows, width = tokens.shape
    model_width = pre_gain.shape[0]
    requests = lengths.shape[0]
    taps = conv_inner.shape[0]
    inner = w_inner.shape[2]
    heads = w_step.shape[1]
    head_size = inner // heads
    state = w_group.shape[3]
    row_at, col_at, seq_at = (lax.axis_index(name) for name in ("row", "col", "seq"))
    row_size, col_size, seq_size = (lax.axis_size(name) for name in ("row", "col", "seq"))
    group_local = col_at * w_group.shape[2] // col_size

    def own_group(table, axis):
        return lax.dynamic_index_in_dim(table, group_local, axis, keepdims=False)

    def in_lanes(values):
        return jnp.pad(values, (0, LANES - heads))[None, :]

    first_row = seq_at * rows
    counts = jnp.concatenate([lengths, deal, jnp.reshape(first_row, (1,)).astype(jnp.int32)])
    marks, segment_row, chooser, slots = call(
        functools.partial(setup_kernel, taps),
        [
            ((rows, LANES), jnp.int32),
            ((8, rows), jnp.int32),
            ((requests, rows), BF16),
            ((requests, 2 * LANES), F32),
        ],
        prefetch=counts,
        vmem=4,
        work=0,
    )
    place = jnp.stack([row_at, col_at, group_local]).astype(jnp.int32)

    init_flat = jnp.reshape(init_states, (requests, inner, state))
    skip_row = in_lanes(skip)
    gains = pre_gain[None, :]

    near, far = tuple(range(col_size // 2)), tuple(range(col_size // 2, col_size))

    def block_of(shifts, at, place):
        shifts = (near, far)[shifts] if isinstance(shifts, int) else shifts
        index, shift = at // len(shifts), at % len(shifts) + shifts[0]
        return (place[0] ^ index) * col_size + (place[1] + shift) % col_size

    n_all = 2 * inner + 2 * state + LANES
    steps_across = jnp.transpose(w_step)

    def weights_of(shifts, gain_row):
        count = row_size * len(shifts)
        parts = count // 2

        def specs(shape, where):
            return [
                pl.BlockSpec(shape, lambda i, p, at=at: where(block_of(shifts, i * parts + at, p)))
                for at in range(parts)
            ]

        return call(
            functools.partial(weights_kernel, parts),
            [((count * width, n_all), BF16), ((1, count * width), F32)],
            *[w_inner] * parts,
            *[w_group] * parts,
            *[steps_across] * parts,
            *[gain_row] * parts,
            prefetch=place,
            grid=(count // parts,),
            in_specs=specs((width,) + w_inner.shape[1:], lambda b: (b, 0, 0))
            + specs((width,) + w_group.shape[1:], lambda b: (b, 0, 0, 0))
            + specs((heads, width), lambda b: (0, b))
            + specs((1, width), lambda b: (0, b)),
            out_specs=[
                pl.BlockSpec((parts * width, n_all), lambda i, p: (i, 0)),
                pl.BlockSpec((1, parts * width), lambda i, p: (0, i)),
            ],
            vmem=58,
        )

    gain_row = pre_gain[None, :]
    token_blocks = [tokens, from_ahead(tokens, "col", 1)]
    later = after(tokens, token_blocks[1])
    token_blocks += [from_ahead(later, "col", shift) for shift in range(2, col_size)]
    near_weights = weights_of(near, after(gain_row, token_blocks[1]))
    token_ends = []
    carry = ()
    for shifts in (near, far):
        first = shifts is near
        pieces = plane_gather(jnp.concatenate([token_blocks[i] for i in shifts], axis=1))
        if first:
            far_weights = weights_of(far, after(gain_row, pieces[1]))
        else:
            ready = pieces[1]
        weights, gains = near_weights if first else far_weights
        count = row_size * len(shifts)
        depth = count * width // 2
        outs = [((requests, count * width), F32)]
        totals = [((rows, n_all), F32), ((rows, LANES), F32)]
        if first:
            outs += totals
        else:
            outs += [((rows, inner), BF16), ((rows, inner + 2 * state), BF16), ((rows, LANES), F32)]
        piece_ends, *carry = call(
            functools.partial(project_kernel, first, inner, model_width),
            outs,
            *pieces,
            chooser,
            gains,
            weights,
            *carry,
            grid=(2,),
            in_specs=[None] * 7
            + [
                pl.BlockSpec((1, depth), lambda i, _: (0, i)),
                pl.BlockSpec((depth, n_all), lambda i, _: (i, 0)),
            ]
            + [None] * len(carry),
            out_specs=[pl.BlockSpec((requests, depth), lambda i, _: (0, i))]
            + [None] * (len(outs) - 1),
            scratch=[] if first else totals,
            vmem=24,
        )
        token_ends.append(piece_ends)
    gate_in, channels, step_raw = carry

    init_last = lax.dynamic_index_in_dim(init_flat, after(marks, ready)[rows - 1, 6], 0, keepdims=False)
    (table,) = call(
        table_kernel,
        [((inner, requests * state), BF16)],
        after(init_flat, ready),
        grid=(requests,),
        in_specs=[pl.BlockSpec((1, inner, state), lambda i, _: (i, 0, 0))],
        out_specs=[pl.BlockSpec((inner, state), lambda i, _: (0, i))],
        vmem=4,
        work=0,
    )
    conv_taps = jnp.concatenate(
        [conv_inner, jnp.reshape(own_group(after(conv_group, ready), 2), (taps, 2 * state))], axis=1
    )
    conv_bias = jnp.concatenate(
        [conv_bias_inner, jnp.reshape(own_group(after(conv_bias_group, ready), 1), (2 * state,))]
    )[None, :]
    edges = jnp.concatenate(
        [after(edge_inner, ready), jnp.reshape(own_group(after(edge_group, ready), 3), (requests, taps - 1, 2 * state))],
        axis=2,
    )
    edges = jnp.reshape(edges, (requests * (taps - 1), inner + 2 * state))

    rim = from_behind(channels[rows - RIM :], "seq", 1)
    x, keys, queries, run, less, spread, leaving, gain_carried = call(
        functools.partial(conv_kernel, heads),
        [
            ((rows, inner), BF16),
            ((rows, state), BF16),
            ((rows, state), BF16),
            ((rows, LANES), F32),
            ((8, rows), F32),
            ((inner, rows), BF16),
            ((inner, state), F32),
            ((inner, state), F32),
        ],
        channels,
        rim,
        edges,
        conv_taps,
        conv_bias,
        step_raw,
        in_lanes(step_bias),
        in_lanes(decay_log),
        marks,
        segment_row,
        init_last,
    )
    entry = from_behind(leaving, "seq", 1)
    for _ in range(seq_size - 2):
        entry = from_behind(gain_carried * entry + leaving, "seq", 1)

    block = 256
    pairs = (rows // block) * (rows // block + 1) // 2
    y = pl.pallas_call(
        functools.partial(scan_kernel, heads, block),
        out_shape=jax.ShapeDtypeStruct((rows, inner), F32),
        grid_spec=pltpu.PrefetchScalarGridSpec(
            num_scalar_prefetch=1,
            grid=(1,),
            in_specs=[
                pl.BlockSpec(a.shape, lambda *_: (0, 0))
                for a in (x, keys, queries, run, less, marks, segment_row, table, skip_row)
            ],
            out_specs=pl.BlockSpec((rows, inner), lambda *_: (0, 0)),
            scratch_shapes=[
                pltpu.VMEM((pairs, block, block), F32),
                pltpu.VMEM((rows, inner), F32),
            ],
        ),
        compiler_params=pltpu.CompilerParams(vmem_limit_bytes=16 * MIB),
    )(
        jnp.zeros((1,), jnp.int32),
        x,
        keys,
        queries,
        run,
        less,
        marks,
        segment_row,
        table,
        skip_row,
    )
    gated, own_squares = call(
        functools.partial(gate_kernel, heads),
        [((rows, inner), BF16), ((8, rows), F32)],
        y,
        queries,
        run,
        marks,
        entry,
        gate_in,
        inner_gain[None, :],
    )
    other_squares = from_partner(own_squares, "col", 0)

    half_out = []
    for shifts in (far, near):
        count = len(shifts)
        side = (rows // 2, 2 * count * width)
        half_out.append(
            call(
                functools.partial(out_kernel, width, count),
                [
                    (side, BF16),
                    (side, F32),
                    (side, BF16),
                    (side, F32),
                    ((requests, row_size * count * width), F32),
                ],
                gated,
                own_squares,
                other_squares,
                chooser,
                *[w_out] * (row_size * count),
                prefetch=place,
                in_specs=[None] * 4
                + [
                    pl.BlockSpec(
                        (inner, width),
                        lambda i, p, at=at, shifts=shifts: (0, block_of(shifts, at, p)),
                    )
                    for at in range(row_size * count)
                ],
                vmem=56 if shifts is far else 16,
                work=0,
            )
        )
    got = []
    for upper_out, _, lower_out, _, _ in half_out:
        got.append((from_partner(upper_out, "row", 0), from_partner(lower_out, "row", 1)))
    end_sum, end_tokens = call(
        functools.partial(ends_kernel, width, block_of),
        [((requests, model_width), F32)] * 2,
        after(half_out[1][4], got[0][0]),
        half_out[0][4],
        *token_ends,
        prefetch=place,
        vmem=4,
        work=0,
    )
    for axis, bit in (("col", 0), ("col", 1), ("row", 0), ("row", 1)):
        end_sum = end_sum + from_partner(end_sum.astype(BF16), axis, bit).astype(F32)

    def finals_after(far_ready):
        end_run = jnp.dot(chooser.astype(F32), run, precision=HIGHEST)[:, :heads]
        ends_here = slots[:, :1]
        end_marks = jnp.concatenate(
            [
                jnp.exp(end_run) * ends_here,
                ends_here,
                slots[:, LANES : LANES + 1],
                jnp.zeros((requests, LANES - heads - 2), F32),
            ],
            axis=1,
        )[:, None, :]

        kept = requests // seq_size

        def finals_of(first, steps, ready, extra):
            count = steps * kept
            by_slot = pl.BlockSpec((kept, inner, state), lambda i, s: (s[0] + i, 0, 0))
            by_step = pl.BlockSpec((kept, inner, state), lambda i, s: (i, 0, 0))
            return call(
                functools.partial(finals_kernel, heads, bool(extra)),
                [((count, inner, state), F32)],
                spread,
                keys,
                marks,
                end_marks,
                entry,
                init_flat,
                after(half_out[1][4], *ready),
                *extra,
                prefetch=jnp.reshape(first, (1,)).astype(jnp.int32),
                grid=(steps,),
                in_specs=[None] * 3
                + [pl.BlockSpec((kept, 1, LANES), lambda i, s: (s[0] + i, 0, 0)), None, by_slot]
                + [pl.BlockSpec(memory_space=pl.ANY)]
                + [by_step] * len(extra),
                out_specs=[by_step],
                vmem=20,
                work=0,
            )[0]

        if seq_size == 2:
            lent = finals_of(1 - seq_at, 1, far_ready, [])
            finals = finals_of(seq_at, 1, (), [from_partner(lent, "seq", 0)])
        else:
            finals = lax.psum_scatter(
                finals_of(jnp.int32(0), seq_size, (), []), "seq", scatter_dimension=0, tiled=True
            )
        return finals

    pieces = {}
    for shifts, outs, (upper_got, lower_got) in zip((far, near), half_out, got):
        _, upper_in, _, lower_in, _ = outs
        wide = len(shifts) * width
        upper, upper_far, lower, lower_near = call(
            near_kernel,
            [((rows // 2, wide), F32), ((rows // 2, wide), BF16)] * 2,
            upper_in,
            upper_got,
            lower_in,
            lower_got,
            vmem=8,
            work=10,
        )
        upper_far = from_partner(upper_far, "row", 1)
        lower_near = from_partner(lower_near, "row", 0)
        sums = call(
            plane_kernel,
            [((rows, width), BF16 if shift else F32) for shift in shifts],
            upper,
            upper_far,
            lower,
            lower_near,
            vmem=8,
            work=10,
        )
        if shifts is far:
            far_ready = sums
        for shift, part in zip(shifts, sums):
            pieces[shift] = from_ahead(part, "col", col_size - shift) if shift else part
    finals = finals_after(far_ready)
    if seq_size == 2:
        ending = after(end_tokens + end_sum, finals)
        ending = ending + from_partner(ending, "seq", 0)
    else:
        ending = lax.psum(end_tokens + end_sum, "seq")
    (hidden_out,) = call(
        hidden_kernel,
        [((rows, width), BF16)],
        tokens,
        *[pieces[shift] for shift in range(col_size)],
        vmem=4,
        work=30,
    )

    last_rows = ending.astype(BF16).astype(F32)
    final_scale = lax.rsqrt(jnp.sum(last_rows * last_rows, axis=1) / model_width + EPSILON)
    head_in = (last_rows * final_scale[:, None] * final_gain).astype(BF16)
    logits = jnp.dot(head_in, w_head, preferred_element_type=F32)

    final_states = jnp.reshape(finals, (finals.shape[0], heads, head_size, state))
    return (hidden_out, final_states, logits)


def solution(mesh):
    in_specs = (
        P("seq", ("row", "col")),
        P(),
        P(),
        P(),
        P(None, None, ("row", "col")),
        P(None, None, "row", None),
        P(None, ("row", "col")),
        P(None, ("row", "col")),
        P(None, None, "row", None),
        P(("row", "col")),
        P(None, "row", None),
        P(None, None, ("row", "col")),
        P(None, None, None, "row", None),
        P(None, ("row", "col"), None, None),
        P(("row", "col")),
        P(("row", "col")),
        P(("row", "col")),
        P(("row", "col")),
        P(("row", "col"), None),
        P(),
        P(None, ("seq", "row", "col")),
    )
    out_specs = (
        P("seq", ("row", "col")),
        P("seq", ("row", "col"), None, None),
        P(None, ("seq", "row", "col")),
    )
    return jax.shard_map(
        per_device, mesh=mesh, in_specs=in_specs, out_specs=out_specs, check_vma=False
    )
```

```python
import functools

import jax
import jax.numpy as jnp
from jax import lax
from jax.experimental import pallas as pl
from jax.experimental.pallas import tpu as pltpu
from jax.sharding import PartitionSpec as P

EPSILON = 1e-05
HIGHEST = lax.Precision.HIGHEST
F32 = jnp.float32
BF16 = jnp.bfloat16
LANES = 128
RIM = 16
MIB = 1024 * 1024
ROWS_BY_ROWS = (((1,), (1,)), ((), ()))


def from_behind(block, axis, distance):
    devices = range(lax.axis_size(axis))
    route = [(i - distance, i) for i in devices if i - distance in devices]
    return lax.ppermute(block, axis, route)


def from_partner(x, axis, bit):
    return lax.ppermute(x, axis, [(i, i ^ 1 << bit) for i in range(lax.axis_size(axis))])


def from_ahead(x, axis, distance):
    size = lax.axis_size(axis)
    return lax.ppermute(x, axis, [((i + distance) % size, i) for i in range(size)])


def after(x, *others):
    return lax.optimization_barrier((x,) + others)[0]


def call(kernel, outs, *args, prefetch=None, grid=(1,), in_specs=None, out_specs=None, scratch=(), vmem=12, work=20):
    params = pltpu.CompilerParams(vmem_limit_bytes=vmem * MIB)
    shapes = [jax.ShapeDtypeStruct(shape, kind) for shape, kind in outs]

    def whole(shape):
        zeros = (0,) * len(shape)
        return pl.BlockSpec(shape, lambda *_: zeros)

    specs = [
        whole(a.shape) if spec is None else spec
        for a, spec in zip(args, in_specs or [None] * len(args))
    ]
    gives = [
        whole(shape) if spec is None else spec
        for (shape, _), spec in zip(outs, out_specs or [None] * len(outs))
    ]
    prefetch = jnp.zeros((1,), jnp.int32) if prefetch is None else prefetch
    spec = pltpu.PrefetchScalarGridSpec(
        num_scalar_prefetch=1, grid=grid, in_specs=specs, out_specs=gives,
        scratch_shapes=[pltpu.VMEM(shape, kind) for shape, kind in scratch],
    )
    return pl.pallas_call(
        kernel,
        out_shape=shapes,
        grid_spec=spec,
        compiler_params=params,
        cost_estimate=pl.CostEstimate(flops=work * 1_000_000_000, bytes_accessed=100_000_000 if work else 1000, transcendentals=0),
    )(prefetch, *args)


def plane_gather(block):
    half = block.shape[0] // 2
    upper, lower = block[:half], block[half:]
    upper_far = from_partner(upper, "row", 1)
    lower_near = from_partner(lower, "row", 0)
    upper_rest = from_partner(jnp.concatenate([upper, upper_far], axis=1), "row", 0)
    lower_rest = from_partner(jnp.concatenate([lower, lower_near], axis=1), "row", 1)
    return upper, upper_far, upper_rest, lower, lower_near, lower_rest


def block_of(shifts, at, place, col_size):
    gap = shifts[-1] - shifts[0] if len(shifts) > 1 else 0
    shift = shifts[0] + (at % len(shifts)) * gap
    return (place[0] ^ (at // len(shifts))) * col_size + (place[1] + shift) % col_size


def setup_kernel(taps, counts, marks_ref, segment_ref, chooser_ref, slots_ref):
    requests = chooser_ref.shape[0]
    rows = marks_ref.shape[0]
    first_row = counts[2 * requests]
    begins, owners = [], []
    total = jnp.int32(0)
    for k in range(requests):
        begins.append(total - first_row)
        owners.append(counts[requests + k])
        total = total + counts[k]
    stops = begins[1:] + [total - first_row]

    def latest(position, values):
        found = jnp.full(position.shape, values[0], jnp.int32)
        for begin, value in zip(begins[1:], values[1:]):
            found = jnp.where(position >= begin, value, found)
        return found

    position = lax.broadcasted_iota(jnp.int32, (rows, LANES), 0)
    lane = lax.broadcasted_iota(jnp.int32, (rows, LANES), 1)
    owner = latest(position, owners)
    begin = latest(position, begins)
    offset = position - begin
    marks = owner
    for back in range(1, taps):
        edge = rows + RIM + owner * (taps - 1) + (taps - 1 - back) + offset
        inside = jnp.where(position >= back, position - back, rows + RIM + position - back)
        marks = jnp.where(lane == back - 1, jnp.where(offset >= back, inside, edge), marks)
    marks = jnp.where((lane == 3) & (begin < 0), requests, marks)
    marks = jnp.where(lane == 4, begin, marks)
    marks = jnp.where(lane == 5, jnp.where(begin < 0, 1, 0), marks)
    marks_ref[...] = marks
    across = lax.broadcasted_iota(jnp.int32, (8, rows), 1)
    segment_ref[...] = latest(across, begins)
    slot = lax.broadcasted_iota(jnp.int32, (requests, rows), 0)
    column = lax.broadcasted_iota(jnp.int32, (requests, rows), 1)
    slot_lane = lax.broadcasted_iota(jnp.int32, (requests, LANES), 0)
    chooser = jnp.zeros((requests, rows), F32)
    slot_begin = jnp.zeros((requests, LANES), F32)
    slot_end = jnp.zeros((requests, LANES), F32)
    for k in range(requests):
        last = stops[k] - 1
        chooser = jnp.where((slot == owners[k]) & (column == last), 1.0, chooser)
        here = jnp.where((last >= 0) & (last < rows), 1.0, 0.0)
        slot_end = jnp.where(slot_lane == owners[k], here, slot_end)
        before = jnp.where(begins[k] < 0, 1.0, 0.0)
        slot_begin = jnp.where(slot_lane == owners[k], before, slot_begin)
    chooser_ref[...] = chooser.astype(BF16)
    slots_ref[:, :LANES] = slot_end
    slots_ref[:, LANES:] = slot_begin


def weights_kernel(parts, place, *refs):
    out_ref, gain_out = refs[4 * parts :]
    rows = refs[0].shape[0]
    for part in range(parts):
        main_ref, group_ref, step_ref, gain_ref = refs[part : 4 * parts : parts]
        weights_block(
            place[2],
            main_ref,
            group_ref,
            step_ref,
            out_ref.at[pl.ds(part * rows, rows)],
        )
        gain_out[:, part * rows : (part + 1) * rows] = gain_ref[...]


def weights_block(group, main_ref, group_ref, step_ref, out_ref):
    rows, _, inner = main_ref.shape
    state = group_ref.shape[3]
    heads = step_ref.shape[0]
    half = rows // 2
    row = lax.broadcasted_iota(jnp.int32, (rows, rows), 0)
    column = lax.broadcasted_iota(jnp.int32, (rows, rows), 1)
    source = jnp.where(row < half, 2 * row, 2 * (row - half) + 1)
    pick = jnp.where(source == column, 1.0, 0.0).astype(BF16)
    flat = main_ref[...].reshape(2 * rows, inner)
    for at in range(2):
        got = jnp.dot(pick, flat[at * rows : (at + 1) * rows], preferred_element_type=F32)
        got = got.astype(BF16)
        out_ref[at * half : (at + 1) * half, :inner] = got[:half]
        out_ref[at * half : (at + 1) * half, inner : 2 * inner] = got[half:]
    take = rows // 4
    row, column = row[:half], column[:half]
    source = jnp.where(row < take, 4 * row, 4 * (row - take) + 2) + group
    pick = jnp.where(source == column, 1.0, 0.0).astype(BF16)
    flat = group_ref[...].reshape(4 * rows, state)
    for at in range(4):
        got = jnp.dot(pick, flat[at * rows : (at + 1) * rows], preferred_element_type=F32)
        got = got.astype(BF16)
        out_ref[at * take : (at + 1) * take, 2 * inner : 2 * inner + state] = got[:take]
        out_ref[at * take : (at + 1) * take, 2 * inner + state : 2 * inner + 2 * state] = got[take:]
    steps = jnp.concatenate(
        [step_ref[...].astype(F32), jnp.zeros((LANES - heads, rows), F32)], axis=0
    )
    out_ref[:, 2 * inner + 2 * state :] = steps.T.astype(BF16)


def table_kernel(unused, init_ref, out_ref):
    del unused
    out_ref[...] = init_ref[0].astype(BF16)


def project_kernel(first, last, inner, model_width, unused, *refs):
    del unused
    pieces, refs = refs[:6], refs[6:]
    chooser_ref, gain_ref, weights_ref, refs = refs[0], refs[1], refs[2], refs[3:]
    if not first:
        total_in, squares_in, refs = refs[0], refs[1], refs[2:]
    if not last:
        ends_ref, total_ref, squares_ref = refs
    else:
        ends_ref, gate_ref, channels_ref, steps_ref, total_ref, squares_ref = refs
    width = pieces[0].shape[1]

    def add(raw, fresh):
        ends_ref[...] = jnp.dot(chooser_ref[...], raw, preferred_element_type=F32)
        wide = raw.astype(F32)
        scaled = (wide * gain_ref[...]).astype(BF16)
        product = jnp.dot(scaled, weights_ref[...], preferred_element_type=F32)
        square = wide * wide
        parts = [square[:, at : at + LANES] for at in range(0, 2 * width, LANES)]
        if fresh:
            total_ref[...] = product if first else product + total_in[...]
            squares_ref[...] = functools.reduce(jnp.add, parts if first else parts + [squares_in[...]])
        else:
            total_ref[...] += product
            squares_ref[...] += functools.reduce(jnp.add, parts)

    upper, upper_far, upper_rest, lower, lower_near, lower_rest = pieces

    @pl.when(pl.program_id(0) == 0)
    def _():
        top = jnp.concatenate([upper[...], upper_rest[:, :width]], axis=1)
        bottom = jnp.concatenate([lower[...], lower_near[...]], axis=1)
        add(jnp.concatenate([top, bottom], axis=0), True)

    @pl.when(pl.program_id(0) == 1)
    def _():
        top = jnp.concatenate([upper_far[...], upper_rest[:, width:]], axis=1)
        add(jnp.concatenate([top, lower_rest[...]], axis=0), False)
        if not last:
            return
        inv_rms = jnp.sum(squares_ref[...], axis=1, keepdims=True) / model_width
        inv_rms = lax.rsqrt(inv_rms + EPSILON)
        gate_ref[...] = (total_ref[:, :inner] * inv_rms).astype(BF16)
        channels_ref[...] = (total_ref[:, inner:-LANES] * inv_rms).astype(BF16)
        steps_ref[...] = total_ref[:, -LANES:] * inv_rms


def both_heads(table, pair, head_size):
    rows = table.shape[0]
    lane = lax.broadcasted_iota(jnp.int32, (rows, 2 * head_size), 1)
    return jnp.where(
        lane < head_size, table[:, 2 * pair : 2 * pair + 1], table[:, 2 * pair + 1 : 2 * pair + 2]
    )


def over_states(row, heads, head_size):
    return jnp.concatenate(
        [jnp.broadcast_to(row[:, h : h + 1], (head_size, LANES)) for h in range(heads)], axis=0
    )


def conv_kernel(
    heads,
    unused,
    channels_ref,
    rim_ref,
    edges_ref,
    taps_ref,
    bias_ref,
    steps_ref,
    step_bias_ref,
    decay_ref,
    marks_ref,
    segment_ref,
    init_ref,
    x_ref,
    keys_ref,
    queries_ref,
    run_ref,
    less_ref,
    spread_ref,
    leaving_ref,
    gain_ref,
):
    del unused
    rows, inner = x_ref.shape
    state = keys_ref.shape[1]
    head_size = inner // heads
    taps = taps_ref.shape[0]
    channels = channels_ref[...]
    sources = jnp.concatenate([channels, rim_ref[...], edges_ref[...]], axis=0)
    summed = bias_ref[...] + taps_ref[taps - 1 : taps] * channels.astype(F32)
    column = lax.broadcasted_iota(jnp.int32, (rows, sources.shape[0]), 1)
    for back in range(1, taps):
        pick = jnp.where(marks_ref[:, back - 1 : back] == column, 1.0, 0.0).astype(BF16)
        value = jnp.dot(pick, sources, preferred_element_type=F32)
        summed = summed + taps_ref[taps - 1 - back : taps - back] * value
    mixed = (summed / (1.0 + jnp.exp(-summed))).astype(BF16)
    x = mixed[:, :inner]
    keys = mixed[:, inner : inner + state]
    x_ref[...] = x
    keys_ref[...] = keys
    queries_ref[...] = mixed[:, inner + state :]
    raw = steps_ref[...] + step_bias_ref[...]
    step = jnp.maximum(raw, 0.0) + jnp.log1p(jnp.exp(-jnp.abs(raw)))
    log_decay = -jnp.exp(decay_ref[...]) * step
    segment = marks_ref[:, 4:5]
    same = segment == segment_ref[0:1, :]
    row = lax.broadcasted_iota(jnp.int32, (rows, rows), 0)
    other = lax.broadcasted_iota(jnp.int32, (rows, rows), 1)
    until = jnp.where(same & (other <= row), 1.0, 0.0)
    after = jnp.where(same & (other > row), 1.0, 0.0)
    run = jnp.dot(until, log_decay, precision=HIGHEST, preferred_element_type=F32)
    tail = jnp.dot(after, log_decay, precision=HIGHEST, preferred_element_type=F32)
    run_ref[...] = run
    less_ref[...] = (run - jnp.log(step)).T[:8]
    share = (jnp.exp(tail) * step).astype(BF16).astype(F32)
    spread = jnp.concatenate(
        [
            both_heads(share, p, head_size)
            * x[:, p * 2 * head_size : (p + 1) * 2 * head_size].astype(F32)
            for p in range(heads // 2)
        ],
        axis=1,
    )
    spread = spread.T.astype(BF16)
    spread_ref[...] = spread
    last = jnp.where(segment == segment[rows - 1 : rows], 1.0, 0.0)
    leaving = jnp.dot(spread, (keys.astype(F32) * last).astype(BF16), preferred_element_type=F32)
    gain = jnp.exp(run[rows - 1 : rows])
    carried = jnp.broadcast_to(marks_ref[rows - 1 : rows, 5:6], (heads * head_size, state)) > 0
    gain_wide = over_states(gain, heads, head_size)
    leaving_ref[...] = jnp.where(carried, leaving, leaving + gain_wide * init_ref[...])
    gain_ref[...] = jnp.where(carried, gain_wide, 0.0)


def scan_kernel(
    heads,
    block,
    unused,
    x_ref,
    keys_ref,
    queries_ref,
    run_ref,
    less_ref,
    marks_ref,
    segment_ref,
    table_ref,
    skip_ref,
    y_ref,
    masked_ref,
    begun_ref,
):
    del unused
    rows, inner = x_ref.shape
    head_size = inner // heads
    slots = table_ref.shape[1] // queries_ref.shape[1]
    queries = queries_ref[...].astype(F32)
    slot = marks_ref[:, 3:4]
    placed = jnp.concatenate(
        [(queries * jnp.where(slot == o, 1.0, 0.0)).astype(BF16) for o in range(slots)], axis=1
    )
    begun_ref[...] = lax.dot_general(
        placed, table_ref[...], ROWS_BY_ROWS, preferred_element_type=F32
    )
    blocks = [(t, s) for t in range(rows // block) for s in range(t + 1)]
    for at, (t, s) in enumerate(blocks):
        here, there = pl.ds(t * block, block), pl.ds(s * block, block)
        scores = lax.dot_general(
            queries_ref[here], keys_ref[there], ROWS_BY_ROWS, preferred_element_type=F32
        )
        same = marks_ref[here, 4:5] == segment_ref[0:1, there]
        if t == s:
            row = lax.broadcasted_iota(jnp.int32, (block, block), 0)
            other = lax.broadcasted_iota(jnp.int32, (block, block), 1)
            same = same & (other <= row)
        masked_ref[at] = jnp.where(same, scores, 0.0)
    grown = jnp.exp(run_ref[...])
    lane = lax.broadcasted_iota(jnp.int32, (block, 2 * head_size), 1)
    for p in range(heads // 2):
        wide = slice(p * 2 * head_size, (p + 1) * 2 * head_size)
        x = x_ref[:, wide].astype(F32)
        y = both_heads(grown, p, head_size) * begun_ref[:, wide] + both_heads(skip_ref[...], p, head_size) * x
        sums = [y[t * block : (t + 1) * block] for t in range(rows // block)]
        for at, (t, s) in enumerate(blocks):
            here, there = slice(t * block, (t + 1) * block), slice(s * block, (s + 1) * block)
            for side in range(2):
                head = 2 * p + side
                mine = (lane < head_size) if side == 0 else (lane >= head_size)
                x_own = jnp.where(mine, x[there], 0.0).astype(BF16)
                gap = run_ref[here, head : head + 1] - less_ref[head : head + 1, there]
                weight = (masked_ref[at] * jnp.exp(jnp.minimum(gap, 80.0))).astype(BF16)
                sums[t] = sums[t] + jnp.dot(weight, x_own, preferred_element_type=F32)
        for t in range(rows // block):
            y_ref[t * block : (t + 1) * block, wide] = sums[t]


def gate_kernel(
    heads, unused, y_ref, queries_ref, run_ref, marks_ref, entry_ref, gate_ref, gain_ref, out_ref, sq_ref
):
    del unused
    rows, inner = y_ref.shape
    head_size = inner // heads
    carried = jnp.where(marks_ref[:, 5:6] > 0, 1.0, 0.0)
    queries = (queries_ref[...].astype(F32) * carried).astype(BF16)
    held = lax.dot_general(
        queries, entry_ref[...].astype(BF16), ROWS_BY_ROWS, preferred_element_type=F32
    )
    grown = jnp.exp(run_ref[...])
    grown = jnp.concatenate([both_heads(grown, p, head_size) for p in range(heads // 2)], axis=1)
    gate = gate_ref[...].astype(F32)
    gated = (y_ref[...] + grown * held) * (gate / (1.0 + jnp.exp(-gate)))
    out_ref[...] = (gated * gain_ref[...]).astype(BF16)
    square = jnp.sum(gated * gated, axis=1, keepdims=True)
    sq_ref[...] = jnp.broadcast_to(square, (rows, LANES)).T[:8]


def norm_scale(own_ref, other_ref, channels):
    scale = lax.rsqrt((own_ref[0:1] + other_ref[0:1]) / channels + EPSILON)
    return jnp.broadcast_to(scale, (LANES, scale.shape[1])).T


def out_kernel(width, count, scaled, blocks, gated_ref, own_ref, other_ref, chooser_ref, *refs):
    del blocks
    weights, outs = refs[: 4 * count], refs[4 * count :]
    upper_out, upper_in, lower_out, lower_in, ends_ref = outs
    rows, inner = gated_ref.shape
    half = rows // 2
    if scaled:
        scale = norm_scale(own_ref, other_ref, 2 * inner)
        scale = jnp.concatenate([scale] * (width // LANES), axis=1)
    else:
        scale = jnp.ones((rows, width), F32)
    gated = gated_ref[...]
    end_rows = jnp.dot(chooser_ref[...], gated, preferred_element_type=F32).astype(BF16)
    end_scale = jnp.dot(
        chooser_ref[...].astype(F32), scale, precision=HIGHEST, preferred_element_type=F32
    )
    for at, w in enumerate(weights):
        index, place = divmod(at, count)
        part = jnp.dot(gated, w[...], preferred_element_type=F32) * scale
        top, bottom = part[:half], part[half:]
        low = (index // 2) * count + place
        target = upper_out if index % 2 else upper_in
        target[:, low * width : (low + 1) * width] = top.astype(target.dtype)
        low = (index % 2) * count + place
        target = lower_out if index // 2 else lower_in
        target[:, low * width : (low + 1) * width] = bottom.astype(target.dtype)
        ends_ref[:, at * width : (at + 1) * width] = (
            jnp.dot(end_rows, w[...], preferred_element_type=F32) * end_scale
        )


def near_kernel(unused, upper_ref, upper_got, lower_ref, lower_got, *outs):
    del unused
    for kept, got, keep_ref, send_ref in (
        (upper_ref, upper_got, outs[0], outs[1]),
        (lower_ref, lower_got, outs[2], outs[3]),
    ):
        wide = keep_ref.shape[1]
        keep_ref[...] = kept[:, :wide].astype(F32) + got[:, :wide].astype(F32)
        send_ref[...] = (kept[:, wide:].astype(F32) + got[:, wide:].astype(F32)).astype(BF16)


def plane_kernel(unused, upper_ref, upper_got, lower_ref, lower_got, *outs):
    del unused
    half, width = upper_ref.shape[0], outs[0].shape[1]
    for at, out_ref in enumerate(outs):
        wide = slice(at * width, (at + 1) * width)
        upper = upper_ref[:, wide] + upper_got[:, wide].astype(F32)
        lower = lower_ref[:, wide] + lower_got[:, wide].astype(F32)
        out_ref[:half] = upper.astype(out_ref.dtype)
        out_ref[half:] = lower.astype(out_ref.dtype)


def hidden_kernel(unused, tokens_ref, own_ref, *refs):
    del unused
    total = own_ref[...]
    for part in refs[:-1]:
        total = total + part[...].astype(F32)
    refs[-1][...] = (tokens_ref[...].astype(F32) + total).astype(BF16)


def scale_kernel(unused, own_ref, other_ref, chooser_ref, channels_ref, *refs):
    del unused
    raw, outs = refs[:5], refs[5:]
    half = raw[0].shape[0]
    scale = norm_scale(own_ref, other_ref, 2 * channels_ref.shape[1])
    end_scale = jnp.dot(
        chooser_ref[...].astype(F32), scale, precision=HIGHEST, preferred_element_type=F32
    )
    for at, (source, out_ref) in enumerate(zip(raw, outs)):
        factor = end_scale if at == 4 else scale[:half] if at < 2 else scale[half:]
        for lane in range(0, source.shape[1], LANES):
            value = source[:, lane : lane + LANES] * factor
            out_ref[:, lane : lane + LANES] = value.astype(out_ref.dtype)


def ends_kernel(width, col_size, sum_groups, gather_groups, place, *refs):
    sources, outs = refs[:-2], refs[-2:]
    groups = [(shifts, outs[0]) for shifts in sum_groups]
    groups += [(shifts, outs[1]) for shifts in gather_groups]
    for source, (shifts, out_ref) in zip(sources, groups):
        for at in range(source.shape[1] // width):
            block = block_of(shifts, at, place, col_size)
            to = pl.ds(pl.multiple_of(block * width, width), width)
            out_ref[:, to] = source[:, at * width : (at + 1) * width]


def finals_kernel(
    heads, added, first, spread_ref, keys_ref, marks_ref, ends_ref, entry_ref, init_ref, _, *refs
):
    out_ref = refs[-1]
    count, inner, state = out_ref.shape
    head_size = inner // heads
    slot = (first[0] + pl.program_id(0)) * count
    keys = keys_ref[...].astype(F32)
    owner = marks_ref[:, 6:7]
    mine = [
        (keys * jnp.where(owner == slot + i, ends_ref[i, :, heads : heads + 1], 0.0)).astype(BF16)
        for i in range(count)
    ]
    states = jnp.dot(
        spread_ref[...], jnp.concatenate(mine, axis=1), preferred_element_type=F32
    )
    for i in range(count):
        gain = over_states(ends_ref[i], heads, head_size)
        carried = jnp.broadcast_to(ends_ref[i, :, heads + 1 : heads + 2], (inner, state)) > 0.5
        value = states[:, i * state : (i + 1) * state]
        value = value + gain * jnp.where(carried, entry_ref[...], init_ref[i])
        out_ref[i] = value + refs[0][i] if added else value


def per_device(
    tokens,
    lengths,
    deal,
    pre_gain,
    w_inner,
    w_group,
    w_step,
    conv_inner,
    conv_group,
    conv_bias_inner,
    conv_bias_group,
    edge_inner,
    edge_group,
    init_states,
    step_bias,
    decay_log,
    skip,
    inner_gain,
    w_out,
    final_gain,
    w_head,
):
    rows, width = tokens.shape
    model_width = pre_gain.shape[0]
    requests = lengths.shape[0]
    taps = conv_inner.shape[0]
    inner = w_inner.shape[2]
    heads = w_step.shape[1]
    head_size = inner // heads
    state = w_group.shape[3]
    row_at, col_at, seq_at = (lax.axis_index(name) for name in ("row", "col", "seq"))
    row_size, col_size, seq_size = (lax.axis_size(name) for name in ("row", "col", "seq"))
    group_local = col_at * w_group.shape[2] // col_size

    def own_group(table, axis):
        return lax.dynamic_index_in_dim(table, group_local, axis, keepdims=False)

    def in_lanes(values):
        return jnp.pad(values, (0, LANES - heads))[None, :]

    first_row = seq_at * rows
    counts = jnp.concatenate([lengths, deal, jnp.reshape(first_row, (1,)).astype(jnp.int32)])
    marks, segment_row, chooser, slots = call(
        functools.partial(setup_kernel, taps),
        [
            ((rows, LANES), jnp.int32),
            ((8, rows), jnp.int32),
            ((requests, rows), BF16),
            ((requests, 2 * LANES), F32),
        ],
        prefetch=counts,
        vmem=4,
        work=0,
    )
    place = jnp.stack([row_at, col_at, group_local]).astype(jnp.int32)

    init_flat = jnp.reshape(init_states, (requests, inner, state))
    skip_row = in_lanes(skip)
    gains = pre_gain[None, :]

    gather_groups = ((0,1),(2,3))
    sum_groups = ((2,3),(0,1))

    n_all = 2 * inner + 2 * state + LANES
    steps_across = jnp.transpose(w_step)

    def weights_of(shifts, gain_row):
        count = row_size * len(shifts)
        parts = count // 2

        def specs(shape, where):
            return [
                pl.BlockSpec(shape, lambda i, p, at=at: where(
                    block_of(shifts, i * parts + at, p, col_size)
                ))
                for at in range(parts)
            ]

        return call(
            functools.partial(weights_kernel, parts),
            [((count * width, n_all), BF16), ((1, count * width), F32)],
            *[w_inner] * parts,
            *[w_group] * parts,
            *[steps_across] * parts,
            *[gain_row] * parts,
            prefetch=place,
            grid=(count // parts,),
            in_specs=specs((width,) + w_inner.shape[1:], lambda b: (b, 0, 0))
            + specs((width,) + w_group.shape[1:], lambda b: (b, 0, 0, 0))
            + specs((heads, width), lambda b: (0, b))
            + specs((1, width), lambda b: (0, b)),
            out_specs=[
                pl.BlockSpec((parts * width, n_all), lambda i, p: (i, 0)),
                pl.BlockSpec((1, parts * width), lambda i, p: (0, i)),
            ],
            vmem=58,
        )

    gain_row = pre_gain[None, :]
    token_blocks = {0: tokens}
    token_blocks[1] = from_ahead(tokens, "col", 1)
    later, token_blocks[1] = lax.optimization_barrier((tokens, token_blocks[1]))
    for shift in range(2, col_size):
        source = token_blocks[1] if shift == 2 else later
        token_blocks[shift] = from_ahead(source, "col", 1 if shift == 2 else shift)
    gain_row = after(gain_row, token_blocks[1])
    token_ends = []
    carry = ()
    ready = ()
    for shifts in gather_groups:
        first, last = shifts == gather_groups[0], shifts == gather_groups[-1]
        pieces = plane_gather(jnp.concatenate([token_blocks[i] for i in shifts], axis=1))
        weights, gains = weights_of(shifts, after(gain_row, *ready) if ready else gain_row)
        ready = (pieces[1],)
        count = row_size * len(shifts)
        depth = count * width // 2
        outs = [((requests, count * width), F32)]
        totals = [((rows, n_all), F32), ((rows, LANES), F32)]
        if not last:
            outs += totals
        else:
            outs += [((rows, inner), BF16), ((rows, inner + 2 * state), BF16), ((rows, LANES), F32)]
        piece_ends, *carry = call(
            functools.partial(project_kernel, first, last, inner, model_width),
            outs,
            *pieces,
            chooser,
            gains,
            weights,
            *carry,
            grid=(2,),
            in_specs=[None] * 7
            + [
                pl.BlockSpec((1, depth), lambda i, _: (0, i)),
                pl.BlockSpec((depth, n_all), lambda i, _: (i, 0)),
            ]
            + [None] * len(carry),
            out_specs=[pl.BlockSpec((requests, depth), lambda i, _: (0, i))]
            + [None] * (len(outs) - 1),
            scratch=totals if last else [],
            vmem=24,
        )
        token_ends.append(piece_ends)
    gate_in, channels, step_raw = carry
    ready = gains

    init_last = lax.dynamic_index_in_dim(init_flat, after(marks, ready)[rows - 1, 6], 0, keepdims=False)
    (table,) = call(
        table_kernel,
        [((inner, requests * state), BF16)],
        after(init_flat, ready),
        grid=(requests,),
        in_specs=[pl.BlockSpec((1, inner, state), lambda i, _: (i, 0, 0))],
        out_specs=[pl.BlockSpec((inner, state), lambda i, _: (0, i))],
        vmem=4,
        work=0,
    )
    conv_taps = jnp.concatenate(
        [conv_inner, jnp.reshape(own_group(after(conv_group, ready), 2), (taps, 2 * state))], axis=1
    )
    conv_bias = jnp.concatenate(
        [conv_bias_inner, jnp.reshape(own_group(after(conv_bias_group, ready), 1), (2 * state,))]
    )[None, :]
    edges = jnp.concatenate(
        [after(edge_inner, ready), jnp.reshape(own_group(after(edge_group, ready), 3), (requests, taps - 1, 2 * state))],
        axis=2,
    )
    edges = jnp.reshape(edges, (requests * (taps - 1), inner + 2 * state))

    rim = from_behind(channels[rows - RIM :], "seq", 1)
    x, keys, queries, run, less, spread, leaving, gain_carried = call(
        functools.partial(conv_kernel, heads),
        [
            ((rows, inner), BF16),
            ((rows, state), BF16),
            ((rows, state), BF16),
            ((rows, LANES), F32),
            ((8, rows), F32),
            ((inner, rows), BF16),
            ((inner, state), F32),
            ((inner, state), F32),
        ],
        channels,
        rim,
        edges,
        conv_taps,
        conv_bias,
        step_raw,
        in_lanes(step_bias),
        in_lanes(decay_log),
        after(marks, table),
        segment_row,
        init_last,
    )
    entry = from_behind(leaving, "seq", 1)
    for _ in range(seq_size - 2):
        entry = from_behind(gain_carried * entry + leaving, "seq", 1)

    block = 256
    pairs = (rows // block) * (rows // block + 1) // 2
    y = pl.pallas_call(
        functools.partial(scan_kernel, heads, block),
        out_shape=jax.ShapeDtypeStruct((rows, inner), F32),
        grid_spec=pltpu.PrefetchScalarGridSpec(
            num_scalar_prefetch=1,
            grid=(1,),
            in_specs=[
                pl.BlockSpec(a.shape, lambda *_: (0, 0))
                for a in (x, keys, queries, run, less, marks, segment_row, table, skip_row)
            ],
            out_specs=pl.BlockSpec((rows, inner), lambda *_: (0, 0)),
            scratch_shapes=[
                pltpu.VMEM((pairs, block, block), F32),
                pltpu.VMEM((rows, inner), F32),
            ],
        ),
        compiler_params=pltpu.CompilerParams(vmem_limit_bytes=16 * MIB),
    )(
        jnp.zeros((1,), jnp.int32),
        x,
        keys,
        queries,
        run,
        less,
        marks,
        segment_row,
        table,
        skip_row,
    )
    gated, own_squares = call(
        functools.partial(gate_kernel, heads),
        [((rows, inner), BF16), ((8, rows), F32)],
        y,
        queries,
        run,
        marks,
        entry,
        gate_in,
        inner_gain[None, :],
    )
    other_squares = from_partner(own_squares, "col", 0)

    half_out, got = [], []
    for shifts in sum_groups:
        count = len(shifts)
        first = shifts == sum_groups[0]
        side = (rows // 2, 2 * count * width)
        kinds = [BF16] * 4
        ends_out = ((requests, row_size * count * width), F32)
        outs = call(
            functools.partial(out_kernel, width, count, not first),
            [(side, F32 if first else kind) for kind in kinds] + [ends_out],
            gated,
            own_squares,
            own_squares if first else other_squares,
            chooser,
            *[w_out] * (row_size * count),
            prefetch=place,
            in_specs=[None] * 4
            + [
                pl.BlockSpec(
                    (inner, width),
                    lambda i, p, at=at, shifts=shifts: (0, block_of(shifts, at, p, col_size)),
                )
                for at in range(row_size * count)
            ],
            vmem=16,
            work=10 if first else 0,
        )
        if first:
            other_squares = after(other_squares, outs[0])
            outs = call(
                scale_kernel,
                [(side, kind) for kind in kinds] + [ends_out],
                own_squares,
                other_squares,
                chooser,
                gated,
                *outs,
                vmem=12,
                work=0,
            )
        half_out.append(outs)
        got.append((from_partner(outs[0], "row", 0), from_partner(outs[2], "row", 1)))
    end_sum, end_tokens = call(
        functools.partial(ends_kernel, width, col_size, sum_groups, gather_groups),
        [((requests, model_width), F32)] * 2,
        after(half_out[0][4], *got[0]),
        *[outs[4] for outs in half_out[1:]],
        *token_ends,
        prefetch=place,
        vmem=4,
        work=0,
    )
    for axis, bit in (("col", 0), ("col", 1), ("row", 0), ("row", 1)):
        end_sum = end_sum + from_partner(end_sum.astype(BF16), axis, bit).astype(F32)

    def finals_after(far_ready):
        end_run = jnp.dot(chooser.astype(F32), run, precision=HIGHEST)[:, :heads]
        ends_here = slots[:, :1]
        end_marks = jnp.concatenate(
            [
                jnp.exp(end_run) * ends_here,
                ends_here,
                slots[:, LANES : LANES + 1],
                jnp.zeros((requests, LANES - heads - 2), F32),
            ],
            axis=1,
        )[:, None, :]

        kept = requests // seq_size

        def finals_of(first, steps, ready, extra):
            count = steps * kept
            by_slot = pl.BlockSpec((kept, inner, state), lambda i, s: (s[0] + i, 0, 0))
            by_step = pl.BlockSpec((kept, inner, state), lambda i, s: (i, 0, 0))
            return call(
                functools.partial(finals_kernel, heads, bool(extra)),
                [((count, inner, state), F32)],
                spread,
                keys,
                marks,
                end_marks,
                entry,
                init_flat,
                after(half_out[1][4], *ready),
                *extra,
                prefetch=jnp.reshape(first, (1,)).astype(jnp.int32),
                grid=(steps,),
                in_specs=[None] * 3
                + [pl.BlockSpec((kept, 1, LANES), lambda i, s: (s[0] + i, 0, 0)), None, by_slot]
                + [pl.BlockSpec(memory_space=pl.ANY)]
                + [by_step] * len(extra),
                out_specs=[by_step],
                vmem=20,
                work=0,
            )[0]

        if seq_size == 2:
            lent = finals_of(1 - seq_at, 1, far_ready, [])
            finals = finals_of(seq_at, 1, (), [from_partner(lent, "seq", 0)])
        else:
            finals = lax.psum_scatter(
                finals_of(jnp.int32(0), seq_size, (), []), "seq", scatter_dimension=0, tiled=True
            )
        return finals

    pieces = {}
    for shifts, outs, (upper_got, lower_got) in zip(sum_groups, half_out, got):
        _, upper_in, _, lower_in, _ = outs
        wide = len(shifts) * width
        upper, upper_far, lower, lower_near = call(
            near_kernel,
            [((rows // 2, wide), F32), ((rows // 2, wide), BF16)] * 2,
            upper_in,
            upper_got,
            lower_in,
            lower_got,
            vmem=8,
            work=10,
        )
        upper_far = from_partner(upper_far, "row", 1)
        lower_near = from_partner(lower_near, "row", 0)
        sums = call(
            plane_kernel,
            [((rows, width), BF16 if shift else F32) for shift in shifts],
            upper,
            upper_far,
            lower,
            lower_near,
            vmem=8,
            work=10,
        )
        if shifts == sum_groups[-2]:
            far_ready = sums
        for shift, part in zip(shifts, sums):
            pieces[shift] = from_ahead(part, "col", col_size - shift) if shift else part
    finals = finals_after(far_ready)
    if seq_size == 2:
        ending = after(end_tokens + end_sum, finals)
        ending = ending + from_partner(ending, "seq", 0)
    else:
        ending = lax.psum(end_tokens + end_sum, "seq")
    (hidden_out,) = call(
        hidden_kernel,
        [((rows, width), BF16)],
        tokens,
        *[pieces[shift] for shift in range(col_size)],
        vmem=4,
        work=30,
    )

    last_rows = ending.astype(BF16).astype(F32)
    final_scale = lax.rsqrt(jnp.sum(last_rows * last_rows, axis=1) / model_width + EPSILON)
    head_in = (last_rows * final_scale[:, None] * final_gain).astype(BF16)
    logits = jnp.dot(head_in, w_head, preferred_element_type=F32)

    final_states = jnp.reshape(finals, (finals.shape[0], heads, head_size, state))
    return (hidden_out, final_states, logits)


def solution(mesh):
    in_specs = (
        P("seq", ("row", "col")),
        P(),
        P(),
        P(),
        P(None, None, ("row", "col")),
        P(None, None, "row", None),
        P(None, ("row", "col")),
        P(None, ("row", "col")),
        P(None, None, "row", None),
        P(("row", "col")),
        P(None, "row", None),
        P(None, None, ("row", "col")),
        P(None, None, None, "row", None),
        P(None, ("row", "col"), None, None),
        P(("row", "col")),
        P(("row", "col")),
        P(("row", "col")),
        P(("row", "col")),
        P(("row", "col"), None),
        P(),
        P(None, ("seq", "row", "col")),
    )
    out_specs = (
        P("seq", ("row", "col")),
        P("seq", ("row", "col"), None, None),
        P(None, ("seq", "row", "col")),
    )
    return jax.shard_map(
        per_device, mesh=mesh, in_specs=in_specs, out_specs=out_specs, check_vma=False
    )
```

```python
import functools

import jax
import jax.numpy as jnp
from jax import lax
from jax.experimental import pallas as pl
from jax.experimental.pallas import tpu as pltpu
from jax.sharding import PartitionSpec as P

EPSILON = 1e-05
HIGHEST = lax.Precision.HIGHEST
F32 = jnp.float32
BF16 = jnp.bfloat16
LANES = 128
RIM = 16
MIB = 1024 * 1024
ROWS_BY_ROWS = (((1,), (1,)), ((), ()))


def from_behind(block, axis, distance):
    devices = range(lax.axis_size(axis))
    route = [(i - distance, i) for i in devices if i - distance in devices]
    return lax.ppermute(block, axis, route)


def from_partner(x, axis, bit):
    return lax.ppermute(x, axis, [(i, i ^ 1 << bit) for i in range(lax.axis_size(axis))])


def from_ahead(x, axis, distance):
    size = lax.axis_size(axis)
    return lax.ppermute(x, axis, [((i + distance) % size, i) for i in range(size)])


def after(x, *others):
    return lax.optimization_barrier((x,) + others)[0]


def call(kernel, outs, *args, prefetch=None, grid=(1,), in_specs=None, out_specs=None, scratch=(), vmem=12, work=20):
    params = pltpu.CompilerParams(vmem_limit_bytes=vmem * MIB)
    shapes = [jax.ShapeDtypeStruct(shape, kind) for shape, kind in outs]

    def whole(shape):
        zeros = (0,) * len(shape)
        return pl.BlockSpec(shape, lambda *_: zeros)

    specs = [
        whole(a.shape) if spec is None else spec
        for a, spec in zip(args, in_specs or [None] * len(args))
    ]
    gives = [
        whole(shape) if spec is None else spec
        for (shape, _), spec in zip(outs, out_specs or [None] * len(outs))
    ]
    prefetch = jnp.zeros((1,), jnp.int32) if prefetch is None else prefetch
    spec = pltpu.PrefetchScalarGridSpec(
        num_scalar_prefetch=1, grid=grid, in_specs=specs, out_specs=gives,
        scratch_shapes=[pltpu.VMEM(shape, kind) for shape, kind in scratch],
    )
    return pl.pallas_call(
        kernel,
        out_shape=shapes,
        grid_spec=spec,
        compiler_params=params,
        cost_estimate=pl.CostEstimate(flops=work * 1_000_000_000, bytes_accessed=100_000_000 if work else 1000, transcendentals=0),
    )(prefetch, *args)


def plane_gather(block):
    half = block.shape[0] // 2
    upper, lower = block[:half], block[half:]
    upper_far = from_partner(upper, "row", 1)
    lower_near = from_partner(lower, "row", 0)
    upper_rest = from_partner(jnp.concatenate([upper, upper_far], axis=1), "row", 0)
    lower_rest = from_partner(jnp.concatenate([lower, lower_near], axis=1), "row", 1)
    return upper, upper_far, upper_rest, lower, lower_near, lower_rest


def block_of(shifts, at, place, col_size):
    gap = shifts[-1] - shifts[0] if len(shifts) > 1 else 0
    shift = shifts[0] + (at % len(shifts)) * gap
    return (place[0] ^ (at // len(shifts))) * col_size + (place[1] + shift) % col_size


def setup_kernel(taps, counts, marks_ref, segment_ref, chooser_ref, slots_ref):
    requests = chooser_ref.shape[0]
    rows = marks_ref.shape[0]
    first_row = counts[2 * requests]
    begins, owners = [], []
    total = jnp.int32(0)
    for k in range(requests):
        begins.append(total - first_row)
        owners.append(counts[requests + k])
        total = total + counts[k]
    stops = begins[1:] + [total - first_row]

    def latest(position, values):
        found = jnp.full(position.shape, values[0], jnp.int32)
        for begin, value in zip(begins[1:], values[1:]):
            found = jnp.where(position >= begin, value, found)
        return found

    position = lax.broadcasted_iota(jnp.int32, (rows, LANES), 0)
    lane = lax.broadcasted_iota(jnp.int32, (rows, LANES), 1)
    owner = latest(position, owners)
    begin = latest(position, begins)
    offset = position - begin
    marks = owner
    for back in range(1, taps):
        edge = rows + RIM + owner * (taps - 1) + (taps - 1 - back) + offset
        inside = jnp.where(position >= back, position - back, rows + RIM + position - back)
        marks = jnp.where(lane == back - 1, jnp.where(offset >= back, inside, edge), marks)
    marks = jnp.where((lane == 3) & (begin < 0), requests, marks)
    marks = jnp.where(lane == 4, begin, marks)
    marks = jnp.where(lane == 5, jnp.where(begin < 0, 1, 0), marks)
    marks_ref[...] = marks
    across = lax.broadcasted_iota(jnp.int32, (8, rows), 1)
    segment_ref[...] = latest(across, begins)
    slot = lax.broadcasted_iota(jnp.int32, (requests, rows), 0)
    column = lax.broadcasted_iota(jnp.int32, (requests, rows), 1)
    slot_lane = lax.broadcasted_iota(jnp.int32, (requests, LANES), 0)
    chooser = jnp.zeros((requests, rows), F32)
    slot_begin = jnp.zeros((requests, LANES), F32)
    slot_end = jnp.zeros((requests, LANES), F32)
    for k in range(requests):
        last = stops[k] - 1
        chooser = jnp.where((slot == owners[k]) & (column == last), 1.0, chooser)
        here = jnp.where((last >= 0) & (last < rows), 1.0, 0.0)
        slot_end = jnp.where(slot_lane == owners[k], here, slot_end)
        before = jnp.where(begins[k] < 0, 1.0, 0.0)
        slot_begin = jnp.where(slot_lane == owners[k], before, slot_begin)
    chooser_ref[...] = chooser.astype(BF16)
    slots_ref[:, :LANES] = slot_end
    slots_ref[:, LANES:] = slot_begin


def weights_kernel(parts, place, *refs):
    out_ref, gain_out = refs[4 * parts :]
    rows = refs[0].shape[0]
    for part in range(parts):
        main_ref, group_ref, step_ref, gain_ref = refs[part : 4 * parts : parts]
        weights_block(
            place[2],
            main_ref,
            group_ref,
            step_ref,
            out_ref.at[pl.ds(part * rows, rows)],
        )
        gain_out[:, part * rows : (part + 1) * rows] = gain_ref[...]


def weights_block(group, main_ref, group_ref, step_ref, out_ref):
    rows, _, inner = main_ref.shape
    state = group_ref.shape[3]
    heads = step_ref.shape[0]
    half = rows // 2
    row = lax.broadcasted_iota(jnp.int32, (rows, rows), 0)
    column = lax.broadcasted_iota(jnp.int32, (rows, rows), 1)
    source = jnp.where(row < half, 2 * row, 2 * (row - half) + 1)
    pick = jnp.where(source == column, 1.0, 0.0).astype(BF16)
    flat = main_ref[...].reshape(2 * rows, inner)
    for at in range(2):
        got = jnp.dot(pick, flat[at * rows : (at + 1) * rows], preferred_element_type=F32)
        got = got.astype(BF16)
        out_ref[at * half : (at + 1) * half, :inner] = got[:half]
        out_ref[at * half : (at + 1) * half, inner : 2 * inner] = got[half:]
    take = rows // 4
    row, column = row[:half], column[:half]
    source = jnp.where(row < take, 4 * row, 4 * (row - take) + 2) + group
    pick = jnp.where(source == column, 1.0, 0.0).astype(BF16)
    flat = group_ref[...].reshape(4 * rows, state)
    for at in range(4):
        got = jnp.dot(pick, flat[at * rows : (at + 1) * rows], preferred_element_type=F32)
        got = got.astype(BF16)
        out_ref[at * take : (at + 1) * take, 2 * inner : 2 * inner + state] = got[:take]
        out_ref[at * take : (at + 1) * take, 2 * inner + state : 2 * inner + 2 * state] = got[take:]
    steps = jnp.concatenate(
        [step_ref[...].astype(F32), jnp.zeros((LANES - heads, rows), F32)], axis=0
    )
    out_ref[:, 2 * inner + 2 * state :] = steps.T.astype(BF16)


def table_kernel(unused, init_ref, out_ref):
    del unused
    out_ref[...] = init_ref[0].astype(BF16)


def project_kernel(first, last, inner, model_width, unused, *refs):
    del unused
    pieces, refs = refs[:6], refs[6:]
    chooser_ref, gain_ref, weights_ref, refs = refs[0], refs[1], refs[2], refs[3:]
    if not first:
        total_in, squares_in, refs = refs[0], refs[1], refs[2:]
    if not last:
        ends_ref, total_ref, squares_ref = refs
    else:
        ends_ref, gate_ref, channels_ref, steps_ref, total_ref, squares_ref = refs
    width = pieces[0].shape[1]

    def add(raw, fresh):
        ends_ref[...] = jnp.dot(chooser_ref[...], raw, preferred_element_type=F32)
        wide = raw.astype(F32)
        scaled = (wide * gain_ref[...]).astype(BF16)
        product = jnp.dot(scaled, weights_ref[...], preferred_element_type=F32)
        square = wide * wide
        parts = [square[:, at : at + LANES] for at in range(0, 2 * width, LANES)]
        if fresh:
            total_ref[...] = product if first else product + total_in[...]
            squares_ref[...] = functools.reduce(jnp.add, parts if first else parts + [squares_in[...]])
        else:
            total_ref[...] += product
            squares_ref[...] += functools.reduce(jnp.add, parts)

    upper, upper_far, upper_rest, lower, lower_near, lower_rest = pieces

    @pl.when(pl.program_id(0) == 0)
    def _():
        top = jnp.concatenate([upper[...], upper_rest[:, :width]], axis=1)
        bottom = jnp.concatenate([lower[...], lower_near[...]], axis=1)
        add(jnp.concatenate([top, bottom], axis=0), True)

    @pl.when(pl.program_id(0) == 1)
    def _():
        top = jnp.concatenate([upper_far[...], upper_rest[:, width:]], axis=1)
        add(jnp.concatenate([top, lower_rest[...]], axis=0), False)
        if not last:
            return
        inv_rms = jnp.sum(squares_ref[...], axis=1, keepdims=True) / model_width
        inv_rms = lax.rsqrt(inv_rms + EPSILON)
        gate_ref[...] = (total_ref[:, :inner] * inv_rms).astype(BF16)
        channels_ref[...] = (total_ref[:, inner:-LANES] * inv_rms).astype(BF16)
        steps_ref[...] = total_ref[:, -LANES:] * inv_rms


def both_heads(table, pair, head_size):
    rows = table.shape[0]
    lane = lax.broadcasted_iota(jnp.int32, (rows, 2 * head_size), 1)
    return jnp.where(
        lane < head_size, table[:, 2 * pair : 2 * pair + 1], table[:, 2 * pair + 1 : 2 * pair + 2]
    )


def over_states(row, heads, head_size):
    return jnp.concatenate(
        [jnp.broadcast_to(row[:, h : h + 1], (head_size, LANES)) for h in range(heads)], axis=0
    )


def conv_kernel(
    heads,
    unused,
    channels_ref,
    rim_ref,
    edges_ref,
    taps_ref,
    bias_ref,
    steps_ref,
    step_bias_ref,
    decay_ref,
    marks_ref,
    segment_ref,
    init_ref,
    x_ref,
    keys_ref,
    queries_ref,
    run_ref,
    less_ref,
    spread_ref,
    leaving_ref,
    gain_ref,
):
    del unused
    rows, inner = x_ref.shape
    state = keys_ref.shape[1]
    head_size = inner // heads
    taps = taps_ref.shape[0]
    channels = channels_ref[...]
    sources = jnp.concatenate([rim_ref[...], edges_ref[...]], axis=0)
    wide = channels.astype(F32)
    summed = bias_ref[...] + taps_ref[taps - 1 : taps] * wide
    column = lax.broadcasted_iota(jnp.int32, (rows, sources.shape[0]), 1)
    for back in range(1, taps):
        mark = marks_ref[:, back - 1 : back]
        pick = jnp.where(mark - rows == column, 1.0, 0.0).astype(BF16)
        value = jnp.dot(pick, sources, preferred_element_type=F32)
        value = value + jnp.where(mark < rows, 1.0, 0.0) * pltpu.roll(wide, back, 0)
        summed = summed + taps_ref[taps - 1 - back : taps - back] * value
    mixed = (summed / (1.0 + jnp.exp(-summed))).astype(BF16)
    x = mixed[:, :inner]
    keys = mixed[:, inner : inner + state]
    x_ref[...] = x
    keys_ref[...] = keys
    queries_ref[...] = mixed[:, inner + state :]
    raw = steps_ref[...] + step_bias_ref[...]
    step = jnp.maximum(raw, 0.0) + jnp.log1p(jnp.exp(-jnp.abs(raw)))
    log_decay = -jnp.exp(decay_ref[...]) * step
    segment = marks_ref[:, 4:5]
    same = segment == segment_ref[0:1, :]
    row = lax.broadcasted_iota(jnp.int32, (rows, rows), 0)
    other = lax.broadcasted_iota(jnp.int32, (rows, rows), 1)
    until = jnp.where(same & (other <= row), 1.0, 0.0).astype(BF16)
    after = jnp.where(same & (other > row), 1.0, 0.0).astype(BF16)
    lane = lax.broadcasted_iota(jnp.int32, log_decay.shape, 1)
    own = jnp.where(lane < heads, log_decay, 0.0)
    high = own.astype(BF16).astype(F32)
    middle = (own - high).astype(BF16).astype(F32)
    low = own - high - middle
    parts = high + pltpu.roll(middle, heads, 1) + pltpu.roll(low, 2 * heads, 1)
    parts = parts.astype(BF16)

    def summed_over(mask):
        sums = jnp.dot(mask, parts, preferred_element_type=F32)
        return (
            sums
            + pltpu.roll(sums, LANES - heads, 1)
            + pltpu.roll(sums, LANES - 2 * heads, 1)
        )

    run = summed_over(until)
    tail = summed_over(after)
    run_ref[...] = run
    less_ref[...] = (run - jnp.log(step)).T[:8]
    share = (jnp.exp(tail) * step).astype(BF16).astype(F32)
    spread = jnp.concatenate(
        [
            both_heads(share, p, head_size)
            * x[:, p * 2 * head_size : (p + 1) * 2 * head_size].astype(F32)
            for p in range(heads // 2)
        ],
        axis=1,
    )
    spread = spread.T.astype(BF16)
    spread_ref[...] = spread
    last = jnp.where(segment == segment[rows - 1 : rows], 1.0, 0.0)
    leaving = jnp.dot(spread, (keys.astype(F32) * last).astype(BF16), preferred_element_type=F32)
    gain = jnp.exp(run[rows - 1 : rows])
    carried = jnp.broadcast_to(marks_ref[rows - 1 : rows, 5:6], (heads * head_size, state)) > 0
    gain_wide = over_states(gain, heads, head_size)
    leaving_ref[...] = jnp.where(carried, leaving, leaving + gain_wide * init_ref[...])
    gain_ref[...] = jnp.where(carried, gain_wide, 0.0)


def scan_kernel(
    heads,
    block,
    unused,
    x_ref,
    keys_ref,
    queries_ref,
    run_ref,
    less_ref,
    marks_ref,
    segment_ref,
    table_ref,
    skip_ref,
    y_ref,
    masked_ref,
    begun_ref,
):
    del unused
    rows, inner = x_ref.shape
    head_size = inner // heads
    slots = table_ref.shape[1] // queries_ref.shape[1]
    queries = queries_ref[...].astype(F32)
    slot = marks_ref[:, 3:4]
    placed = jnp.concatenate(
        [(queries * jnp.where(slot == o, 1.0, 0.0)).astype(BF16) for o in range(slots)], axis=1
    )
    begun_ref[...] = lax.dot_general(
        placed, table_ref[...], ROWS_BY_ROWS, preferred_element_type=F32
    )
    blocks = [(t, s) for t in range(rows // block) for s in range(t + 1)]
    for at, (t, s) in enumerate(blocks):
        here, there = pl.ds(t * block, block), pl.ds(s * block, block)
        scores = lax.dot_general(
            queries_ref[here], keys_ref[there], ROWS_BY_ROWS, preferred_element_type=F32
        )
        same = marks_ref[here, 4:5] == segment_ref[0:1, there]
        if t == s:
            row = lax.broadcasted_iota(jnp.int32, (block, block), 0)
            other = lax.broadcasted_iota(jnp.int32, (block, block), 1)
            same = same & (other <= row)
        masked_ref[at] = jnp.where(same, scores, 0.0)
    grown = jnp.exp(run_ref[...])
    lane = lax.broadcasted_iota(jnp.int32, (block, 2 * head_size), 1)
    for p in range(heads // 2):
        wide = slice(p * 2 * head_size, (p + 1) * 2 * head_size)
        x = x_ref[:, wide].astype(F32)
        y = both_heads(grown, p, head_size) * begun_ref[:, wide] + both_heads(skip_ref[...], p, head_size) * x
        sums = [y[t * block : (t + 1) * block] for t in range(rows // block)]
        for at, (t, s) in enumerate(blocks):
            here, there = slice(t * block, (t + 1) * block), slice(s * block, (s + 1) * block)
            for side in range(2):
                head = 2 * p + side
                mine = (lane < head_size) if side == 0 else (lane >= head_size)
                x_own = jnp.where(mine, x[there], 0.0).astype(BF16)
                gap = run_ref[here, head : head + 1] - less_ref[head : head + 1, there]
                weight = (masked_ref[at] * jnp.exp(jnp.minimum(gap, 80.0))).astype(BF16)
                sums[t] = sums[t] + jnp.dot(weight, x_own, preferred_element_type=F32)
        for t in range(rows // block):
            y_ref[t * block : (t + 1) * block, wide] = sums[t]


def gate_kernel(
    heads, unused, y_ref, queries_ref, run_ref, marks_ref, entry_ref, gate_ref, gain_ref, out_ref, sq_ref
):
    del unused
    rows, inner = y_ref.shape
    head_size = inner // heads
    carried = jnp.where(marks_ref[:, 5:6] > 0, 1.0, 0.0)
    queries = (queries_ref[...].astype(F32) * carried).astype(BF16)
    held = lax.dot_general(
        queries, entry_ref[...].astype(BF16), ROWS_BY_ROWS, preferred_element_type=F32
    )
    grown = jnp.exp(run_ref[...])
    grown = jnp.concatenate([both_heads(grown, p, head_size) for p in range(heads // 2)], axis=1)
    gate = gate_ref[...].astype(F32)
    gated = (y_ref[...] + grown * held) * (gate / (1.0 + jnp.exp(-gate)))
    out_ref[...] = (gated * gain_ref[...]).astype(BF16)
    square = jnp.sum(gated * gated, axis=1, keepdims=True)
    sq_ref[...] = jnp.broadcast_to(square, (rows, LANES)).T[:8]


def norm_scale(own_ref, other_ref, channels):
    scale = lax.rsqrt((own_ref[0:1] + other_ref[0:1]) / channels + EPSILON)
    return jnp.broadcast_to(scale, (LANES, scale.shape[1])).T


def out_kernel(width, count, scaled, blocks, gated_ref, own_ref, other_ref, chooser_ref, *refs):
    del blocks
    weights, outs = refs[: 4 * count], refs[4 * count :]
    upper_out, upper_in, lower_out, lower_in, ends_ref = outs
    rows, inner = gated_ref.shape
    half = rows // 2
    if scaled:
        scale = norm_scale(own_ref, other_ref, 2 * inner)
        scale = jnp.concatenate([scale] * (width // LANES), axis=1)
    else:
        scale = jnp.ones((rows, width), F32)
    gated = gated_ref[...]
    end_rows = jnp.dot(chooser_ref[...], gated, preferred_element_type=F32).astype(BF16)
    end_scale = jnp.dot(
        chooser_ref[...].astype(F32), scale, precision=HIGHEST, preferred_element_type=F32
    )
    for at, w in enumerate(weights):
        index, place = divmod(at, count)
        part = jnp.dot(gated, w[...], preferred_element_type=F32) * scale
        top, bottom = part[:half], part[half:]
        low = (index // 2) * count + place
        target = upper_out if index % 2 else upper_in
        target[:, low * width : (low + 1) * width] = top.astype(target.dtype)
        low = (index % 2) * count + place
        target = lower_out if index // 2 else lower_in
        target[:, low * width : (low + 1) * width] = bottom.astype(target.dtype)
        ends_ref[:, at * width : (at + 1) * width] = (
            jnp.dot(end_rows, w[...], preferred_element_type=F32) * end_scale
        )


def near_kernel(unused, upper_ref, upper_got, lower_ref, lower_got, *outs):
    del unused
    for kept, got, keep_ref, send_ref in (
        (upper_ref, upper_got, outs[0], outs[1]),
        (lower_ref, lower_got, outs[2], outs[3]),
    ):
        wide = keep_ref.shape[1]
        keep_ref[...] = kept[:, :wide].astype(F32) + got[:, :wide].astype(F32)
        send_ref[...] = (kept[:, wide:].astype(F32) + got[:, wide:].astype(F32)).astype(BF16)


def plane_kernel(unused, upper_ref, upper_got, lower_ref, lower_got, *outs):
    del unused
    half, width = upper_ref.shape[0], outs[0].shape[1]
    for at, out_ref in enumerate(outs):
        wide = slice(at * width, (at + 1) * width)
        upper = upper_ref[:, wide] + upper_got[:, wide].astype(F32)
        lower = lower_ref[:, wide] + lower_got[:, wide].astype(F32)
        out_ref[:half] = upper.astype(out_ref.dtype)
        out_ref[half:] = lower.astype(out_ref.dtype)


def hidden_kernel(unused, tokens_ref, own_ref, *refs):
    del unused
    total = own_ref[...]
    for part in refs[:-1]:
        total = total + part[...].astype(F32)
    refs[-1][...] = (tokens_ref[...].astype(F32) + total).astype(BF16)


def scale_kernel(unused, own_ref, other_ref, chooser_ref, channels_ref, *refs):
    del unused
    raw, outs = refs[:5], refs[5:]
    half = raw[0].shape[0]
    scale = norm_scale(own_ref, other_ref, 2 * channels_ref.shape[1])
    end_scale = jnp.dot(
        chooser_ref[...].astype(F32), scale, precision=HIGHEST, preferred_element_type=F32
    )
    for at, (source, out_ref) in enumerate(zip(raw, outs)):
        factor = end_scale if at == 4 else scale[:half] if at < 2 else scale[half:]
        for lane in range(0, source.shape[1], LANES):
            value = source[:, lane : lane + LANES] * factor
            out_ref[:, lane : lane + LANES] = value.astype(out_ref.dtype)


def ends_kernel(width, col_size, sum_groups, gather_groups, place, *refs):
    sources, outs = refs[:-2], refs[-2:]
    groups = [(shifts, outs[0]) for shifts in sum_groups]
    groups += [(shifts, outs[1]) for shifts in gather_groups]
    for source, (shifts, out_ref) in zip(sources, groups):
        for at in range(source.shape[1] // width):
            block = block_of(shifts, at, place, col_size)
            to = pl.ds(pl.multiple_of(block * width, width), width)
            out_ref[:, to] = source[:, at * width : (at + 1) * width]


def finals_kernel(
    heads, added, first, spread_ref, keys_ref, marks_ref, ends_ref, entry_ref, init_ref, _, *refs
):
    out_ref = refs[-1]
    count, inner, state = out_ref.shape
    head_size = inner // heads
    slot = (first[0] + pl.program_id(0)) * count
    keys = keys_ref[...].astype(F32)
    owner = marks_ref[:, 6:7]
    mine = [
        (keys * jnp.where(owner == slot + i, ends_ref[i, :, heads : heads + 1], 0.0)).astype(BF16)
        for i in range(count)
    ]
    states = jnp.dot(
        spread_ref[...], jnp.concatenate(mine, axis=1), preferred_element_type=F32
    )
    for i in range(count):
        gain = over_states(ends_ref[i], heads, head_size)
        carried = jnp.broadcast_to(ends_ref[i, :, heads + 1 : heads + 2], (inner, state)) > 0.5
        value = states[:, i * state : (i + 1) * state]
        value = value + gain * jnp.where(carried, entry_ref[...], init_ref[i])
        out_ref[i] = value + refs[0][i] if added else value


def per_device(
    tokens,
    lengths,
    deal,
    pre_gain,
    w_inner,
    w_group,
    w_step,
    conv_inner,
    conv_group,
    conv_bias_inner,
    conv_bias_group,
    edge_inner,
    edge_group,
    init_states,
    step_bias,
    decay_log,
    skip,
    inner_gain,
    w_out,
    final_gain,
    w_head,
):
    rows, width = tokens.shape
    model_width = pre_gain.shape[0]
    requests = lengths.shape[0]
    taps = conv_inner.shape[0]
    inner = w_inner.shape[2]
    heads = w_step.shape[1]
    head_size = inner // heads
    state = w_group.shape[3]
    row_at, col_at, seq_at = (lax.axis_index(name) for name in ("row", "col", "seq"))
    row_size, col_size, seq_size = (lax.axis_size(name) for name in ("row", "col", "seq"))
    group_local = col_at * w_group.shape[2] // col_size

    def own_group(table, axis):
        return lax.dynamic_index_in_dim(table, group_local, axis, keepdims=False)

    def in_lanes(values):
        return jnp.pad(values, (0, LANES - heads))[None, :]

    first_row = seq_at * rows
    counts = jnp.concatenate([lengths, deal, jnp.reshape(first_row, (1,)).astype(jnp.int32)])
    marks, segment_row, chooser, slots = call(
        functools.partial(setup_kernel, taps),
        [
            ((rows, LANES), jnp.int32),
            ((8, rows), jnp.int32),
            ((requests, rows), BF16),
            ((requests, 2 * LANES), F32),
        ],
        prefetch=counts,
        vmem=4,
        work=0,
    )
    place = jnp.stack([row_at, col_at, group_local]).astype(jnp.int32)

    init_flat = jnp.reshape(init_states, (requests, inner, state))
    skip_row = in_lanes(skip)
    gains = pre_gain[None, :]

    gather_groups = ((0,1),(2,3))
    sum_groups = ((2,3),(0,1))

    n_all = 2 * inner + 2 * state + LANES
    steps_across = jnp.transpose(w_step)

    def weights_of(shifts, gain_row):
        count = row_size * len(shifts)
        parts = count // 2

        def specs(shape, where):
            return [
                pl.BlockSpec(shape, lambda i, p, at=at: where(
                    block_of(shifts, i * parts + at, p, col_size)
                ))
                for at in range(parts)
            ]

        return call(
            functools.partial(weights_kernel, parts),
            [((count * width, n_all), BF16), ((1, count * width), F32)],
            *[w_inner] * parts,
            *[w_group] * parts,
            *[steps_across] * parts,
            *[gain_row] * parts,
            prefetch=place,
            grid=(count // parts,),
            in_specs=specs((width,) + w_inner.shape[1:], lambda b: (b, 0, 0))
            + specs((width,) + w_group.shape[1:], lambda b: (b, 0, 0, 0))
            + specs((heads, width), lambda b: (0, b))
            + specs((1, width), lambda b: (0, b)),
            out_specs=[
                pl.BlockSpec((parts * width, n_all), lambda i, p: (i, 0)),
                pl.BlockSpec((1, parts * width), lambda i, p: (0, i)),
            ],
            vmem=58,
        )

    gain_row = pre_gain[None, :]
    token_blocks = {0: tokens}
    token_blocks[1] = from_ahead(tokens, "col", 1)
    later = after(tokens, token_blocks[1])
    for shift in range(2, col_size):
        source = token_blocks[1] if shift == 2 else later
        token_blocks[shift] = from_ahead(source, "col", 1 if shift == 2 else shift)
    gain_row = after(gain_row, token_blocks[1])
    token_ends = []
    carry = ()
    ready = ()
    for shifts in gather_groups:
        first, last = shifts == gather_groups[0], shifts == gather_groups[-1]
        pieces = plane_gather(jnp.concatenate([token_blocks[i] for i in shifts], axis=1))
        weights, gains = weights_of(shifts, after(gain_row, *ready) if ready else gain_row)
        ready = (pieces[1],)
        count = row_size * len(shifts)
        depth = count * width // 2
        outs = [((requests, count * width), F32)]
        totals = [((rows, n_all), F32), ((rows, LANES), F32)]
        if not last:
            outs += totals
        else:
            outs += [((rows, inner), BF16), ((rows, inner + 2 * state), BF16), ((rows, LANES), F32)]
        piece_ends, *carry = call(
            functools.partial(project_kernel, first, last, inner, model_width),
            outs,
            *pieces,
            chooser,
            gains,
            weights,
            *carry,
            grid=(2,),
            in_specs=[None] * 7
            + [
                pl.BlockSpec((1, depth), lambda i, _: (0, i)),
                pl.BlockSpec((depth, n_all), lambda i, _: (i, 0)),
            ]
            + [None] * len(carry),
            out_specs=[pl.BlockSpec((requests, depth), lambda i, _: (0, i))]
            + [None] * (len(outs) - 1),
            scratch=totals if last else [],
            vmem=24,
        )
        token_ends.append(piece_ends)
    gate_in, channels, step_raw = carry
    ready = gains

    init_last = lax.dynamic_index_in_dim(init_flat, after(marks, ready)[rows - 1, 6], 0, keepdims=False)
    (table,) = call(
        table_kernel,
        [((inner, requests * state), BF16)],
        after(init_flat, ready),
        grid=(requests,),
        in_specs=[pl.BlockSpec((1, inner, state), lambda i, _: (i, 0, 0))],
        out_specs=[pl.BlockSpec((inner, state), lambda i, _: (0, i))],
        vmem=4,
        work=0,
    )
    conv_taps = jnp.concatenate(
        [conv_inner, jnp.reshape(own_group(after(conv_group, ready), 2), (taps, 2 * state))], axis=1
    )
    conv_bias = jnp.concatenate(
        [conv_bias_inner, jnp.reshape(own_group(after(conv_bias_group, ready), 1), (2 * state,))]
    )[None, :]
    edges = jnp.concatenate(
        [after(edge_inner, ready), jnp.reshape(own_group(after(edge_group, ready), 3), (requests, taps - 1, 2 * state))],
        axis=2,
    )
    edges = jnp.reshape(edges, (requests * (taps - 1), inner + 2 * state))

    rim = from_behind(channels[rows - RIM :], "seq", 1)
    x, keys, queries, run, less, spread, leaving, gain_carried = call(
        functools.partial(conv_kernel, heads),
        [
            ((rows, inner), BF16),
            ((rows, state), BF16),
            ((rows, state), BF16),
            ((rows, LANES), F32),
            ((8, rows), F32),
            ((inner, rows), BF16),
            ((inner, state), F32),
            ((inner, state), F32),
        ],
        channels,
        rim,
        edges,
        conv_taps,
        conv_bias,
        step_raw,
        in_lanes(step_bias),
        in_lanes(decay_log),
        after(marks, table),
        segment_row,
        init_last,
    )
    entry = from_behind(leaving, "seq", 1)
    for _ in range(seq_size - 2):
        entry = from_behind(gain_carried * entry + leaving, "seq", 1)

    block = 256
    pairs = (rows // block) * (rows // block + 1) // 2
    y = pl.pallas_call(
        functools.partial(scan_kernel, heads, block),
        out_shape=jax.ShapeDtypeStruct((rows, inner), F32),
        grid_spec=pltpu.PrefetchScalarGridSpec(
            num_scalar_prefetch=1,
            grid=(1,),
            in_specs=[
                pl.BlockSpec(a.shape, lambda *_: (0, 0))
                for a in (x, keys, queries, run, less, marks, segment_row, table, skip_row)
            ],
            out_specs=pl.BlockSpec((rows, inner), lambda *_: (0, 0)),
            scratch_shapes=[
                pltpu.VMEM((pairs, block, block), F32),
                pltpu.VMEM((rows, inner), F32),
            ],
        ),
        compiler_params=pltpu.CompilerParams(vmem_limit_bytes=16 * MIB),
    )(
        jnp.zeros((1,), jnp.int32),
        x,
        keys,
        queries,
        run,
        less,
        marks,
        segment_row,
        table,
        skip_row,
    )
    gated, own_squares = call(
        functools.partial(gate_kernel, heads),
        [((rows, inner), BF16), ((8, rows), F32)],
        y,
        queries,
        run,
        marks,
        entry,
        gate_in,
        inner_gain[None, :],
    )
    other_squares = from_partner(own_squares, "col", 0)

    half_out, got = [], []
    for shifts in sum_groups:
        count = len(shifts)
        first = shifts == sum_groups[0]
        side = (rows // 2, 2 * count * width)
        kinds = [BF16] * 4
        ends_out = ((requests, row_size * count * width), F32)
        outs = call(
            functools.partial(out_kernel, width, count, not first),
            [(side, F32 if first else kind) for kind in kinds] + [ends_out],
            gated,
            own_squares,
            own_squares if first else other_squares,
            chooser,
            *[w_out] * (row_size * count),
            prefetch=place,
            in_specs=[None] * 4
            + [
                pl.BlockSpec(
                    (inner, width),
                    lambda i, p, at=at, shifts=shifts: (0, block_of(shifts, at, p, col_size)),
                )
                for at in range(row_size * count)
            ],
            vmem=16,
            work=10 if first else 0,
        )
        if first:
            other_squares = after(other_squares, outs[0])
            outs = call(
                scale_kernel,
                [(side, kind) for kind in kinds] + [ends_out],
                own_squares,
                other_squares,
                chooser,
                gated,
                *outs,
                vmem=12,
                work=0,
            )
        half_out.append(outs)
        got.append((from_partner(outs[0], "row", 0), from_partner(outs[2], "row", 1)))
    end_sum, end_tokens = call(
        functools.partial(ends_kernel, width, col_size, sum_groups, gather_groups),
        [((requests, model_width), F32)] * 2,
        after(half_out[0][4], *got[0]),
        *[outs[4] for outs in half_out[1:]],
        *token_ends,
        prefetch=place,
        vmem=4,
        work=0,
    )
    for axis, bit in (("col", 0), ("col", 1), ("row", 0), ("row", 1)):
        end_sum = end_sum + from_partner(end_sum.astype(BF16), axis, bit).astype(F32)

    def finals_after(far_ready):
        end_run = jnp.dot(chooser.astype(F32), run, precision=HIGHEST)[:, :heads]
        ends_here = slots[:, :1]
        end_marks = jnp.concatenate(
            [
                jnp.exp(end_run) * ends_here,
                ends_here,
                slots[:, LANES : LANES + 1],
                jnp.zeros((requests, LANES - heads - 2), F32),
            ],
            axis=1,
        )[:, None, :]

        kept = requests // seq_size

        def finals_of(first, steps, ready, extra):
            count = steps * kept
            by_slot = pl.BlockSpec((kept, inner, state), lambda i, s: (s[0] + i, 0, 0))
            by_step = pl.BlockSpec((kept, inner, state), lambda i, s: (i, 0, 0))
            return call(
                functools.partial(finals_kernel, heads, bool(extra)),
                [((count, inner, state), F32)],
                spread,
                keys,
                marks,
                end_marks,
                entry,
                init_flat,
                after(half_out[1][4], *ready),
                *extra,
                prefetch=jnp.reshape(first, (1,)).astype(jnp.int32),
                grid=(steps,),
                in_specs=[None] * 3
                + [pl.BlockSpec((kept, 1, LANES), lambda i, s: (s[0] + i, 0, 0)), None, by_slot]
                + [pl.BlockSpec(memory_space=pl.ANY)]
                + [by_step] * len(extra),
                out_specs=[by_step],
                vmem=20,
                work=0,
            )[0]

        if seq_size == 2:
            lent = finals_of(1 - seq_at, 1, far_ready, [])
            finals = finals_of(seq_at, 1, (), [from_partner(lent, "seq", 0)])
        else:
            finals = lax.psum_scatter(
                finals_of(jnp.int32(0), seq_size, (), []), "seq", scatter_dimension=0, tiled=True
            )
        return finals

    pieces = {}
    for shifts, outs, (upper_got, lower_got) in zip(sum_groups, half_out, got):
        _, upper_in, _, lower_in, _ = outs
        wide = len(shifts) * width
        upper, upper_far, lower, lower_near = call(
            near_kernel,
            [((rows // 2, wide), F32), ((rows // 2, wide), BF16)] * 2,
            upper_in,
            upper_got,
            lower_in,
            lower_got,
            vmem=8,
            work=10,
        )
        upper_far = from_partner(upper_far, "row", 1)
        lower_near = from_partner(lower_near, "row", 0)
        sums = call(
            plane_kernel,
            [((rows, width), BF16 if shift else F32) for shift in shifts],
            upper,
            upper_far,
            lower,
            lower_near,
            vmem=8,
            work=10,
        )
        if shifts == sum_groups[-2]:
            far_ready = sums
        for shift, part in zip(shifts, sums):
            pieces[shift] = from_ahead(part, "col", col_size - shift) if shift else part
    finals = finals_after(far_ready)
    if seq_size == 2:
        ending = after(end_tokens + end_sum, finals)
        ending = ending + from_partner(ending, "seq", 0)
    else:
        ending = lax.psum(end_tokens + end_sum, "seq")
    (hidden_out,) = call(
        hidden_kernel,
        [((rows, width), BF16)],
        tokens,
        *[pieces[shift] for shift in range(col_size)],
        vmem=4,
        work=30,
    )

    last_rows = ending.astype(BF16).astype(F32)
    final_scale = lax.rsqrt(jnp.sum(last_rows * last_rows, axis=1) / model_width + EPSILON)
    head_in = (last_rows * final_scale[:, None] * final_gain).astype(BF16)
    logits = jnp.dot(head_in, w_head, preferred_element_type=F32)

    final_states = jnp.reshape(finals, (finals.shape[0], heads, head_size, state))
    return (hidden_out, final_states, logits)


def solution(mesh):
    in_specs = (
        P("seq", ("row", "col")),
        P(),
        P(),
        P(),
        P(None, None, ("row", "col")),
        P(None, None, "row", None),
        P(None, ("row", "col")),
        P(None, ("row", "col")),
        P(None, None, "row", None),
        P(("row", "col")),
        P(None, "row", None),
        P(None, None, ("row", "col")),
        P(None, None, None, "row", None),
        P(None, ("row", "col"), None, None),
        P(("row", "col")),
        P(("row", "col")),
        P(("row", "col")),
        P(("row", "col")),
        P(("row", "col"), None),
        P(),
        P(None, ("seq", "row", "col")),
    )
    out_specs = (
        P("seq", ("row", "col")),
        P("seq", ("row", "col"), None, None),
        P(None, ("seq", "row", "col")),
    )
    return jax.shard_map(
        per_device, mesh=mesh, in_specs=in_specs, out_specs=out_specs, check_vma=False
    )
```

```python
import functools

import jax
import jax.numpy as jnp
from jax import lax
from jax.experimental import pallas as pl
from jax.experimental.pallas import tpu as pltpu
from jax.sharding import PartitionSpec as P

EPSILON = 1e-05
HIGHEST = lax.Precision.HIGHEST
F32 = jnp.float32
BF16 = jnp.bfloat16
LANES = 128
RIM = 16
MIB = 1024 * 1024
ROWS_BY_ROWS = (((1,), (1,)), ((), ()))


def from_behind(block, axis, distance):
    devices = range(lax.axis_size(axis))
    route = [(i - distance, i) for i in devices if i - distance in devices]
    return lax.ppermute(block, axis, route)


def from_partner(x, axis, bit):
    return lax.ppermute(x, axis, [(i, i ^ 1 << bit) for i in range(lax.axis_size(axis))])


def from_ahead(x, axis, distance):
    size = lax.axis_size(axis)
    return lax.ppermute(x, axis, [((i + distance) % size, i) for i in range(size)])


def after(x, *others):
    return lax.optimization_barrier((x,) + others)[0]


def call(kernel, outs, *args, prefetch=None, grid=(1,), in_specs=None, out_specs=None, scratch=(), vmem=12, work=20):
    params = pltpu.CompilerParams(vmem_limit_bytes=vmem * MIB)
    shapes = [jax.ShapeDtypeStruct(shape, kind) for shape, kind in outs]

    def whole(shape):
        zeros = (0,) * len(shape)
        return pl.BlockSpec(shape, lambda *_: zeros)

    specs = [
        whole(a.shape) if spec is None else spec
        for a, spec in zip(args, in_specs or [None] * len(args))
    ]
    gives = [
        whole(shape) if spec is None else spec
        for (shape, _), spec in zip(outs, out_specs or [None] * len(outs))
    ]
    prefetch = jnp.zeros((1,), jnp.int32) if prefetch is None else prefetch
    spec = pltpu.PrefetchScalarGridSpec(
        num_scalar_prefetch=1, grid=grid, in_specs=specs, out_specs=gives,
        scratch_shapes=[pltpu.VMEM(shape, kind) for shape, kind in scratch],
    )
    return pl.pallas_call(
        kernel,
        out_shape=shapes,
        grid_spec=spec,
        compiler_params=params,
        cost_estimate=pl.CostEstimate(flops=work * 1_000_000_000, bytes_accessed=100_000_000 if work else 1000, transcendentals=0),
    )(prefetch, *args)


def plane_gather(block):
    half = block.shape[0] // 2
    upper, lower = block[:half], block[half:]
    upper_far = from_partner(upper, "row", 1)
    lower_near = from_partner(lower, "row", 0)
    upper_rest = from_partner(jnp.concatenate([upper, upper_far], axis=1), "row", 0)
    lower_rest = from_partner(jnp.concatenate([lower, lower_near], axis=1), "row", 1)
    return upper, upper_far, upper_rest, lower, lower_near, lower_rest


def block_of(shifts, at, place, col_size):
    gap = shifts[-1] - shifts[0] if len(shifts) > 1 else 0
    shift = shifts[0] + (at % len(shifts)) * gap
    return (place[0] ^ (at // len(shifts))) * col_size + (place[1] + shift) % col_size


def setup_kernel(taps, counts, marks_ref, segment_ref, chooser_ref, slots_ref):
    requests = chooser_ref.shape[0]
    rows = marks_ref.shape[0]
    first_row = counts[2 * requests]
    begins, owners = [], []
    total = jnp.int32(0)
    for k in range(requests):
        begins.append(total - first_row)
        owners.append(counts[requests + k])
        total = total + counts[k]
    stops = begins[1:] + [total - first_row]

    def latest(position, values):
        found = jnp.full(position.shape, values[0], jnp.int32)
        for begin, value in zip(begins[1:], values[1:]):
            found = jnp.where(position >= begin, value, found)
        return found

    position = lax.broadcasted_iota(jnp.int32, (rows, LANES), 0)
    lane = lax.broadcasted_iota(jnp.int32, (rows, LANES), 1)
    owner = latest(position, owners)
    begin = latest(position, begins)
    offset = position - begin
    marks = owner
    for back in range(1, taps):
        edge = rows + RIM + owner * (taps - 1) + (taps - 1 - back) + offset
        inside = jnp.where(position >= back, position - back, rows + RIM + position - back)
        marks = jnp.where(lane == back - 1, jnp.where(offset >= back, inside, edge), marks)
    marks = jnp.where((lane == 3) & (begin < 0), requests, marks)
    marks = jnp.where(lane == 4, begin, marks)
    marks = jnp.where(lane == 5, jnp.where(begin < 0, 1, 0), marks)
    marks_ref[...] = marks
    across = lax.broadcasted_iota(jnp.int32, (8, rows), 1)
    segment_ref[...] = latest(across, begins)
    slot = lax.broadcasted_iota(jnp.int32, (requests, rows), 0)
    column = lax.broadcasted_iota(jnp.int32, (requests, rows), 1)
    slot_lane = lax.broadcasted_iota(jnp.int32, (requests, LANES), 0)
    chooser = jnp.zeros((requests, rows), F32)
    slot_begin = jnp.zeros((requests, LANES), F32)
    slot_end = jnp.zeros((requests, LANES), F32)
    for k in range(requests):
        last = stops[k] - 1
        chooser = jnp.where((slot == owners[k]) & (column == last), 1.0, chooser)
        here = jnp.where((last >= 0) & (last < rows), 1.0, 0.0)
        slot_end = jnp.where(slot_lane == owners[k], here, slot_end)
        before = jnp.where(begins[k] < 0, 1.0, 0.0)
        slot_begin = jnp.where(slot_lane == owners[k], before, slot_begin)
    chooser_ref[...] = chooser.astype(BF16)
    slots_ref[:, :LANES] = slot_end
    slots_ref[:, LANES:] = slot_begin


def weights_kernel(parts, place, *refs):
    out_ref, gain_out = refs[4 * parts :]
    rows = refs[0].shape[0]
    for part in range(parts):
        main_ref, group_ref, step_ref, gain_ref = refs[part : 4 * parts : parts]
        weights_block(
            place[2],
            main_ref,
            group_ref,
            step_ref,
            out_ref.at[pl.ds(part * rows, rows)],
        )
        gain_out[:, part * rows : (part + 1) * rows] = gain_ref[...]


def weights_block(group, main_ref, group_ref, step_ref, out_ref):
    rows, _, inner = main_ref.shape
    state = group_ref.shape[3]
    heads = step_ref.shape[0]
    half = rows // 2
    row = lax.broadcasted_iota(jnp.int32, (rows, rows), 0)
    column = lax.broadcasted_iota(jnp.int32, (rows, rows), 1)
    source = jnp.where(row < half, 2 * row, 2 * (row - half) + 1)
    pick = jnp.where(source == column, 1.0, 0.0).astype(BF16)
    flat = main_ref[...].reshape(2 * rows, inner)
    for at in range(2):
        got = jnp.dot(pick, flat[at * rows : (at + 1) * rows], preferred_element_type=F32)
        got = got.astype(BF16)
        out_ref[at * half : (at + 1) * half, :inner] = got[:half]
        out_ref[at * half : (at + 1) * half, inner : 2 * inner] = got[half:]
    take = rows // 4
    row, column = row[:half], column[:half]
    source = jnp.where(row < take, 4 * row, 4 * (row - take) + 2) + group
    pick = jnp.where(source == column, 1.0, 0.0).astype(BF16)
    flat = group_ref[...].reshape(4 * rows, state)
    for at in range(4):
        got = jnp.dot(pick, flat[at * rows : (at + 1) * rows], preferred_element_type=F32)
        got = got.astype(BF16)
        out_ref[at * take : (at + 1) * take, 2 * inner : 2 * inner + state] = got[:take]
        out_ref[at * take : (at + 1) * take, 2 * inner + state : 2 * inner + 2 * state] = got[take:]
    steps = jnp.concatenate(
        [step_ref[...].astype(F32), jnp.zeros((LANES - heads, rows), F32)], axis=0
    )
    out_ref[:, 2 * inner + 2 * state :] = steps.T.astype(BF16)


def table_kernel(unused, init_ref, out_ref):
    del unused
    out_ref[...] = init_ref[0].astype(BF16)


def project_kernel(first, last, inner, model_width, unused, *refs):
    del unused
    pieces, refs = refs[:6], refs[6:]
    chooser_ref, gain_ref, weights_ref, refs = refs[0], refs[1], refs[2], refs[3:]
    if not first:
        total_in, squares_in, refs = refs[0], refs[1], refs[2:]
    if not last:
        ends_ref, total_ref, squares_ref = refs
    else:
        ends_ref, gate_ref, channels_ref, steps_ref, total_ref, squares_ref = refs
    width = pieces[0].shape[1]

    def add(raw, fresh):
        ends_ref[...] = jnp.dot(chooser_ref[...], raw, preferred_element_type=F32)
        wide = raw.astype(F32)
        scaled = (wide * gain_ref[...]).astype(BF16)
        product = jnp.dot(scaled, weights_ref[...], preferred_element_type=F32)
        square = wide * wide
        parts = [square[:, at : at + LANES] for at in range(0, 2 * width, LANES)]
        if fresh:
            total_ref[...] = product if first else product + total_in[...]
            squares_ref[...] = functools.reduce(jnp.add, parts if first else parts + [squares_in[...]])
        else:
            total_ref[...] += product
            squares_ref[...] += functools.reduce(jnp.add, parts)

    upper, upper_far, upper_rest, lower, lower_near, lower_rest = pieces

    @pl.when(pl.program_id(0) == 0)
    def _():
        top = jnp.concatenate([upper[...], upper_rest[:, :width]], axis=1)
        bottom = jnp.concatenate([lower[...], lower_near[...]], axis=1)
        add(jnp.concatenate([top, bottom], axis=0), True)

    @pl.when(pl.program_id(0) == 1)
    def _():
        top = jnp.concatenate([upper_far[...], upper_rest[:, width:]], axis=1)
        add(jnp.concatenate([top, lower_rest[...]], axis=0), False)
        if not last:
            return
        inv_rms = jnp.sum(squares_ref[...], axis=1, keepdims=True) / model_width
        inv_rms = lax.rsqrt(inv_rms + EPSILON)
        gate_ref[...] = (total_ref[:, :inner] * inv_rms).astype(BF16)
        channels_ref[...] = (total_ref[:, inner:-LANES] * inv_rms).astype(BF16)
        steps_ref[...] = total_ref[:, -LANES:] * inv_rms


def both_heads(table, pair, head_size):
    rows = table.shape[0]
    lane = lax.broadcasted_iota(jnp.int32, (rows, 2 * head_size), 1)
    return jnp.where(
        lane < head_size, table[:, 2 * pair : 2 * pair + 1], table[:, 2 * pair + 1 : 2 * pair + 2]
    )


def over_states(row, heads, head_size):
    return jnp.concatenate(
        [jnp.broadcast_to(row[:, h : h + 1], (head_size, LANES)) for h in range(heads)], axis=0
    )


def conv_kernel(
    heads,
    unused,
    channels_ref,
    rim_ref,
    edges_ref,
    taps_ref,
    bias_ref,
    steps_ref,
    step_bias_ref,
    decay_ref,
    marks_ref,
    segment_ref,
    init_ref,
    x_ref,
    keys_ref,
    queries_ref,
    run_ref,
    less_ref,
    spread_ref,
    leaving_ref,
    gain_ref,
):
    del unused
    rows, inner = x_ref.shape
    state = keys_ref.shape[1]
    head_size = inner // heads
    taps = taps_ref.shape[0]
    channels = channels_ref[...]
    sources = jnp.concatenate([rim_ref[...], edges_ref[...]], axis=0)
    wide = channels.astype(F32)
    summed = bias_ref[...] + taps_ref[taps - 1 : taps] * wide
    column = lax.broadcasted_iota(jnp.int32, (rows, sources.shape[0]), 1)
    for back in range(1, taps):
        mark = marks_ref[:, back - 1 : back]
        pick = jnp.where(mark - rows == column, 1.0, 0.0).astype(BF16)
        value = jnp.dot(pick, sources, preferred_element_type=F32)
        value = value + jnp.where(mark < rows, 1.0, 0.0) * pltpu.roll(wide, back, 0)
        summed = summed + taps_ref[taps - 1 - back : taps - back] * value
    mixed = (summed / (1.0 + jnp.exp(-summed))).astype(BF16)
    x = mixed[:, :inner]
    keys = mixed[:, inner : inner + state]
    x_ref[...] = x
    keys_ref[...] = keys
    queries_ref[...] = mixed[:, inner + state :]
    raw = steps_ref[...] + step_bias_ref[...]
    step = jnp.maximum(raw, 0.0) + jnp.log1p(jnp.exp(-jnp.abs(raw)))
    log_decay = -jnp.exp(decay_ref[...]) * step
    segment = marks_ref[:, 4:5]
    same = segment == segment_ref[0:1, :]
    row = lax.broadcasted_iota(jnp.int32, (rows, rows), 0)
    other = lax.broadcasted_iota(jnp.int32, (rows, rows), 1)
    until = jnp.where(same & (other <= row), 1.0, 0.0).astype(BF16)
    after = jnp.where(same & (other > row), 1.0, 0.0).astype(BF16)
    lane = lax.broadcasted_iota(jnp.int32, log_decay.shape, 1)
    own = jnp.where(lane < heads, log_decay, 0.0)
    high = own.astype(BF16).astype(F32)
    middle = (own - high).astype(BF16).astype(F32)
    low = own - high - middle
    parts = high + pltpu.roll(middle, heads, 1) + pltpu.roll(low, 2 * heads, 1)
    parts = parts.astype(BF16)

    def summed_over(mask):
        sums = jnp.dot(mask, parts, preferred_element_type=F32)
        return (
            sums
            + pltpu.roll(sums, LANES - heads, 1)
            + pltpu.roll(sums, LANES - 2 * heads, 1)
        )

    run = summed_over(until)
    tail = summed_over(after)
    run_ref[...] = run
    less_ref[...] = (run - jnp.log(step)).T[:8]
    share = (jnp.exp(tail) * step).astype(BF16).astype(F32)
    spread = jnp.concatenate(
        [
            both_heads(share, p, head_size)
            * x[:, p * 2 * head_size : (p + 1) * 2 * head_size].astype(F32)
            for p in range(heads // 2)
        ],
        axis=1,
    )
    spread = spread.T.astype(BF16)
    spread_ref[...] = spread
    last = jnp.where(segment == segment[rows - 1 : rows], 1.0, 0.0)
    leaving = jnp.dot(spread, (keys.astype(F32) * last).astype(BF16), preferred_element_type=F32)
    gain = jnp.exp(run[rows - 1 : rows])
    carried = jnp.broadcast_to(marks_ref[rows - 1 : rows, 5:6], (heads * head_size, state)) > 0
    gain_wide = over_states(gain, heads, head_size)
    leaving_ref[...] = jnp.where(carried, leaving, leaving + gain_wide * init_ref[...])
    gain_ref[...] = jnp.where(carried, gain_wide, 0.0)


def scan_kernel(
    heads,
    block,
    unused,
    x_ref,
    keys_ref,
    queries_ref,
    run_ref,
    less_ref,
    marks_ref,
    segment_ref,
    table_ref,
    skip_ref,
    y_ref,
    masked_ref,
    begun_ref,
):
    del unused
    rows, inner = x_ref.shape
    head_size = inner // heads
    slots = table_ref.shape[1] // queries_ref.shape[1]
    queries = queries_ref[...].astype(F32)
    slot = marks_ref[:, 3:4]
    placed = jnp.concatenate(
        [(queries * jnp.where(slot == o, 1.0, 0.0)).astype(BF16) for o in range(slots)], axis=1
    )
    begun_ref[...] = lax.dot_general(
        placed, table_ref[...], ROWS_BY_ROWS, preferred_element_type=F32
    )
    blocks = [(t, s) for t in range(rows // block) for s in range(t + 1)]
    for at, (t, s) in enumerate(blocks):
        here, there = pl.ds(t * block, block), pl.ds(s * block, block)
        scores = lax.dot_general(
            queries_ref[here], keys_ref[there], ROWS_BY_ROWS, preferred_element_type=F32
        )
        same = marks_ref[here, 4:5] == segment_ref[0:1, there]
        if t == s:
            row = lax.broadcasted_iota(jnp.int32, (block, block), 0)
            other = lax.broadcasted_iota(jnp.int32, (block, block), 1)
            same = same & (other <= row)
        masked_ref[at] = jnp.where(same, scores, 0.0)
    grown = jnp.exp(run_ref[...])
    lane = lax.broadcasted_iota(jnp.int32, (block, 2 * head_size), 1)
    for p in range(heads // 2):
        wide = slice(p * 2 * head_size, (p + 1) * 2 * head_size)
        x = x_ref[:, wide].astype(F32)
        y = both_heads(grown, p, head_size) * begun_ref[:, wide] + both_heads(skip_ref[...], p, head_size) * x
        sums = [y[t * block : (t + 1) * block] for t in range(rows // block)]
        for at, (t, s) in enumerate(blocks):
            here, there = slice(t * block, (t + 1) * block), slice(s * block, (s + 1) * block)
            for side in range(2):
                head = 2 * p + side
                mine = (lane < head_size) if side == 0 else (lane >= head_size)
                x_own = jnp.where(mine, x[there], 0.0).astype(BF16)
                gap = run_ref[here, head : head + 1] - less_ref[head : head + 1, there]
                weight = (masked_ref[at] * jnp.exp(jnp.minimum(gap, 80.0))).astype(BF16)
                sums[t] = sums[t] + jnp.dot(weight, x_own, preferred_element_type=F32)
        for t in range(rows // block):
            y_ref[t * block : (t + 1) * block, wide] = sums[t]


def gate_kernel(
    heads, unused, y_ref, queries_ref, run_ref, marks_ref, entry_ref, gate_ref, gain_ref, out_ref, sq_ref
):
    del unused
    rows, inner = y_ref.shape
    head_size = inner // heads
    carried = jnp.where(marks_ref[:, 5:6] > 0, 1.0, 0.0)
    queries = (queries_ref[...].astype(F32) * carried).astype(BF16)
    held = lax.dot_general(
        queries, entry_ref[...].astype(BF16), ROWS_BY_ROWS, preferred_element_type=F32
    )
    grown = jnp.exp(run_ref[...])
    grown = jnp.concatenate([both_heads(grown, p, head_size) for p in range(heads // 2)], axis=1)
    gate = gate_ref[...].astype(F32)
    gated = (y_ref[...] + grown * held) * (gate / (1.0 + jnp.exp(-gate)))
    out_ref[...] = (gated * gain_ref[...]).astype(BF16)
    square = jnp.sum(gated * gated, axis=1, keepdims=True)
    sq_ref[...] = jnp.broadcast_to(square, (rows, LANES)).T[:8]


def norm_scale(own_ref, other_ref, channels):
    scale = lax.rsqrt((own_ref[0:1] + other_ref[0:1]) / channels + EPSILON)
    return jnp.broadcast_to(scale, (LANES, scale.shape[1])).T


def out_kernel(width, count, scaled, blocks, gated_ref, own_ref, other_ref, chooser_ref, *refs):
    del blocks
    weights, outs = refs[: 4 * count], refs[4 * count :]
    upper_out, upper_in, lower_out, lower_in, ends_ref = outs
    rows, inner = gated_ref.shape
    half = rows // 2
    if scaled:
        scale = norm_scale(own_ref, other_ref, 2 * inner)
        scale = jnp.concatenate([scale] * (width // LANES), axis=1)
    else:
        scale = jnp.ones((rows, width), F32)
    gated = gated_ref[...]
    end_rows = jnp.dot(chooser_ref[...], gated, preferred_element_type=F32).astype(BF16)
    end_scale = jnp.dot(
        chooser_ref[...].astype(F32), scale, precision=HIGHEST, preferred_element_type=F32
    )
    for at, w in enumerate(weights):
        index, place = divmod(at, count)
        part = jnp.dot(gated, w[...], preferred_element_type=F32) * scale
        top, bottom = part[:half], part[half:]
        low = (index // 2) * count + place
        target = upper_out if index % 2 else upper_in
        target[:, low * width : (low + 1) * width] = top.astype(target.dtype)
        low = (index % 2) * count + place
        target = lower_out if index // 2 else lower_in
        target[:, low * width : (low + 1) * width] = bottom.astype(target.dtype)
        ends_ref[:, at * width : (at + 1) * width] = (
            jnp.dot(end_rows, w[...], preferred_element_type=F32) * end_scale
        )


def near_kernel(unused, upper_ref, upper_got, lower_ref, lower_got, *outs):
    del unused
    for kept, got, keep_ref, send_ref in (
        (upper_ref, upper_got, outs[0], outs[1]),
        (lower_ref, lower_got, outs[2], outs[3]),
    ):
        wide = keep_ref.shape[1]
        keep_ref[...] = kept[:, :wide].astype(F32) + got[:, :wide].astype(F32)
        send_ref[...] = (kept[:, wide:].astype(F32) + got[:, wide:].astype(F32)).astype(BF16)


def plane_kernel(unused, upper_ref, upper_got, lower_ref, lower_got, *outs):
    del unused
    half, width = upper_ref.shape[0], outs[0].shape[1]
    for at, out_ref in enumerate(outs):
        wide = slice(at * width, (at + 1) * width)
        upper = upper_ref[:, wide] + upper_got[:, wide].astype(F32)
        lower = lower_ref[:, wide] + lower_got[:, wide].astype(F32)
        out_ref[:half] = upper.astype(out_ref.dtype)
        out_ref[half:] = lower.astype(out_ref.dtype)


def hidden_kernel(unused, tokens_ref, own_ref, *refs):
    del unused
    total = own_ref[...]
    for part in refs[:-1]:
        total = total + part[...].astype(F32)
    refs[-1][...] = (tokens_ref[...].astype(F32) + total).astype(BF16)


def scale_kernel(unused, own_ref, other_ref, chooser_ref, channels_ref, *refs):
    del unused
    raw, outs = refs[:5], refs[5:]
    half = raw[0].shape[0]
    scale = norm_scale(own_ref, other_ref, 2 * channels_ref.shape[1])
    end_scale = jnp.dot(
        chooser_ref[...].astype(F32), scale, precision=HIGHEST, preferred_element_type=F32
    )
    for at, (source, out_ref) in enumerate(zip(raw, outs)):
        factor = end_scale if at == 4 else scale[:half] if at < 2 else scale[half:]
        for lane in range(0, source.shape[1], LANES):
            value = source[:, lane : lane + LANES] * factor
            out_ref[:, lane : lane + LANES] = value.astype(out_ref.dtype)


def ends_kernel(width, col_size, sum_groups, gather_groups, place, *refs):
    sources, outs = refs[:-2], refs[-2:]
    groups = [(shifts, outs[0]) for shifts in sum_groups]
    groups += [(shifts, outs[1]) for shifts in gather_groups]
    for source, (shifts, out_ref) in zip(sources, groups):
        for at in range(source.shape[1] // width):
            block = block_of(shifts, at, place, col_size)
            to = pl.ds(pl.multiple_of(block * width, width), width)
            out_ref[:, to] = source[:, at * width : (at + 1) * width]


def finals_kernel(
    heads, added, first, spread_ref, keys_ref, marks_ref, ends_ref, entry_ref, init_ref, _, *refs
):
    out_ref = refs[-1]
    count, inner, state = out_ref.shape
    head_size = inner // heads
    slot = (first[0] + pl.program_id(0)) * count
    keys = keys_ref[...].astype(F32)
    owner = marks_ref[:, 6:7]
    mine = [
        (keys * jnp.where(owner == slot + i, ends_ref[i, :, heads : heads + 1], 0.0)).astype(BF16)
        for i in range(count)
    ]
    states = jnp.dot(
        spread_ref[...], jnp.concatenate(mine, axis=1), preferred_element_type=F32
    )
    for i in range(count):
        gain = over_states(ends_ref[i], heads, head_size)
        carried = jnp.broadcast_to(ends_ref[i, :, heads + 1 : heads + 2], (inner, state)) > 0.5
        value = states[:, i * state : (i + 1) * state]
        value = value + gain * jnp.where(carried, entry_ref[...], init_ref[i])
        out_ref[i] = value + refs[0][i] if added else value


def per_device(
    tokens,
    lengths,
    deal,
    pre_gain,
    w_inner,
    w_group,
    w_step,
    conv_inner,
    conv_group,
    conv_bias_inner,
    conv_bias_group,
    edge_inner,
    edge_group,
    init_states,
    step_bias,
    decay_log,
    skip,
    inner_gain,
    w_out,
    final_gain,
    w_head,
):
    rows, width = tokens.shape
    model_width = pre_gain.shape[0]
    requests = lengths.shape[0]
    taps = conv_inner.shape[0]
    inner = w_inner.shape[2]
    heads = w_step.shape[1]
    head_size = inner // heads
    state = w_group.shape[3]
    row_at, col_at, seq_at = (lax.axis_index(name) for name in ("row", "col", "seq"))
    row_size, col_size, seq_size = (lax.axis_size(name) for name in ("row", "col", "seq"))
    group_local = col_at * w_group.shape[2] // col_size

    def own_group(table, axis):
        return lax.dynamic_index_in_dim(table, group_local, axis, keepdims=False)

    def in_lanes(values):
        return jnp.pad(values, (0, LANES - heads))[None, :]

    first_row = seq_at * rows
    counts = jnp.concatenate([lengths, deal, jnp.reshape(first_row, (1,)).astype(jnp.int32)])
    marks, segment_row, chooser, slots = call(
        functools.partial(setup_kernel, taps),
        [
            ((rows, LANES), jnp.int32),
            ((8, rows), jnp.int32),
            ((requests, rows), BF16),
            ((requests, 2 * LANES), F32),
        ],
        prefetch=counts,
        vmem=4,
        work=0,
    )
    place = jnp.stack([row_at, col_at, group_local]).astype(jnp.int32)

    init_flat = jnp.reshape(init_states, (requests, inner, state))
    skip_row = in_lanes(skip)
    gains = pre_gain[None, :]

    gather_groups = ((0,1),(2,3))
    sum_groups = ((2,3),(0,1))

    n_all = 2 * inner + 2 * state + LANES
    steps_across = jnp.transpose(w_step)

    def weights_of(shifts, gain_row):
        count = row_size * len(shifts)
        parts = count // 2

        def specs(shape, where):
            return [
                pl.BlockSpec(shape, lambda i, p, at=at: where(
                    block_of(shifts, i * parts + at, p, col_size)
                ))
                for at in range(parts)
            ]

        return call(
            functools.partial(weights_kernel, parts),
            [((count * width, n_all), BF16), ((1, count * width), F32)],
            *[w_inner] * parts,
            *[w_group] * parts,
            *[steps_across] * parts,
            *[gain_row] * parts,
            prefetch=place,
            grid=(count // parts,),
            in_specs=specs((width,) + w_inner.shape[1:], lambda b: (b, 0, 0))
            + specs((width,) + w_group.shape[1:], lambda b: (b, 0, 0, 0))
            + specs((heads, width), lambda b: (0, b))
            + specs((1, width), lambda b: (0, b)),
            out_specs=[
                pl.BlockSpec((parts * width, n_all), lambda i, p: (i, 0)),
                pl.BlockSpec((1, parts * width), lambda i, p: (0, i)),
            ],
            vmem=58,
        )

    gain_row = pre_gain[None, :]
    token_blocks = {0: tokens}
    token_blocks[1] = from_ahead(tokens, "col", 1)
    later = after(tokens, token_blocks[1])
    for shift in range(2, col_size):
        source = token_blocks[1] if shift == 2 else later
        token_blocks[shift] = from_ahead(source, "col", 1 if shift == 2 else shift)
    gain_row = after(gain_row, token_blocks[1])
    token_ends = []
    carry = ()
    ready = ()
    for shifts in gather_groups:
        first, last = shifts == gather_groups[0], shifts == gather_groups[-1]
        pieces = plane_gather(jnp.concatenate([token_blocks[i] for i in shifts], axis=1))
        weights, gains = weights_of(shifts, after(gain_row, *ready) if ready else gain_row)
        ready = (pieces[1],)
        count = row_size * len(shifts)
        depth = count * width // 2
        outs = [((requests, count * width), F32)]
        totals = [((rows, n_all), F32), ((rows, LANES), F32)]
        if not last:
            outs += totals
        else:
            outs += [((rows, inner), BF16), ((rows, inner + 2 * state), BF16), ((rows, LANES), F32)]
        piece_ends, *carry = call(
            functools.partial(project_kernel, first, last, inner, model_width),
            outs,
            *pieces,
            chooser,
            gains,
            weights,
            *carry,
            grid=(2,),
            in_specs=[None] * 7
            + [
                pl.BlockSpec((1, depth), lambda i, _: (0, i)),
                pl.BlockSpec((depth, n_all), lambda i, _: (i, 0)),
            ]
            + [None] * len(carry),
            out_specs=[pl.BlockSpec((requests, depth), lambda i, _: (0, i))]
            + [None] * (len(outs) - 1),
            scratch=totals if last else [],
            vmem=24,
        )
        token_ends.append(piece_ends)
    gate_in, channels, step_raw = carry
    ready = gains

    init_last = lax.dynamic_index_in_dim(init_flat, after(marks, ready)[rows - 1, 6], 0, keepdims=False)
    (table,) = call(
        table_kernel,
        [((inner, requests * state), BF16)],
        after(init_flat, ready),
        grid=(requests,),
        in_specs=[pl.BlockSpec((1, inner, state), lambda i, _: (i, 0, 0))],
        out_specs=[pl.BlockSpec((inner, state), lambda i, _: (0, i))],
        vmem=4,
        work=0,
    )
    conv_taps = jnp.concatenate(
        [conv_inner, jnp.reshape(own_group(after(conv_group, ready), 2), (taps, 2 * state))], axis=1
    )
    conv_bias = jnp.concatenate(
        [conv_bias_inner, jnp.reshape(own_group(after(conv_bias_group, ready), 1), (2 * state,))]
    )[None, :]
    edges = jnp.concatenate(
        [after(edge_inner, ready), jnp.reshape(own_group(after(edge_group, ready), 3), (requests, taps - 1, 2 * state))],
        axis=2,
    )
    edges = jnp.reshape(edges, (requests * (taps - 1), inner + 2 * state))

    rim = from_behind(channels[rows - RIM :], "seq", 1)
    x, keys, queries, run, less, spread, leaving, gain_carried = call(
        functools.partial(conv_kernel, heads),
        [
            ((rows, inner), BF16),
            ((rows, state), BF16),
            ((rows, state), BF16),
            ((rows, LANES), F32),
            ((8, rows), F32),
            ((inner, rows), BF16),
            ((inner, state), F32),
            ((inner, state), F32),
        ],
        channels,
        rim,
        edges,
        conv_taps,
        conv_bias,
        step_raw,
        in_lanes(step_bias),
        in_lanes(decay_log),
        after(marks, table),
        segment_row,
        init_last,
        work=4,
    )
    entry = from_behind(leaving, "seq", 1)
    for _ in range(seq_size - 2):
        entry = from_behind(gain_carried * entry + leaving, "seq", 1)

    block = 256
    pairs = (rows // block) * (rows // block + 1) // 2
    y = pl.pallas_call(
        functools.partial(scan_kernel, heads, block),
        out_shape=jax.ShapeDtypeStruct((rows, inner), F32),
        grid_spec=pltpu.PrefetchScalarGridSpec(
            num_scalar_prefetch=1,
            grid=(1,),
            in_specs=[
                pl.BlockSpec(a.shape, lambda *_: (0, 0))
                for a in (x, keys, queries, run, less, marks, segment_row, table, skip_row)
            ],
            out_specs=pl.BlockSpec((rows, inner), lambda *_: (0, 0)),
            scratch_shapes=[
                pltpu.VMEM((pairs, block, block), F32),
                pltpu.VMEM((rows, inner), F32),
            ],
        ),
        compiler_params=pltpu.CompilerParams(vmem_limit_bytes=16 * MIB),
    )(
        jnp.zeros((1,), jnp.int32),
        x,
        keys,
        queries,
        run,
        less,
        marks,
        segment_row,
        table,
        skip_row,
    )
    gated, own_squares = call(
        functools.partial(gate_kernel, heads),
        [((rows, inner), BF16), ((8, rows), F32)],
        y,
        queries,
        run,
        marks,
        entry,
        gate_in,
        inner_gain[None, :],
        work=1,
    )
    other_squares = from_partner(own_squares, "col", 0)

    half_out, got = [], []
    for shifts in sum_groups:
        count = len(shifts)
        first = shifts == sum_groups[0]
        side = (rows // 2, 2 * count * width)
        kinds = [BF16] * 4
        ends_out = ((requests, row_size * count * width), F32)
        outs = call(
            functools.partial(out_kernel, width, count, not first),
            [(side, F32 if first else kind) for kind in kinds] + [ends_out],
            gated,
            own_squares,
            own_squares if first else other_squares,
            chooser,
            *[w_out] * (row_size * count),
            prefetch=place,
            in_specs=[None] * 4
            + [
                pl.BlockSpec(
                    (inner, width),
                    lambda i, p, at=at, shifts=shifts: (0, block_of(shifts, at, p, col_size)),
                )
                for at in range(row_size * count)
            ],
            vmem=16,
            work=2 if first else 0,
        )
        if first:
            other_squares = after(other_squares, outs[0])
            outs = call(
                scale_kernel,
                [(side, kind) for kind in kinds] + [ends_out],
                own_squares,
                other_squares,
                chooser,
                gated,
                *outs,
                vmem=12,
                work=0,
            )
        half_out.append(outs)
        got.append((from_partner(outs[0], "row", 0), from_partner(outs[2], "row", 1)))
    end_sum, end_tokens = call(
        functools.partial(ends_kernel, width, col_size, sum_groups, gather_groups),
        [((requests, model_width), F32)] * 2,
        after(half_out[0][4], *got[0]),
        *[outs[4] for outs in half_out[1:]],
        *token_ends,
        prefetch=place,
        vmem=4,
        work=0,
    )
    for axis, bit in (("col", 0), ("col", 1), ("row", 0), ("row", 1)):
        end_sum = end_sum + from_partner(end_sum.astype(BF16), axis, bit).astype(F32)

    def finals_after(far_ready):
        end_run = jnp.dot(chooser.astype(F32), run, precision=HIGHEST)[:, :heads]
        ends_here = slots[:, :1]
        end_marks = jnp.concatenate(
            [
                jnp.exp(end_run) * ends_here,
                ends_here,
                slots[:, LANES : LANES + 1],
                jnp.zeros((requests, LANES - heads - 2), F32),
            ],
            axis=1,
        )[:, None, :]

        kept = requests // seq_size

        def finals_of(first, steps, ready, extra):
            count = steps * kept
            by_slot = pl.BlockSpec((kept, inner, state), lambda i, s: (s[0] + i, 0, 0))
            by_step = pl.BlockSpec((kept, inner, state), lambda i, s: (i, 0, 0))
            return call(
                functools.partial(finals_kernel, heads, bool(extra)),
                [((count, inner, state), F32)],
                spread,
                keys,
                marks,
                end_marks,
                entry,
                init_flat,
                after(half_out[1][4], *ready),
                *extra,
                prefetch=jnp.reshape(first, (1,)).astype(jnp.int32),
                grid=(steps,),
                in_specs=[None] * 3
                + [pl.BlockSpec((kept, 1, LANES), lambda i, s: (s[0] + i, 0, 0)), None, by_slot]
                + [pl.BlockSpec(memory_space=pl.ANY)]
                + [by_step] * len(extra),
                out_specs=[by_step],
                vmem=20,
                work=0,
            )[0]

        if seq_size == 2:
            lent = finals_of(1 - seq_at, 1, far_ready, [])
            finals = finals_of(seq_at, 1, (), [from_partner(lent, "seq", 0)])
        else:
            finals = lax.psum_scatter(
                finals_of(jnp.int32(0), seq_size, (), []), "seq", scatter_dimension=0, tiled=True
            )
        return finals

    pieces = {}
    for shifts, outs, (upper_got, lower_got) in zip(sum_groups, half_out, got):
        _, upper_in, _, lower_in, _ = outs
        wide = len(shifts) * width
        upper, upper_far, lower, lower_near = call(
            near_kernel,
            [((rows // 2, wide), F32), ((rows // 2, wide), BF16)] * 2,
            upper_in,
            upper_got,
            lower_in,
            lower_got,
            vmem=8,
            work=10,
        )
        upper_far = from_partner(upper_far, "row", 1)
        lower_near = from_partner(lower_near, "row", 0)
        sums = call(
            plane_kernel,
            [((rows, width), BF16 if shift else F32) for shift in shifts],
            upper,
            upper_far,
            lower,
            lower_near,
            vmem=8,
            work=10,
        )
        if shifts == sum_groups[-2]:
            far_ready = sums
        for shift, part in zip(shifts, sums):
            pieces[shift] = from_ahead(part, "col", col_size - shift) if shift else part
    finals = finals_after(far_ready)
    if seq_size == 2:
        ending = after(end_tokens + end_sum, finals)
        ending = ending + from_partner(ending, "seq", 0)
    else:
        ending = lax.psum(end_tokens + end_sum, "seq")
    (hidden_out,) = call(
        hidden_kernel,
        [((rows, width), BF16)],
        tokens,
        *[pieces[shift] for shift in range(col_size)],
        vmem=4,
        work=30,
    )

    last_rows = ending.astype(BF16).astype(F32)
    final_scale = lax.rsqrt(jnp.sum(last_rows * last_rows, axis=1) / model_width + EPSILON)
    head_in = (last_rows * final_scale[:, None] * final_gain).astype(BF16)
    logits = jnp.dot(head_in, w_head, preferred_element_type=F32)

    final_states = jnp.reshape(finals, (finals.shape[0], heads, head_size, state))
    return (hidden_out, final_states, logits)


def solution(mesh):
    in_specs = (
        P("seq", ("row", "col")),
        P(),
        P(),
        P(),
        P(None, None, ("row", "col")),
        P(None, None, "row", None),
        P(None, ("row", "col")),
        P(None, ("row", "col")),
        P(None, None, "row", None),
        P(("row", "col")),
        P(None, "row", None),
        P(None, None, ("row", "col")),
        P(None, None, None, "row", None),
        P(None, ("row", "col"), None, None),
        P(("row", "col")),
        P(("row", "col")),
        P(("row", "col")),
        P(("row", "col")),
        P(("row", "col"), None),
        P(),
        P(None, ("seq", "row", "col")),
    )
    out_specs = (
        P("seq", ("row", "col")),
        P("seq", ("row", "col"), None, None),
        P(None, ("seq", "row", "col")),
    )
    return jax.shard_map(
        per_device, mesh=mesh, in_specs=in_specs, out_specs=out_specs, check_vma=False
    )
```

```python
import functools

import jax
import jax.numpy as jnp
from jax import lax
from jax.experimental import pallas as pl
from jax.experimental.pallas import tpu as pltpu
from jax.sharding import PartitionSpec as P

EPSILON = 1e-05
HIGHEST = lax.Precision.HIGHEST
F32 = jnp.float32
BF16 = jnp.bfloat16
LANES = 128
RIM = 16
MIB = 1024 * 1024
ROWS_BY_ROWS = (((1,), (1,)), ((), ()))


def from_behind(block, axis, distance):
    devices = range(lax.axis_size(axis))
    route = [(i - distance, i) for i in devices if i - distance in devices]
    return lax.ppermute(block, axis, route)


def from_partner(x, axis, bit):
    return lax.ppermute(x, axis, [(i, i ^ 1 << bit) for i in range(lax.axis_size(axis))])


def from_ahead(x, axis, distance):
    size = lax.axis_size(axis)
    return lax.ppermute(x, axis, [((i + distance) % size, i) for i in range(size)])


def after(x, *others):
    return lax.optimization_barrier((x,) + others)[0]


def call(kernel, outs, *args, prefetch=None, grid=(1,), in_specs=None, out_specs=None, scratch=(), vmem=12, work=20):
    params = pltpu.CompilerParams(vmem_limit_bytes=vmem * MIB)
    shapes = [jax.ShapeDtypeStruct(shape, kind) for shape, kind in outs]

    def whole(shape):
        zeros = (0,) * len(shape)
        return pl.BlockSpec(shape, lambda *_: zeros)

    specs = [
        whole(a.shape) if spec is None else spec
        for a, spec in zip(args, in_specs or [None] * len(args))
    ]
    gives = [
        whole(shape) if spec is None else spec
        for (shape, _), spec in zip(outs, out_specs or [None] * len(outs))
    ]
    prefetch = jnp.zeros((1,), jnp.int32) if prefetch is None else prefetch
    spec = pltpu.PrefetchScalarGridSpec(
        num_scalar_prefetch=1, grid=grid, in_specs=specs, out_specs=gives,
        scratch_shapes=[pltpu.VMEM(shape, kind) for shape, kind in scratch],
    )
    return pl.pallas_call(
        kernel,
        out_shape=shapes,
        grid_spec=spec,
        compiler_params=params,
        cost_estimate=pl.CostEstimate(flops=work * 1_000_000_000, bytes_accessed=100_000_000 if work else 1000, transcendentals=0),
    )(prefetch, *args)


def plane_gather(block):
    half = block.shape[0] // 2
    upper, lower = block[:half], block[half:]
    upper_far = from_partner(upper, "row", 1)
    lower_near = from_partner(lower, "row", 0)
    upper_rest = from_partner(jnp.concatenate([upper, upper_far], axis=1), "row", 0)
    lower_rest = from_partner(jnp.concatenate([lower, lower_near], axis=1), "row", 1)
    return upper, upper_far, upper_rest, lower, lower_near, lower_rest


def block_of(shifts, at, place, col_size):
    gap = shifts[-1] - shifts[0] if len(shifts) > 1 else 0
    shift = shifts[0] + (at % len(shifts)) * gap
    return (place[0] ^ (at // len(shifts))) * col_size + (place[1] + shift) % col_size


def setup_kernel(taps, counts, marks_ref, segment_ref, chooser_ref, slots_ref):
    requests = chooser_ref.shape[0]
    rows = marks_ref.shape[0]
    first_row = counts[2 * requests]
    begins, owners = [], []
    total = jnp.int32(0)
    for k in range(requests):
        begins.append(total - first_row)
        owners.append(counts[requests + k])
        total = total + counts[k]
    stops = begins[1:] + [total - first_row]

    def latest(position, values):
        found = jnp.full(position.shape, values[0], jnp.int32)
        for begin, value in zip(begins[1:], values[1:]):
            found = jnp.where(position >= begin, value, found)
        return found

    position = lax.broadcasted_iota(jnp.int32, (rows, LANES), 0)
    lane = lax.broadcasted_iota(jnp.int32, (rows, LANES), 1)
    owner = latest(position, owners)
    begin = latest(position, begins)
    offset = position - begin
    marks = owner
    for back in range(1, taps):
        edge = rows + RIM + owner * (taps - 1) + (taps - 1 - back) + offset
        inside = jnp.where(position >= back, position - back, rows + RIM + position - back)
        marks = jnp.where(lane == back - 1, jnp.where(offset >= back, inside, edge), marks)
    marks = jnp.where((lane == 3) & (begin < 0), requests, marks)
    marks = jnp.where(lane == 4, begin, marks)
    marks = jnp.where(lane == 5, jnp.where(begin < 0, 1, 0), marks)
    marks_ref[...] = marks
    across = lax.broadcasted_iota(jnp.int32, (8, rows), 1)
    segment_ref[...] = latest(across, begins)
    slot = lax.broadcasted_iota(jnp.int32, (requests, rows), 0)
    column = lax.broadcasted_iota(jnp.int32, (requests, rows), 1)
    slot_lane = lax.broadcasted_iota(jnp.int32, (requests, LANES), 0)
    chooser = jnp.zeros((requests, rows), F32)
    slot_begin = jnp.zeros((requests, LANES), F32)
    slot_end = jnp.zeros((requests, LANES), F32)
    for k in range(requests):
        last = stops[k] - 1
        chooser = jnp.where((slot == owners[k]) & (column == last), 1.0, chooser)
        here = jnp.where((last >= 0) & (last < rows), 1.0, 0.0)
        slot_end = jnp.where(slot_lane == owners[k], here, slot_end)
        before = jnp.where(begins[k] < 0, 1.0, 0.0)
        slot_begin = jnp.where(slot_lane == owners[k], before, slot_begin)
    chooser_ref[...] = chooser.astype(BF16)
    slots_ref[:, :LANES] = slot_end
    slots_ref[:, LANES:] = slot_begin


def weights_kernel(parts, place, *refs):
    out_ref, gain_out = refs[4 * parts :]
    rows = refs[0].shape[0]
    for part in range(parts):
        main_ref, group_ref, step_ref, gain_ref = refs[part : 4 * parts : parts]
        weights_block(
            place[2],
            main_ref,
            group_ref,
            step_ref,
            out_ref.at[pl.ds(part * rows, rows)],
        )
        gain_out[:, part * rows : (part + 1) * rows] = gain_ref[...]


def weights_block(group, main_ref, group_ref, step_ref, out_ref):
    rows, _, inner = main_ref.shape
    state = group_ref.shape[3]
    heads = step_ref.shape[0]
    half = rows // 2
    row = lax.broadcasted_iota(jnp.int32, (rows, rows), 0)
    column = lax.broadcasted_iota(jnp.int32, (rows, rows), 1)
    source = jnp.where(row < half, 2 * row, 2 * (row - half) + 1)
    pick = jnp.where(source == column, 1.0, 0.0).astype(BF16)
    flat = main_ref[...].reshape(2 * rows, inner)
    for at in range(2):
        got = jnp.dot(pick, flat[at * rows : (at + 1) * rows], preferred_element_type=F32)
        got = got.astype(BF16)
        out_ref[at * half : (at + 1) * half, :inner] = got[:half]
        out_ref[at * half : (at + 1) * half, inner : 2 * inner] = got[half:]
    take = rows // 4
    row, column = row[:half], column[:half]
    source = jnp.where(row < take, 4 * row, 4 * (row - take) + 2) + group
    pick = jnp.where(source == column, 1.0, 0.0).astype(BF16)
    flat = group_ref[...].reshape(4 * rows, state)
    for at in range(4):
        got = jnp.dot(pick, flat[at * rows : (at + 1) * rows], preferred_element_type=F32)
        got = got.astype(BF16)
        out_ref[at * take : (at + 1) * take, 2 * inner : 2 * inner + state] = got[:take]
        out_ref[at * take : (at + 1) * take, 2 * inner + state : 2 * inner + 2 * state] = got[take:]
    steps = jnp.concatenate(
        [step_ref[...].astype(F32), jnp.zeros((LANES - heads, rows), F32)], axis=0
    )
    out_ref[:, 2 * inner + 2 * state :] = steps.T.astype(BF16)


def table_kernel(unused, init_ref, out_ref):
    del unused
    out_ref[...] = init_ref[0].astype(BF16)


def project_kernel(first, last, inner, model_width, unused, *refs):
    del unused
    pieces, refs = refs[:6], refs[6:]
    chooser_ref, gain_ref, weights_ref, refs = refs[0], refs[1], refs[2], refs[3:]
    if not first:
        total_in, squares_in, refs = refs[0], refs[1], refs[2:]
    if not last:
        ends_ref, total_ref, squares_ref = refs
    else:
        ends_ref, gate_ref, channels_ref, steps_ref, total_ref, squares_ref = refs
    width = pieces[0].shape[1]

    def add(raw, fresh):
        ends_ref[...] = jnp.dot(chooser_ref[...], raw, preferred_element_type=F32)
        wide = raw.astype(F32)
        scaled = (wide * gain_ref[...]).astype(BF16)
        product = jnp.dot(scaled, weights_ref[...], preferred_element_type=F32)
        square = wide * wide
        parts = [square[:, at : at + LANES] for at in range(0, 2 * width, LANES)]
        if fresh:
            total_ref[...] = product if first else product + total_in[...]
            squares_ref[...] = functools.reduce(jnp.add, parts if first else parts + [squares_in[...]])
        else:
            total_ref[...] += product
            squares_ref[...] += functools.reduce(jnp.add, parts)

    upper, upper_far, upper_rest, lower, lower_near, lower_rest = pieces

    @pl.when(pl.program_id(0) == 0)
    def _():
        top = jnp.concatenate([upper[...], upper_rest[:, :width]], axis=1)
        bottom = jnp.concatenate([lower[...], lower_near[...]], axis=1)
        add(jnp.concatenate([top, bottom], axis=0), True)

    @pl.when(pl.program_id(0) == 1)
    def _():
        top = jnp.concatenate([upper_far[...], upper_rest[:, width:]], axis=1)
        add(jnp.concatenate([top, lower_rest[...]], axis=0), False)
        if not last:
            return
        inv_rms = jnp.sum(squares_ref[...], axis=1, keepdims=True) / model_width
        inv_rms = lax.rsqrt(inv_rms + EPSILON)
        gate_ref[...] = (total_ref[:, :inner] * inv_rms).astype(BF16)
        channels_ref[...] = (total_ref[:, inner:-LANES] * inv_rms).astype(BF16)
        steps_ref[...] = total_ref[:, -LANES:] * inv_rms


def both_heads(table, pair, head_size):
    rows = table.shape[0]
    lane = lax.broadcasted_iota(jnp.int32, (rows, 2 * head_size), 1)
    return jnp.where(
        lane < head_size, table[:, 2 * pair : 2 * pair + 1], table[:, 2 * pair + 1 : 2 * pair + 2]
    )


def over_states(row, heads, head_size):
    return jnp.concatenate(
        [jnp.broadcast_to(row[:, h : h + 1], (head_size, LANES)) for h in range(heads)], axis=0
    )


def conv_kernel(
    heads,
    unused,
    channels_ref,
    rim_ref,
    edges_ref,
    taps_ref,
    bias_ref,
    steps_ref,
    step_bias_ref,
    decay_ref,
    marks_ref,
    segment_ref,
    init_ref,
    x_ref,
    keys_ref,
    queries_ref,
    run_ref,
    less_ref,
    spread_ref,
    leaving_ref,
    gain_ref,
):
    del unused
    rows, inner = x_ref.shape
    state = keys_ref.shape[1]
    head_size = inner // heads
    taps = taps_ref.shape[0]
    channels = channels_ref[...]
    sources = jnp.concatenate([rim_ref[...], edges_ref[...]], axis=0)
    wide = channels.astype(F32)
    summed = bias_ref[...] + taps_ref[taps - 1 : taps] * wide
    column = lax.broadcasted_iota(jnp.int32, (rows, sources.shape[0]), 1)
    for back in range(1, taps):
        mark = marks_ref[:, back - 1 : back]
        pick = jnp.where(mark - rows == column, 1.0, 0.0).astype(BF16)
        value = jnp.dot(pick, sources, preferred_element_type=F32)
        value = value + jnp.where(mark < rows, 1.0, 0.0) * pltpu.roll(wide, back, 0)
        summed = summed + taps_ref[taps - 1 - back : taps - back] * value
    mixed = (summed / (1.0 + jnp.exp(-summed))).astype(BF16)
    x = mixed[:, :inner]
    keys = mixed[:, inner : inner + state]
    x_ref[...] = x
    keys_ref[...] = keys
    queries_ref[...] = mixed[:, inner + state :]
    raw = steps_ref[...] + step_bias_ref[...]
    step = jnp.maximum(raw, 0.0) + jnp.log1p(jnp.exp(-jnp.abs(raw)))
    log_decay = -jnp.exp(decay_ref[...]) * step
    segment = marks_ref[:, 4:5]
    same = segment == segment_ref[0:1, :]
    row = lax.broadcasted_iota(jnp.int32, (rows, rows), 0)
    other = lax.broadcasted_iota(jnp.int32, (rows, rows), 1)
    until = jnp.where(same & (other <= row), 1.0, 0.0).astype(BF16)
    after = jnp.where(same & (other > row), 1.0, 0.0).astype(BF16)
    lane = lax.broadcasted_iota(jnp.int32, log_decay.shape, 1)
    own = jnp.where(lane < heads, log_decay, 0.0)
    high = own.astype(BF16).astype(F32)
    middle = (own - high).astype(BF16).astype(F32)
    low = own - high - middle
    parts = high + pltpu.roll(middle, heads, 1) + pltpu.roll(low, 2 * heads, 1)
    parts = parts.astype(BF16)

    def summed_over(mask):
        sums = jnp.dot(mask, parts, preferred_element_type=F32)
        return (
            sums
            + pltpu.roll(sums, LANES - heads, 1)
            + pltpu.roll(sums, LANES - 2 * heads, 1)
        )

    run = summed_over(until)
    tail = summed_over(after)
    run_ref[...] = run
    less_ref[...] = (run - jnp.log(step)).T[:8]
    share = (jnp.exp(tail) * step).astype(BF16).astype(F32)
    spread = jnp.concatenate(
        [
            both_heads(share, p, head_size)
            * x[:, p * 2 * head_size : (p + 1) * 2 * head_size].astype(F32)
            for p in range(heads // 2)
        ],
        axis=1,
    )
    spread = spread.T.astype(BF16)
    spread_ref[...] = spread
    last = jnp.where(segment == segment[rows - 1 : rows], 1.0, 0.0)
    leaving = jnp.dot(spread, (keys.astype(F32) * last).astype(BF16), preferred_element_type=F32)
    gain = jnp.exp(run[rows - 1 : rows])
    carried = jnp.broadcast_to(marks_ref[rows - 1 : rows, 5:6], (heads * head_size, state)) > 0
    gain_wide = over_states(gain, heads, head_size)
    leaving_ref[...] = jnp.where(carried, leaving, leaving + gain_wide * init_ref[...])
    gain_ref[...] = jnp.where(carried, gain_wide, 0.0)


def scan_kernel(
    heads,
    block,
    unused,
    x_ref,
    keys_ref,
    queries_ref,
    run_ref,
    less_ref,
    marks_ref,
    segment_ref,
    table_ref,
    skip_ref,
    y_ref,
    masked_ref,
    begun_ref,
):
    del unused
    rows, inner = x_ref.shape
    head_size = inner // heads
    slots = table_ref.shape[1] // queries_ref.shape[1]
    queries = queries_ref[...].astype(F32)
    slot = marks_ref[:, 3:4]
    placed = jnp.concatenate(
        [(queries * jnp.where(slot == o, 1.0, 0.0)).astype(BF16) for o in range(slots)], axis=1
    )
    begun_ref[...] = lax.dot_general(
        placed, table_ref[...], ROWS_BY_ROWS, preferred_element_type=F32
    )
    blocks = [(t, s) for t in range(rows // block) for s in range(t + 1)]
    for at, (t, s) in enumerate(blocks):
        here, there = pl.ds(t * block, block), pl.ds(s * block, block)
        scores = lax.dot_general(
            queries_ref[here], keys_ref[there], ROWS_BY_ROWS, preferred_element_type=F32
        )
        same = marks_ref[here, 4:5] == segment_ref[0:1, there]
        if t == s:
            row = lax.broadcasted_iota(jnp.int32, (block, block), 0)
            other = lax.broadcasted_iota(jnp.int32, (block, block), 1)
            same = same & (other <= row)
        masked_ref[at] = jnp.where(same, scores, 0.0)
    grown = jnp.exp(run_ref[...])
    lane = lax.broadcasted_iota(jnp.int32, (block, 2 * head_size), 1)
    for p in range(heads // 2):
        wide = slice(p * 2 * head_size, (p + 1) * 2 * head_size)
        x = x_ref[:, wide].astype(F32)
        y = both_heads(grown, p, head_size) * begun_ref[:, wide] + both_heads(skip_ref[...], p, head_size) * x
        sums = [y[t * block : (t + 1) * block] for t in range(rows // block)]
        for at, (t, s) in enumerate(blocks):
            here, there = slice(t * block, (t + 1) * block), slice(s * block, (s + 1) * block)
            for side in range(2):
                head = 2 * p + side
                mine = (lane < head_size) if side == 0 else (lane >= head_size)
                x_own = jnp.where(mine, x[there], 0.0).astype(BF16)
                gap = run_ref[here, head : head + 1] - less_ref[head : head + 1, there]
                weight = (masked_ref[at] * jnp.exp(jnp.minimum(gap, 80.0))).astype(BF16)
                sums[t] = sums[t] + jnp.dot(weight, x_own, preferred_element_type=F32)
        for t in range(rows // block):
            y_ref[t * block : (t + 1) * block, wide] = sums[t]


def gate_kernel(
    heads, unused, y_ref, queries_ref, run_ref, marks_ref, entry_ref, gate_ref, gain_ref, out_ref, sq_ref
):
    del unused
    rows, inner = y_ref.shape
    head_size = inner // heads
    carried = jnp.where(marks_ref[:, 5:6] > 0, 1.0, 0.0)
    queries = (queries_ref[...].astype(F32) * carried).astype(BF16)
    held = lax.dot_general(
        queries, entry_ref[...].astype(BF16), ROWS_BY_ROWS, preferred_element_type=F32
    )
    grown = jnp.exp(run_ref[...])
    grown = jnp.concatenate([both_heads(grown, p, head_size) for p in range(heads // 2)], axis=1)
    gate = gate_ref[...].astype(F32)
    gated = (y_ref[...] + grown * held) * (gate / (1.0 + jnp.exp(-gate)))
    out_ref[...] = (gated * gain_ref[...]).astype(BF16)
    square = jnp.sum(gated * gated, axis=1, keepdims=True)
    sq_ref[...] = jnp.broadcast_to(square, (rows, LANES)).T[:8]


def norm_scale(own_ref, other_ref, channels):
    scale = lax.rsqrt((own_ref[0:1] + other_ref[0:1]) / channels + EPSILON)
    return jnp.broadcast_to(scale, (LANES, scale.shape[1])).T


def out_kernel(width, count, scaled, blocks, gated_ref, own_ref, other_ref, chooser_ref, *refs):
    del blocks
    weights, outs = refs[: 4 * count], refs[4 * count :]
    upper_out, upper_in, lower_out, lower_in, ends_ref = outs
    rows, inner = gated_ref.shape
    half = rows // 2
    if scaled:
        scale = norm_scale(own_ref, other_ref, 2 * inner)
        scale = jnp.concatenate([scale] * (width // LANES), axis=1)
    else:
        scale = jnp.ones((rows, width), F32)
    gated = gated_ref[...]
    end_rows = jnp.dot(chooser_ref[...], gated, preferred_element_type=F32).astype(BF16)
    end_scale = jnp.dot(
        chooser_ref[...].astype(F32), scale, precision=HIGHEST, preferred_element_type=F32
    )
    for at, w in enumerate(weights):
        index, place = divmod(at, count)
        part = jnp.dot(gated, w[...], preferred_element_type=F32) * scale
        top, bottom = part[:half], part[half:]
        low = (index // 2) * count + place
        target = upper_out if index % 2 else upper_in
        target[:, low * width : (low + 1) * width] = top.astype(target.dtype)
        low = (index % 2) * count + place
        target = lower_out if index // 2 else lower_in
        target[:, low * width : (low + 1) * width] = bottom.astype(target.dtype)
        ends_ref[:, at * width : (at + 1) * width] = (
            jnp.dot(end_rows, w[...], preferred_element_type=F32) * end_scale
        )


def near_kernel(unused, upper_ref, upper_got, lower_ref, lower_got, *outs):
    del unused
    for kept, got, keep_ref, send_ref in (
        (upper_ref, upper_got, outs[0], outs[1]),
        (lower_ref, lower_got, outs[2], outs[3]),
    ):
        wide = keep_ref.shape[1]
        keep_ref[...] = kept[:, :wide].astype(F32) + got[:, :wide].astype(F32)
        send_ref[...] = (kept[:, wide:].astype(F32) + got[:, wide:].astype(F32)).astype(BF16)


def plane_kernel(unused, upper_ref, upper_got, lower_ref, lower_got, *outs):
    del unused
    half, width = upper_ref.shape[0], outs[0].shape[1]
    for at, out_ref in enumerate(outs):
        wide = slice(at * width, (at + 1) * width)
        upper = upper_ref[:, wide] + upper_got[:, wide].astype(F32)
        lower = lower_ref[:, wide] + lower_got[:, wide].astype(F32)
        out_ref[:half] = upper.astype(out_ref.dtype)
        out_ref[half:] = lower.astype(out_ref.dtype)


def hidden_kernel(unused, tokens_ref, own_ref, *refs):
    del unused
    total = own_ref[...]
    for part in refs[:-1]:
        total = total + part[...].astype(F32)
    refs[-1][...] = (tokens_ref[...].astype(F32) + total).astype(BF16)


def scale_kernel(unused, own_ref, other_ref, chooser_ref, channels_ref, *refs):
    del unused
    raw, outs = refs[:5], refs[5:]
    half = raw[0].shape[0]
    scale = norm_scale(own_ref, other_ref, 2 * channels_ref.shape[1])
    end_scale = jnp.dot(
        chooser_ref[...].astype(F32), scale, precision=HIGHEST, preferred_element_type=F32
    )
    for at, (source, out_ref) in enumerate(zip(raw, outs)):
        factor = end_scale if at == 4 else scale[:half] if at < 2 else scale[half:]
        for lane in range(0, source.shape[1], LANES):
            value = source[:, lane : lane + LANES].astype(F32) * factor
            out_ref[:, lane : lane + LANES] = value.astype(out_ref.dtype)


def ends_kernel(width, col_size, sum_groups, gather_groups, place, *refs):
    sources, outs = refs[:-2], refs[-2:]
    groups = [(shifts, outs[0]) for shifts in sum_groups]
    groups += [(shifts, outs[1]) for shifts in gather_groups]
    for source, (shifts, out_ref) in zip(sources, groups):
        for at in range(source.shape[1] // width):
            block = block_of(shifts, at, place, col_size)
            to = pl.ds(pl.multiple_of(block * width, width), width)
            out_ref[:, to] = source[:, at * width : (at + 1) * width]


def finals_kernel(
    heads, added, first, spread_ref, keys_ref, marks_ref, ends_ref, entry_ref, init_ref, _, *refs
):
    out_ref = refs[-1]
    count, inner, state = out_ref.shape
    head_size = inner // heads
    slot = (first[0] + pl.program_id(0)) * count
    keys = keys_ref[...].astype(F32)
    owner = marks_ref[:, 6:7]
    mine = [
        (keys * jnp.where(owner == slot + i, ends_ref[i, :, heads : heads + 1], 0.0)).astype(BF16)
        for i in range(count)
    ]
    states = jnp.dot(
        spread_ref[...], jnp.concatenate(mine, axis=1), preferred_element_type=F32
    )
    for i in range(count):
        gain = over_states(ends_ref[i], heads, head_size)
        carried = jnp.broadcast_to(ends_ref[i, :, heads + 1 : heads + 2], (inner, state)) > 0.5
        value = states[:, i * state : (i + 1) * state]
        value = value + gain * jnp.where(carried, entry_ref[...], init_ref[i])
        out_ref[i] = value + refs[0][i] if added else value


def per_device(
    tokens,
    lengths,
    deal,
    pre_gain,
    w_inner,
    w_group,
    w_step,
    conv_inner,
    conv_group,
    conv_bias_inner,
    conv_bias_group,
    edge_inner,
    edge_group,
    init_states,
    step_bias,
    decay_log,
    skip,
    inner_gain,
    w_out,
    final_gain,
    w_head,
):
    rows, width = tokens.shape
    model_width = pre_gain.shape[0]
    requests = lengths.shape[0]
    taps = conv_inner.shape[0]
    inner = w_inner.shape[2]
    heads = w_step.shape[1]
    head_size = inner // heads
    state = w_group.shape[3]
    row_at, col_at, seq_at = (lax.axis_index(name) for name in ("row", "col", "seq"))
    row_size, col_size, seq_size = (lax.axis_size(name) for name in ("row", "col", "seq"))
    group_local = col_at * w_group.shape[2] // col_size

    def own_group(table, axis):
        return lax.dynamic_index_in_dim(table, group_local, axis, keepdims=False)

    def in_lanes(values):
        return jnp.pad(values, (0, LANES - heads))[None, :]

    first_row = seq_at * rows
    counts = jnp.concatenate([lengths, deal, jnp.reshape(first_row, (1,)).astype(jnp.int32)])
    marks, segment_row, chooser, slots = call(
        functools.partial(setup_kernel, taps),
        [
            ((rows, LANES), jnp.int32),
            ((8, rows), jnp.int32),
            ((requests, rows), BF16),
            ((requests, 2 * LANES), F32),
        ],
        prefetch=counts,
        vmem=4,
        work=0,
    )
    place = jnp.stack([row_at, col_at, group_local]).astype(jnp.int32)

    init_flat = jnp.reshape(init_states, (requests, inner, state))
    skip_row = in_lanes(skip)
    gains = pre_gain[None, :]

    gather_groups = ((0,1),(2,3))
    sum_groups = ((2,3),(0,1))

    n_all = 2 * inner + 2 * state + LANES
    steps_across = jnp.transpose(w_step)

    def weights_of(shifts, gain_row):
        count = row_size * len(shifts)
        parts = count // 2

        def specs(shape, where):
            return [
                pl.BlockSpec(shape, lambda i, p, at=at: where(
                    block_of(shifts, i * parts + at, p, col_size)
                ))
                for at in range(parts)
            ]

        return call(
            functools.partial(weights_kernel, parts),
            [((count * width, n_all), BF16), ((1, count * width), F32)],
            *[w_inner] * parts,
            *[w_group] * parts,
            *[steps_across] * parts,
            *[gain_row] * parts,
            prefetch=place,
            grid=(count // parts,),
            in_specs=specs((width,) + w_inner.shape[1:], lambda b: (b, 0, 0))
            + specs((width,) + w_group.shape[1:], lambda b: (b, 0, 0, 0))
            + specs((heads, width), lambda b: (0, b))
            + specs((1, width), lambda b: (0, b)),
            out_specs=[
                pl.BlockSpec((parts * width, n_all), lambda i, p: (i, 0)),
                pl.BlockSpec((1, parts * width), lambda i, p: (0, i)),
            ],
            vmem=58,
        )

    gain_row = pre_gain[None, :]
    token_blocks = {0: tokens}
    token_blocks[1] = from_ahead(tokens, "col", 1)
    later = after(tokens, token_blocks[1])
    for shift in range(2, col_size):
        source = token_blocks[1] if shift == 2 else later
        token_blocks[shift] = from_ahead(source, "col", 1 if shift == 2 else shift)
    gain_row = after(gain_row, token_blocks[1])
    token_ends = []
    carry = ()
    ready = ()
    for shifts in gather_groups:
        first, last = shifts == gather_groups[0], shifts == gather_groups[-1]
        pieces = plane_gather(jnp.concatenate([token_blocks[i] for i in shifts], axis=1))
        weights, gains = weights_of(shifts, after(gain_row, *ready) if ready else gain_row)
        ready = (pieces[1],)
        count = row_size * len(shifts)
        depth = count * width // 2
        outs = [((requests, count * width), F32)]
        totals = [((rows, n_all), F32), ((rows, LANES), F32)]
        if not last:
            outs += totals
        else:
            outs += [((rows, inner), BF16), ((rows, inner + 2 * state), BF16), ((rows, LANES), F32)]
        piece_ends, *carry = call(
            functools.partial(project_kernel, first, last, inner, model_width),
            outs,
            *pieces,
            chooser,
            gains,
            weights,
            *carry,
            grid=(2,),
            in_specs=[None] * 7
            + [
                pl.BlockSpec((1, depth), lambda i, _: (0, i)),
                pl.BlockSpec((depth, n_all), lambda i, _: (i, 0)),
            ]
            + [None] * len(carry),
            out_specs=[pl.BlockSpec((requests, depth), lambda i, _: (0, i))]
            + [None] * (len(outs) - 1),
            scratch=totals if last else [],
            vmem=24,
        )
        token_ends.append(piece_ends)
    gate_in, channels, step_raw = carry
    ready = gains

    init_last = lax.dynamic_index_in_dim(init_flat, after(marks, ready)[rows - 1, 6], 0, keepdims=False)
    (table,) = call(
        table_kernel,
        [((inner, requests * state), BF16)],
        after(init_flat, ready),
        grid=(requests,),
        in_specs=[pl.BlockSpec((1, inner, state), lambda i, _: (i, 0, 0))],
        out_specs=[pl.BlockSpec((inner, state), lambda i, _: (0, i))],
        vmem=4,
        work=0,
    )
    conv_taps = jnp.concatenate(
        [conv_inner, jnp.reshape(own_group(after(conv_group, ready), 2), (taps, 2 * state))], axis=1
    )
    conv_bias = jnp.concatenate(
        [conv_bias_inner, jnp.reshape(own_group(after(conv_bias_group, ready), 1), (2 * state,))]
    )[None, :]
    edges = jnp.concatenate(
        [after(edge_inner, ready), jnp.reshape(own_group(after(edge_group, ready), 3), (requests, taps - 1, 2 * state))],
        axis=2,
    )
    edges = jnp.reshape(edges, (requests * (taps - 1), inner + 2 * state))

    rim = from_behind(channels[rows - RIM :], "seq", 1)
    x, keys, queries, run, less, spread, leaving, gain_carried = call(
        functools.partial(conv_kernel, heads),
        [
            ((rows, inner), BF16),
            ((rows, state), BF16),
            ((rows, state), BF16),
            ((rows, LANES), F32),
            ((8, rows), F32),
            ((inner, rows), BF16),
            ((inner, state), F32),
            ((inner, state), F32),
        ],
        channels,
        rim,
        edges,
        conv_taps,
        conv_bias,
        step_raw,
        in_lanes(step_bias),
        in_lanes(decay_log),
        after(marks, table),
        segment_row,
        init_last,
        work=4,
    )
    entry = from_behind(leaving, "seq", 1)
    for _ in range(seq_size - 2):
        entry = from_behind(gain_carried * entry + leaving, "seq", 1)

    block = 256
    pairs = (rows // block) * (rows // block + 1) // 2
    y = pl.pallas_call(
        functools.partial(scan_kernel, heads, block),
        out_shape=jax.ShapeDtypeStruct((rows, inner), F32),
        grid_spec=pltpu.PrefetchScalarGridSpec(
            num_scalar_prefetch=1,
            grid=(1,),
            in_specs=[
                pl.BlockSpec(a.shape, lambda *_: (0, 0))
                for a in (x, keys, queries, run, less, marks, segment_row, table, skip_row)
            ],
            out_specs=pl.BlockSpec((rows, inner), lambda *_: (0, 0)),
            scratch_shapes=[
                pltpu.VMEM((pairs, block, block), F32),
                pltpu.VMEM((rows, inner), F32),
            ],
        ),
        compiler_params=pltpu.CompilerParams(vmem_limit_bytes=16 * MIB),
    )(
        jnp.zeros((1,), jnp.int32),
        x,
        keys,
        queries,
        run,
        less,
        marks,
        segment_row,
        table,
        skip_row,
    )
    gated, own_squares = call(
        functools.partial(gate_kernel, heads),
        [((rows, inner), BF16), ((8, rows), F32)],
        y,
        queries,
        run,
        marks,
        entry,
        gate_in,
        inner_gain[None, :],
        work=1,
    )
    other_squares = from_partner(own_squares, "col", 0)

    half_out, got = [], []
    for shifts in sum_groups:
        count = len(shifts)
        first = shifts == sum_groups[0]
        side = (rows // 2, 2 * count * width)
        kinds = [BF16] * 4
        ends_out = ((requests, row_size * count * width), F32)
        outs = call(
            functools.partial(out_kernel, width, count, not first),
            [(side, kind) for kind in kinds] + [ends_out],
            gated,
            own_squares,
            own_squares if first else other_squares,
            chooser,
            *[w_out] * (row_size * count),
            prefetch=place,
            in_specs=[None] * 4
            + [
                pl.BlockSpec(
                    (inner, width),
                    lambda i, p, at=at, shifts=shifts: (0, block_of(shifts, at, p, col_size)),
                )
                for at in range(row_size * count)
            ],
            vmem=16,
            work=2 if first else 0,
        )
        if first:
            other_squares = after(other_squares, outs[0])
            outs = call(
                scale_kernel,
                [(side, kind) for kind in kinds] + [ends_out],
                own_squares,
                other_squares,
                chooser,
                gated,
                *outs,
                vmem=12,
                work=0,
            )
        half_out.append(outs)
        got.append((from_partner(outs[0], "row", 0), from_partner(outs[2], "row", 1)))
    end_sum, end_tokens = call(
        functools.partial(ends_kernel, width, col_size, sum_groups, gather_groups),
        [((requests, model_width), F32)] * 2,
        after(half_out[0][4], *got[0]),
        *[outs[4] for outs in half_out[1:]],
        *token_ends,
        prefetch=place,
        vmem=4,
        work=0,
    )
    for axis, bit in (("col", 0), ("col", 1), ("row", 0), ("row", 1)):
        end_sum = end_sum + from_partner(end_sum.astype(BF16), axis, bit).astype(F32)

    def finals_after(far_ready):
        end_run = jnp.dot(chooser.astype(F32), run, precision=HIGHEST)[:, :heads]
        ends_here = slots[:, :1]
        end_marks = jnp.concatenate(
            [
                jnp.exp(end_run) * ends_here,
                ends_here,
                slots[:, LANES : LANES + 1],
                jnp.zeros((requests, LANES - heads - 2), F32),
            ],
            axis=1,
        )[:, None, :]

        kept = requests // seq_size

        def finals_of(first, steps, ready, extra):
            count = steps * kept
            by_slot = pl.BlockSpec((kept, inner, state), lambda i, s: (s[0] + i, 0, 0))
            by_step = pl.BlockSpec((kept, inner, state), lambda i, s: (i, 0, 0))
            return call(
                functools.partial(finals_kernel, heads, bool(extra)),
                [((count, inner, state), F32)],
                spread,
                keys,
                marks,
                end_marks,
                entry,
                init_flat,
                after(half_out[1][4], *ready),
                *extra,
                prefetch=jnp.reshape(first, (1,)).astype(jnp.int32),
                grid=(steps,),
                in_specs=[None] * 3
                + [pl.BlockSpec((kept, 1, LANES), lambda i, s: (s[0] + i, 0, 0)), None, by_slot]
                + [pl.BlockSpec(memory_space=pl.ANY)]
                + [by_step] * len(extra),
                out_specs=[by_step],
                vmem=20,
                work=0,
            )[0]

        if seq_size == 2:
            lent = finals_of(1 - seq_at, 1, far_ready, [])
            finals = finals_of(seq_at, 1, (), [from_partner(lent, "seq", 0)])
        else:
            finals = lax.psum_scatter(
                finals_of(jnp.int32(0), seq_size, (), []), "seq", scatter_dimension=0, tiled=True
            )
        return finals

    pieces = {}
    for shifts, outs, (upper_got, lower_got) in zip(sum_groups, half_out, got):
        _, upper_in, _, lower_in, _ = outs
        wide = len(shifts) * width
        upper, upper_far, lower, lower_near = call(
            near_kernel,
            [((rows // 2, wide), F32), ((rows // 2, wide), BF16)] * 2,
            upper_in,
            upper_got,
            lower_in,
            lower_got,
            vmem=8,
            work=10,
        )
        upper_far = from_partner(upper_far, "row", 1)
        lower_near = from_partner(lower_near, "row", 0)
        sums = call(
            plane_kernel,
            [((rows, width), BF16 if shift else F32) for shift in shifts],
            upper,
            upper_far,
            lower,
            lower_near,
            vmem=8,
            work=10,
        )
        if shifts == sum_groups[-2]:
            far_ready = sums
        for shift, part in zip(shifts, sums):
            pieces[shift] = from_ahead(part, "col", col_size - shift) if shift else part
    finals = finals_after(far_ready)
    if seq_size == 2:
        ending = after(end_tokens + end_sum, finals)
        ending = ending + from_partner(ending, "seq", 0)
    else:
        ending = lax.psum(end_tokens + end_sum, "seq")
    (hidden_out,) = call(
        hidden_kernel,
        [((rows, width), BF16)],
        tokens,
        *[pieces[shift] for shift in range(col_size)],
        vmem=4,
        work=30,
    )

    last_rows = ending.astype(BF16).astype(F32)
    final_scale = lax.rsqrt(jnp.sum(last_rows * last_rows, axis=1) / model_width + EPSILON)
    head_in = (last_rows * final_scale[:, None] * final_gain).astype(BF16)
    logits = jnp.dot(head_in, w_head, preferred_element_type=F32)

    final_states = jnp.reshape(finals, (finals.shape[0], heads, head_size, state))
    return (hidden_out, final_states, logits)


def solution(mesh):
    in_specs = (
        P("seq", ("row", "col")),
        P(),
        P(),
        P(),
        P(None, None, ("row", "col")),
        P(None, None, "row", None),
        P(None, ("row", "col")),
        P(None, ("row", "col")),
        P(None, None, "row", None),
        P(("row", "col")),
        P(None, "row", None),
        P(None, None, ("row", "col")),
        P(None, None, None, "row", None),
        P(None, ("row", "col"), None, None),
        P(("row", "col")),
        P(("row", "col")),
        P(("row", "col")),
        P(("row", "col")),
        P(("row", "col"), None),
        P(),
        P(None, ("seq", "row", "col")),
    )
    out_specs = (
        P("seq", ("row", "col")),
        P("seq", ("row", "col"), None, None),
        P(None, ("seq", "row", "col")),
    )
    return jax.shard_map(
        per_device, mesh=mesh, in_specs=in_specs, out_specs=out_specs, check_vma=False
    )
```
